128 devices in a mesh: pipe: 2 (over y_hi), dp: 32 (over x, y_lo, z), tensor: 2 (over core).
Axes of the slice: x: 4, y: 4 (y_hi: 2, y_lo: 2; y = y_hi * 2 + y_lo), z: 4, core: 2. Of those that a mesh axis runs over, the one named last changes fastest.
Arguments:
- inputs: bfloat16 [4, 4096, 768], P(None, 'dp'), may hold values from -6 to 6
- cotangent: bfloat16 [4, 4096, 768], P(None, 'dp'), may hold values from -6 to 6
- segments: int32 [4, 4096], P(None, 'dp'), may hold values from 0 to 95, never falling along the last dimension, each value on 1 to 128 neighbouring positions
- routes: int32 [2, 4, 4096, 1], P('pipe', None, 'dp'), may hold values from 0 to 1
- gain_attn: float32 [2, 768], P('pipe'), may hold values from 0.5 to 1.5
- w_qkv: bfloat16 [2, 3, 768, 768], P('pipe', None, None, 'tensor'), may hold values from -0.21875 to 0.21875
- rel_table: float32 [2, 32, 12], P('pipe', None, 'tensor'), may hold values from -3 to 3
- w_att_out: bfloat16 [2, 768, 768], P('pipe', 'tensor'), may hold values from -0.875 to 0.875
- gain_ffn: float32 [2, 768], P('pipe'), may hold values from 0.5 to 1.5
- router: float32 [2, 768, 2], P('pipe'), may hold values from -0.16 to 0.16
- w_in: bfloat16 [2, 2, 768, 3072], P('pipe', None, None, 'tensor'), may hold values from -0.21875 to 0.21875
- w_out: bfloat16 [2, 2, 3072, 768], P('pipe', None, 'tensor'), may hold values from -0.3125 to 0.3125
Outputs:
- section_out: bfloat16 [2, 4, 4096, 768], P('pipe', None, 'dp')
- input_grad: bfloat16 [2, 4, 4096, 768], P('pipe', None, 'dp')
- grad_gain_attn: float32 [2, 768], P('pipe')
- grad_qkv: float32 [2, 3, 768, 768], P('pipe', None, 'dp', 'tensor')
- grad_table: float32 [2, 32, 12], P('pipe', None, 'tensor')
- grad_att_out: float32 [2, 768, 768], P('pipe', 'tensor', 'dp')
- grad_gain_ffn: float32 [2, 768], P('pipe')
- grad_router: float32 [2, 768, 2], P('pipe')
- grad_in: float32 [2, 2, 768, 3072], P('pipe', None, 'dp', 'tensor')
- grad_out: float32 [2, 2, 3072, 768], P('pipe', None, 'tensor', 'dp')
The draws below stay inside these ranges and needn't reach their ends.
Inputs may be any that keep to these rules, and one draw needn't show every extreme that they name: `segments`: segment numbers never fall along a micro-batch's tokens; each document holds 1 to 128 tokens and one holds exactly 128. `routes`: every expert is named by some token.
All inputs are finite; a program needn't handle non-finite values.
Results may differ from the reference program's by a relative error of at most 0.03.
Values may be sent and summed in bfloat16 or wider, within the bound.
A program may use at most 320 MiB of HBM per device.

```python
import math
import jax
import jax.numpy as jnp
import numpy as np
from jax import lax

D = 768
HEADS = 12
HEAD = 64
FF = 3072
BUCKETS = 32
EXPERTS = 2
MICRO = 4
LEN = 128
TOKENS = 4096
N_PIPE = 2
N_DP = 32


def raised(values, key, source, target, blocks, factor):
    def block_of(position):
        return (jnp.arange(values.shape[position]) // (values.shape[position] // blocks)).reshape((-1,) + (1,) * (values.ndim - 1 - position))

    first = jax.random.permutation(key, blocks)[block_of(target)]
    far = (block_of(target) + blocks // 2) % blocks
    return jnp.where((block_of(source) == first) | (block_of(source) == far), factor * values, values)


def block_levels(key, shape, split, least, high):
    level, own = 1.0, jax.random.fold_in(key, 6)
    for dim, shards_of in split:
        heights = jnp.exp(jax.random.uniform(jax.random.fold_in(own, dim), (shards_of,), jnp.float32, least / len(split), high / len(split)))
        level = level * jnp.repeat(heights, shape[dim] // shards_of).reshape([-1 if axis == dim else 1 for axis in range(len(shape))])
    return level


def choose_distinct(key, rows, amount, top, lift):
    sequence = jax.random.permutation(jax.random.fold_in(key, 1), amount)
    favour = sequence
    for power in range(3):
        favour = favour * favour // amount
    favour = favour * lift // amount
    lots = jax.random.randint(jax.random.fold_in(key, 2), (rows, amount), 0, 4096) + favour
    sure = jax.random.permutation(jax.random.fold_in(key, 3), rows)[jnp.arange(amount) % rows]
    lots = jnp.where(jnp.arange(rows)[:, None] == sure[None, :], 1 << 14, lots)
    merit = lots * amount + jnp.arange(amount)
    return lax.top_k(merit.astype(jnp.int32), top)[1].astype(jnp.int32)


def split_up(amount, total, most, slope):
    portions = [(1 << 20) // math.isqrt(rank ** slope) + 1 for rank in range(2, amount + 1)]
    spare, counts = total - most - (amount - 1), [1] * (amount - 1)
    while spare > 0:
        movable = [i for i in range(amount - 1) if counts[i] < most]
        mass, left = sum([portions[i] for i in movable]), spare
        for i in movable:
            addition = min(most - counts[i], max(1, left * portions[i] // mass), spare)
            counts[i] = counts[i] + addition
            spare = spare - addition
    return np.array([most] + counts)


def ragged_sizes(stream_key, amount, total, bound, skew):
    if amount == 2:
        one = jax.random.randint(stream_key, (), max(1, total - bound), min(bound, total - 1) + 1)
        return jnp.stack([one, total - one])
    lengths = jnp.asarray(split_up(amount, total, bound, skew), jnp.int32)
    couples = (amount - 1) // 2
    donor, receiver = lengths[1:1 + 2 * couples:2], lengths[2:2 + 2 * couples:2]
    room = jnp.minimum(donor - 1, bound - receiver)
    shifted = jax.random.randint(jax.random.fold_in(stream_key, 1), (couples,), 0, 1 << 20) % (room + 1)
    lengths = lengths.at[1:1 + 2 * couples:2].set(donor - shifted).at[2:2 + 2 * couples:2].set(receiver + shifted)
    return lengths[jax.random.permutation(jax.random.fold_in(stream_key, 2), amount)]


def noise(rng, dims, deviation, limit, shards=(), held_as=jnp.bfloat16):
    values = deviation * jax.random.normal(rng, dims, jnp.float32)
    if shards:
        values = values * block_levels(rng, dims, shards, -0.22, 0.18)
    return jnp.clip(values, -limit, limit).astype(held_as)


def gaussian_with(stream_key, shape, scale, reach, split, heavy, kind=jnp.bfloat16):
    array = scale * jax.random.normal(stream_key, shape, jnp.float32)
    if split:
        array = array * block_levels(stream_key, shape, split, -0.22, 0.18)
    return jnp.clip(raised(array, jax.random.fold_in(stream_key, 3), *heavy), -reach, reach).astype(kind)


def setup_inputs(seed: int = 0) -> dict:
    streams_of = jax.random.split(jax.random.key(seed), 13)
    return {
        "inputs": gaussian_with(streams_of[0], (MICRO, TOKENS, D), 1.0, 6.0, ((1, 32),), (1, 2, 32, 2.75)),
        "cotangent": gaussian_with(streams_of[1], (MICRO, TOKENS, D), 1.0, 6.0, ((1, 32),), (1, 2, 32, 2.75)),
        "segments": jax.vmap(lambda own: jnp.searchsorted(jnp.cumsum(ragged_sizes(own, 3 * N_DP, TOKENS, LEN, 0)), jnp.arange(TOKENS), side="right"))(jax.random.split(streams_of[2], MICRO)).reshape((MICRO, TOKENS)).astype(jnp.int32),
        "routes": choose_distinct(streams_of[3], N_PIPE * MICRO * TOKENS, EXPERTS, 1, 4096).reshape((N_PIPE, MICRO, TOKENS, 1)),
        "gain_attn": jnp.clip(1.0 + 0.1 * jax.random.normal(streams_of[4], (N_PIPE, D), jnp.float32), 0.5, 1.5),
        "w_qkv": noise(streams_of[5], (N_PIPE, 3, D, D), D ** -0.5, 0.21875, ((0, 2), (3, 2))),
        "rel_table": noise(streams_of[6], (N_PIPE, BUCKETS, HEADS), 0.5, 3.0, ((0, 2), (2, 2)), jnp.float32),
        "w_att_out": noise(streams_of[7], (N_PIPE, D, D), (D // 16) ** -0.5, 0.875, ((0, 2), (1, 2))),
        "gain_ffn": jnp.clip(1.0 + 0.1 * jax.random.normal(streams_of[8], (N_PIPE, D), jnp.float32), 0.5, 1.5),
        "router": noise(streams_of[9], (N_PIPE, D, EXPERTS), 0.027, 0.16, ((0, 2),), jnp.float32),
        "w_in": noise(streams_of[10], (N_PIPE, EXPERTS, D, FF), D ** -0.5, 0.21875, ((0, 2), (3, 2))),
        "w_out": noise(streams_of[11], (N_PIPE, EXPERTS, FF, D), (FF // 8) ** -0.5, 0.3125, ((0, 2), (2, 2))),
    }


@jax.custom_vjp
def low(v):
    return lax.optimization_barrier(v.astype(jnp.bfloat16)).astype(jnp.float32)

@jax.custom_vjp
def low_back(v):
    return v

def low_keep(v):
    return (low(v), None)

def low_pass(kept, grad):
    return (grad,)

def back_keep(v):
    return (v, None)

def back_low(kept, grad):
    return (low(grad),)
low.defvjp(low_keep, low_pass)
low_back.defvjp(back_keep, back_low)
epsilon = 1e-06
highest = lax.Precision.HIGHEST
masked_value = -1e+30

def bucket_onehot(length, buckets):
    places = np.arange(length)
    offset = places[None, :] - places[:, None]
    half = buckets // 2
    exact = half // 2
    upper = (offset > 0).astype(np.int64) * half
    distance = np.abs(offset)
    ratio = np.log(np.maximum(distance, 1) / exact) / np.log(128.0 / exact)
    far_bucket = np.minimum(exact + np.floor(ratio * (half - exact) + 1e-09).astype(np.int64), half - 1)
    bucket = upper + np.where(distance < exact, distance, far_bucket)
    return (bucket.reshape(-1)[None, :] == np.arange(buckets)[:, None]).astype(np.float32)

def rms_norm(values, gain):
    return values * lax.rsqrt(lax.optimization_barrier(jnp.mean(values * values, axis=-1, keepdims=True)) + epsilon) * gain

def layer(params, hidden, segs, route, onehot_t):
    gain_attn, w_qkv, rel_table, w_att_out, gain_ffn, router, w_in, w_out = params
    tokens = hidden.shape[0]
    seqs = tokens // LEN
    normed = low(rms_norm(hidden, gain_attn))
    projected = low(low_back(jnp.einsum('td,cdf->ctf', normed, w_qkv, precision=highest)))
    heads_of = projected.reshape(3, seqs, LEN, HEADS, HEAD)
    scores = jnp.einsum('sqhc,skhc->shqk', heads_of[0], heads_of[1], precision=highest) * HEAD ** (-0.5)
    bias = jnp.dot(rel_table.T, onehot_t, precision=highest).reshape(HEADS, LEN, LEN)
    scores = low_back(scores + bias[None])
    grouped = segs.reshape(seqs, LEN)
    same = grouped[:, None, :, None] == grouped[:, None, None, :]
    scores = jnp.where(same, scores, masked_value)
    probs = low(jax.nn.softmax(scores, axis=-1))
    mixed = jnp.einsum('shqk,skhc->sqhc', probs, heads_of[2], precision=highest)
    mixed = low(low_back(mixed)).reshape(tokens, D)
    after = hidden + low_back(jnp.dot(mixed, w_att_out, precision=highest))
    normed2 = low(rms_norm(after, gain_ffn))
    gates = jax.nn.softmax(jnp.dot(normed2, router, precision=highest), axis=-1)
    picked = (route[:, None] == jnp.arange(EXPERTS)[None, :]).astype(jnp.float32)
    chosen = lax.optimization_barrier(jnp.sum(gates * picked, axis=-1))
    total = jnp.zeros_like(after)
    for expert in range(EXPERTS):
        inner = low_back(jnp.dot(normed2, w_in[expert], precision=highest))
        active = low(jax.nn.gelu(inner))
        result = low_back(jnp.dot(active, w_out[expert], precision=highest))
        total = total + (picked[:, expert] * chosen)[:, None] * result
    return after + total

def reference(inputs, cotangent, segments, routes, gain_attn, w_qkv, rel_table, w_att_out, gain_ffn, router, w_in, w_out):
    onehot_t = jnp.asarray(bucket_onehot(LEN, BUCKETS))
    params = [item.astype(jnp.float32) for item in (gain_attn, w_qkv, rel_table, w_att_out, gain_ffn, router, w_in, w_out)]
    starts = inputs.astype(jnp.float32)
    probe = jnp.zeros_like(starts)

    def run(params, starts, probe):
        firsts = []
        lasts = []
        for micro in range(MICRO):
            mid = layer([item[0] for item in params], starts[micro], segments[micro], routes[0, micro, :, 0], onehot_t)
            mid = low(low_back(mid))
            firsts.append(mid)
            lasts.append(layer([item[1] for item in params], mid + probe[micro], segments[micro], routes[1, micro, :, 0], onehot_t))
        return (jnp.stack(firsts), jnp.stack(lasts))
    (firsts, lasts), pullback = jax.vjp(run, params, starts, probe)
    grads, d_starts, d_probe = pullback((jnp.zeros_like(firsts), cotangent.astype(jnp.float32)))
    section_out = jnp.stack([firsts, lasts]).astype(jnp.bfloat16)
    input_grad = jnp.stack([d_starts, d_probe]).astype(jnp.bfloat16)
    return (section_out, input_grad, grads[0], grads[1], grads[2], grads[3], grads[4], grads[5], grads[6], grads[7])
```

```python
import functools

import jax
import jax.numpy as jnp
import numpy as np
from jax import lax
from jax.experimental import pallas as pl
from jax.experimental.pallas import tpu as pltpu
from jax.sharding import PartitionSpec as P

HEAD = 64
LEN = 128
PAIRS = 3
SEQS = 2
epsilon = 1e-06
masked_value = -1e30
F32 = jnp.float32
BF16 = jnp.bfloat16
NT = (((1,), (1,)), ((), ()))
TN = (((0,), (0,)), ((), ()))


def far_limits(buckets):
    half = buckets // 2
    exact = half // 2
    distance = np.arange(LEN)
    ratio = np.log(np.maximum(distance, 1) / exact) / np.log(128.0 / exact)
    bucket = np.minimum(exact + np.floor(ratio * (half - exact) + 1e-09).astype(np.int64), half - 1)
    bucket = np.where(distance < exact, distance, bucket)
    return [int(np.argmax(bucket >= b)) for b in range(1, half) if np.any(bucket >= b)]


def bucket_map(buckets):
    query = lax.broadcasted_iota(jnp.int32, (LEN, LEN), 0)
    key = lax.broadcasted_iota(jnp.int32, (LEN, LEN), 1)
    offset = key - query
    distance = jnp.abs(offset)
    bucket = jnp.where(offset > 0, buckets // 2, 0)
    for limit in far_limits(buckets):
        bucket = bucket + jnp.where(distance >= limit, 1, 0)
    return bucket


def dot(a, b, dims=None):
    if dims is None:
        return jnp.dot(a, b, preferred_element_type=F32)
    return lax.dot_general(a, b, dims, preferred_element_type=F32)


def over_rows(values):
    return jnp.sum(values, axis=0, keepdims=True)


def over_lanes(values):
    return jnp.sum(values, axis=1, keepdims=True)


def kernel(
    x_hbm, dy_hbm, segs, routes, gain_a, table, gain_f, rdiff, wqkv_hbm, watt_hbm, win_hbm, wout_hbm,
    sec, dgrad, grads, small, tables,
    wqkv, watt, win, wout, hs, dys, xt, nt, rt, at, proj, probs, mixed, after, slope, act2, back2,
    result, chosens, dproj, send, recv, bias, dsum,
    load_sem, out_sem, in_sem, pipe_out, pipe_in,
):
    pipe = lax.axis_index("pipe")
    tensor = lax.axis_index("tensor")
    first = pipe == 0
    last = pipe == 1
    chunks, rows, width = hs.shape
    hidden = slope.shape[-1]
    step = 512
    buckets = table.shape[0]

    loads = [
        pltpu.make_async_copy(source, target, load_sem.at[i])
        for i, (source, target) in enumerate(
            ((wqkv_hbm, wqkv), (watt_hbm, watt), (win_hbm, win), (wout_hbm, wout))
        )
    ]
    load_x = pltpu.make_async_copy(x_hbm, hs, load_sem.at[4])
    load_dy = pltpu.make_async_copy(dy_hbm, dys, load_sem.at[4])

    @pl.when(first)
    def _():
        load_x.start()

    @pl.when(last)
    def _():
        load_dy.start()

    for load in loads:
        load.start()

    barrier = pltpu.get_barrier_semaphore()
    pl.semaphore_signal(barrier, inc=1, device_id={"tensor": 1 - tensor}, device_id_type=pl.DeviceIdType.MESH)
    pl.semaphore_signal(barrier, inc=1, device_id={"pipe": 1 - pipe}, device_id_type=pl.DeviceIdType.MESH)
    pl.semaphore_wait(barrier, 2)

    def to_other_core(slot):
        return pltpu.make_async_remote_copy(
            src_ref=send.at[slot], dst_ref=recv.at[slot], send_sem=out_sem.at[slot],
            recv_sem=in_sem.at[slot], device_id={"tensor": 1 - tensor},
            device_id_type=pl.DeviceIdType.MESH,
        )

    def to_other_section(source, target, slot):
        return pltpu.make_async_remote_copy(
            src_ref=source, dst_ref=target, send_sem=pipe_out.at[slot],
            recv_sem=pipe_in.at[slot], device_id={"pipe": 1 - pipe},
            device_id_type=pl.DeviceIdType.MESH,
        )

    def forward_copy(c):
        return to_other_section(sec.at[c], hs.at[c], c)

    def backward_copy(c):
        return to_other_section(dgrad.at[c], dys.at[c], chunks + c)

    def exchanged(slot, part):
        send[slot] = part.astype(BF16)
        copy = to_other_core(slot)
        copy.start()
        copy.wait()
        return send[slot].astype(F32) + recv[slot].astype(F32)

    bucket = bucket_map(buckets)
    lane = lax.broadcasted_iota(jnp.int32, (LEN, LEN), 1)
    upper = lane >= HEAD
    bias[...] = jnp.zeros_like(bias)
    dsum[...] = jnp.zeros_like(dsum)
    small[...] = jnp.zeros_like(small)

    def add_bias(b, carry):
        hit = bucket == b
        for pair in range(PAIRS):
            for side in range(2):
                at_lanes = pl.ds(side * LEN, LEN)
                bias[pair, :, at_lanes] = jnp.where(hit, table[b, 2 * pair + side], bias[pair, :, at_lanes])
        return carry

    lax.fori_loop(0, buckets, add_bias, 0)

    def stacked(values):
        zero = jnp.zeros_like(values)
        return jnp.concatenate([jnp.where(upper, zero, values), jnp.where(upper, values, zero)], axis=0)

    def unstacked(values):
        return jnp.where(upper, values[LEN:], values[:LEN])

    def per_head(values, reduce):
        left = reduce(values[:, :LEN], axis=1, keepdims=True)
        right = reduce(values[:, LEN:], axis=1, keepdims=True)
        return jnp.concatenate(
            [jnp.broadcast_to(left, (LEN, LEN)), jnp.broadcast_to(right, (LEN, LEN))], axis=1
        )

    for load in loads:
        load.wait()

    @pl.when(first)
    def _():
        load_x.wait()

    def forward(c, carry):
        @pl.when(last)
        def _():
            forward_copy(c).wait_recv()

        spot = pl.multiple_of(c * rows, rows)
        here = pl.ds(spot, rows)
        h = hs[c].astype(F32)
        scale = lax.rsqrt(jnp.mean(h * h, axis=1, keepdims=True) + epsilon)
        normed = (h * scale * gain_a[...]).astype(BF16)
        xt[:, here] = normed.T
        for part in range(3):
            proj[part, here, :] = dot(normed, wqkv[part]).astype(BF16)
        for s in range(SEQS):
            seq = pl.ds(pl.multiple_of(spot + s * LEN, LEN), LEN)
            along = jnp.broadcast_to(segs[pl.ds(c * SEQS + s, 1), :].astype(F32), (LEN, LEN))
            same = along == along.T
            same = jnp.concatenate([same, same], axis=1)
            for pair in range(PAIRS):
                lanes = pl.ds(pair * LEN, LEN)
                query = proj[0, seq, lanes]
                keys = stacked(proj[1, seq, lanes])
                values = stacked(proj[2, seq, lanes])
                scores = dot(query, keys, NT) * HEAD ** (-0.5) + bias[pair]
                scores = jnp.where(same, scores, masked_value)
                raised = jnp.exp(scores - per_head(scores, jnp.max))
                prob = raised / per_head(raised, jnp.sum)
                probs[c * SEQS + s, pair] = prob
                mixed[seq, lanes] = dot(prob.astype(BF16), values).astype(BF16)
        a = h + exchanged(4 * c, dot(mixed[here, :], watt[...]))
        after[here, :] = a
        scale = lax.rsqrt(jnp.mean(a * a, axis=1, keepdims=True) + epsilon)
        normed2 = (a * scale * gain_f[...]).astype(BF16)
        nt[:, here] = normed2.T
        route = routes[c]
        sign = (1 - 2 * route).astype(F32)
        logit = over_lanes(normed2.astype(F32) * rdiff[...])
        chosen = 1.0 / (1.0 + jnp.exp(-sign * logit))
        chosens[c] = chosen
        to_zero = (route == 0).astype(BF16)
        to_one = (route == 1).astype(BF16)
        doubled = jnp.concatenate([normed2 * to_zero, normed2 * to_one], axis=1)

        def inner_tile(n, carry):
            lanes = pl.ds(pl.multiple_of(n * step, step), step)
            inner = dot(doubled, win[:, lanes])
            squared = inner * inner
            root = np.sqrt(2 / np.pi).astype(np.float32)
            bend = jnp.tanh(root * inner * (1.0 + 0.044715 * squared))
            slope[here, lanes] = 0.5 * (1.0 + bend) + 0.5 * inner * (1.0 - bend * bend) * root * (
                1.0 + 3 * 0.044715 * squared
            )
            active = (0.5 * inner * (1.0 + bend)).astype(BF16)
            act2[here, lanes] = active * to_zero
            act2[here, pl.ds(pl.multiple_of(hidden + n * step, step), step)] = active * to_one
            return carry

        lax.fori_loop(0, hidden // step, inner_tile, 0)
        total = exchanged(4 * c + 1, dot(act2[here, :], wout[...]))
        result[here, :] = total
        sec[c] = (after[here, :] + chosen * total).astype(BF16)

        @pl.when(first)
        def _():
            forward_copy(c).start()

        return carry

    lax.fori_loop(0, chunks, forward, 0)

    @pl.when(last)
    def _():
        load_dy.wait()

    def backward(c, carry):
        @pl.when(first)
        def _():
            backward_copy(c).wait_recv()

        spot = pl.multiple_of(c * rows, rows)
        here = pl.ds(spot, rows)
        dy = dys[c].astype(F32)
        route = routes[c]
        sign = (1 - 2 * route).astype(F32)
        to_zero = (route == 0).astype(BF16)
        to_one = (route == 1).astype(BF16)
        chosen = chosens[c]
        d_logit = sign * over_lanes(dy * result[here, :]) * chosen * (1.0 - chosen)
        d_result = (chosen * dy).astype(BF16)
        rt[:, here] = d_result.T
        zero_part = d_result * to_zero
        one_part = d_result * to_one

        def active_tile(n, carry):
            low = pl.multiple_of(n * step, step)
            high = pl.multiple_of(hidden + n * step, step)
            d_active = dot(zero_part, wout[pl.ds(low, step), :], NT) + dot(
                one_part, wout[pl.ds(high, step), :], NT
            )
            d_inner = (d_active * slope[here, pl.ds(low, step)]).astype(BF16)
            back2[here, pl.ds(low, step)] = d_inner * to_zero
            back2[here, pl.ds(high, step)] = d_inner * to_one
            return carry

        lax.fori_loop(0, hidden // step, active_tile, 0)
        d_normed2 = dot(back2[here, :hidden], win[:width, :], NT) + dot(
            back2[here, hidden:], win[width:, :], NT
        )
        d_normed2 = exchanged(4 * c + 2, d_normed2) + d_logit * rdiff[...]
        a = after[here, :]
        scale = lax.rsqrt(jnp.mean(a * a, axis=1, keepdims=True) + epsilon)
        plain = a * scale
        normed2 = (plain * gain_f[...]).astype(BF16).astype(F32)
        small[1:2, :] += over_rows(d_normed2 * plain)
        small[2:3, :] += over_rows(normed2 * d_logit)
        pulled = d_normed2 * gain_f[...]
        d_after = dy + scale * (pulled - plain * jnp.mean(pulled * plain, axis=1, keepdims=True))
        after[here, :] = d_after
        d_attn = d_after.astype(BF16)
        at[:, here] = d_attn.T
        d_mixed = dot(d_attn, watt[...], NT).astype(BF16)
        for s in range(SEQS):
            seq = pl.ds(pl.multiple_of(spot + s * LEN, LEN), LEN)
            for pair in range(PAIRS):
                lanes = pl.ds(pair * LEN, LEN)
                query = proj[0, seq, lanes]
                keys = stacked(proj[1, seq, lanes])
                values = stacked(proj[2, seq, lanes])
                prob = probs[c * SEQS + s, pair]
                d_mix = d_mixed[s * LEN : (s + 1) * LEN, pair * LEN : (pair + 1) * LEN]
                product = prob * dot(d_mix, values, NT)
                d_scores = (product - prob * per_head(product, jnp.sum)).astype(BF16)
                dsum[pair] += d_scores.astype(F32)
                dproj[seq, pl.ds(pair * LEN, LEN)] = (dot(d_scores, keys) * HEAD ** (-0.5)).astype(BF16)
                d_keys = unstacked(dot(d_scores, query, TN)) * HEAD ** (-0.5)
                dproj[seq, pl.ds((PAIRS + pair) * LEN, LEN)] = d_keys.astype(BF16)
                d_values = unstacked(dot(prob.astype(BF16), d_mix, TN))
                dproj[seq, pl.ds((2 * PAIRS + pair) * LEN, LEN)] = d_values.astype(BF16)
        part = PAIRS * LEN
        d_normed = dot(dproj[here, :part], wqkv[0], NT)
        d_normed = d_normed + dot(dproj[here, part : 2 * part], wqkv[1], NT)
        d_normed = d_normed + dot(dproj[here, 2 * part :], wqkv[2], NT)
        d_normed = exchanged(4 * c + 3, d_normed)
        h = hs[c].astype(F32)
        scale = lax.rsqrt(jnp.mean(h * h, axis=1, keepdims=True) + epsilon)
        plain = h * scale
        small[0:1, :] += over_rows(d_normed * plain)
        pulled = d_normed * gain_a[...]
        d_hidden = after[here, :] + scale * (
            pulled - plain * jnp.mean(pulled * plain, axis=1, keepdims=True)
        )
        dgrad[c] = d_hidden.astype(BF16)

        @pl.when(last)
        def _():
            backward_copy(c).start()

        return carry

    lax.fori_loop(0, chunks, backward, 0)

    def keep(tile, left, right):
        shards, double, _ = grads.shape
        both = [side.reshape(shards, double // 2, LEN) for side in (left, right)]
        grads[:, :, pl.ds(pl.multiple_of(tile * LEN, LEN), LEN)] = jnp.concatenate(both, axis=1).astype(BF16)

    def product_tiles(tile, lefts, rights, count):
        def one(n, carry):
            lanes = pl.ds(pl.multiple_of(n * 2 * LEN, 2 * LEN), 2 * LEN)
            made = dot(lefts[...], rights[:, lanes])
            keep(tile + n, made[:, :LEN], made[:, LEN:])
            return carry

        lax.fori_loop(0, count, one, 0)

    out_tiles = 2 * hidden // (2 * LEN)
    product_tiles(0, rt, act2, out_tiles)
    product_tiles(out_tiles, nt, back2, out_tiles)
    product_tiles(2 * out_tiles, xt, dproj, 4)
    keep(2 * out_tiles + 4, dot(xt[...], dproj[:, 8 * LEN :]), dot(at[...], mixed[:, 2 * LEN :]))
    made = dot(at[...], mixed[:, : 2 * LEN])
    keep(2 * out_tiles + 5, made[:, :LEN], made[:, LEN:])

    def table_rows(b, carry):
        hit = bucket == b
        for pair in range(PAIRS):
            for side in range(2):
                picked = jnp.where(hit, dsum[pair, :, pl.ds(side * LEN, LEN)], 0.0)
                tables[2 * pair + side, pl.ds(b, 1), :] = over_rows(picked)
        return carry

    lax.fori_loop(0, buckets, table_rows, 0)

    def finish(c, carry):
        @pl.when(first)
        def _():
            forward_copy(c).wait_send()

        @pl.when(last)
        def _():
            backward_copy(c).wait_send()

        return carry

    lax.fori_loop(0, chunks, finish, 0)


def local_pass(inputs, cotangent, segments, routes, gain_attn, w_qkv, rel_table, w_att_out, gain_ffn, router, w_in, w_out, shards):
    micros, length, width = inputs.shape
    chunks = micros // SEQS
    rows = SEQS * length
    tokens = micros * length
    experts, _, hidden = w_in.shape
    heads = w_att_out.shape[0]
    buckets = rel_table.shape[0]
    columns = (3 * heads + heads + 2 * experts * hidden) // 2
    vmem = pl.BlockSpec(memory_space=pltpu.VMEM)
    smem = pl.BlockSpec(memory_space=pltpu.SMEM)
    anywhere = pl.BlockSpec(memory_space=pl.ANY)
    slots = 4 * chunks
    scratch = [
        pltpu.VMEM(w_qkv.shape, BF16),
        pltpu.VMEM(w_att_out.shape, BF16),
        pltpu.VMEM((experts * width, hidden), BF16),
        pltpu.VMEM((experts * hidden, width), BF16),
        pltpu.VMEM((chunks, rows, width), BF16),
        pltpu.VMEM((chunks, rows, width), BF16),
        pltpu.VMEM((width, tokens), BF16),
        pltpu.VMEM((width, tokens), BF16),
        pltpu.VMEM((width, tokens), BF16),
        pltpu.VMEM((width, tokens), BF16),
        pltpu.VMEM((3, tokens, heads), BF16),
        pltpu.VMEM((micros, PAIRS, LEN, 2 * LEN), F32),
        pltpu.VMEM((tokens, heads), BF16),
        pltpu.VMEM((tokens, width), F32),
        pltpu.VMEM((tokens, hidden), F32),
        pltpu.VMEM((tokens, experts * hidden), BF16),
        pltpu.VMEM((tokens, experts * hidden), BF16),
        pltpu.VMEM((tokens, width), F32),
        pltpu.VMEM((chunks, rows, 1), F32),
        pltpu.VMEM((tokens, 3 * heads), BF16),
        pltpu.VMEM((slots, rows, width), BF16),
        pltpu.VMEM((slots, rows, width), BF16),
        pltpu.VMEM((PAIRS, LEN, 2 * LEN), F32),
        pltpu.VMEM((PAIRS, LEN, 2 * LEN), F32),
        pltpu.SemaphoreType.DMA((5,)),
        pltpu.SemaphoreType.DMA((slots,)),
        pltpu.SemaphoreType.DMA((slots,)),
        pltpu.SemaphoreType.DMA((2 * chunks,)),
        pltpu.SemaphoreType.DMA((2 * chunks,)),
    ]
    return pl.pallas_call(
        kernel,
        out_shape=[
            jax.ShapeDtypeStruct((chunks, rows, width), BF16),
            jax.ShapeDtypeStruct((chunks, rows, width), BF16),
            jax.ShapeDtypeStruct((shards, 2 * width // shards, columns), BF16),
            jax.ShapeDtypeStruct((8, width), F32),
            jax.ShapeDtypeStruct((2 * PAIRS, buckets, LEN), F32),
        ],
        in_specs=[anywhere, anywhere, vmem, vmem, vmem, smem, vmem, vmem] + [anywhere] * 4,
        out_specs=[vmem] * 5,
        scratch_shapes=scratch,
        compiler_params=pltpu.CompilerParams(
            collective_id=0, has_side_effects=True, vmem_limit_bytes=62 * 2**20
        ),
        cost_estimate=pl.CostEstimate(flops=18 * 10**9, bytes_accessed=30 * 10**6, transcendentals=10**6),
    )(
        inputs.reshape(chunks, rows, width),
        cotangent.reshape(chunks, rows, width),
        segments,
        routes.reshape(chunks, rows, 1),
        gain_attn,
        rel_table,
        gain_ffn,
        (router[:, 0] - router[:, 1])[None, :],
        w_qkv,
        w_att_out,
        w_in.reshape(experts * width, hidden),
        w_out.reshape(experts * hidden, width),
    )


def unfolded(shard, columns):
    tiles = columns // (2 * LEN)
    rows = shard.shape[0] // 2
    return shard.reshape(2, rows, tiles, LEN).transpose(1, 2, 0, 3).reshape(rows, columns)


def per_device(
    inputs, cotangent, segments, routes, gain_attn, w_qkv, rel_table, w_att_out, gain_ffn, router, w_in, w_out
):
    experts, width, hidden = w_in.shape[1:]
    heads = w_att_out.shape[1]
    shards = lax.axis_size("dp")
    sec, dgrad, grads, small, tables = local_pass(
        inputs, cotangent, segments, routes[0], gain_attn, w_qkv[0], rel_table[0], w_att_out[0],
        gain_ffn, router[0], w_in[0], w_out[0], shards,
    )
    columns = 2 * grads.shape[2]
    mine = lax.psum_scatter(grads, "dp", scatter_dimension=0, tiled=True)[0].astype(F32)
    mine = unfolded(mine, columns)
    rows = mine.shape[0]
    both = experts * hidden
    g_out = mine[:, :both].reshape(rows, experts, hidden).transpose(1, 2, 0)
    g_in = mine[:, both : 2 * both].reshape(rows, experts, hidden).transpose(1, 0, 2)
    rest = mine[:, 2 * both :]
    g_qkv = rest[:, : 3 * heads].reshape(rows, 3, heads).transpose(1, 0, 2)
    g_att = jnp.concatenate([rest[:, 3 * heads + LEN :], rest[:, 3 * heads : 3 * heads + LEN]], axis=1).T
    flat = jnp.concatenate([small[:3].reshape(-1), tables.sum(axis=2).T.reshape(-1)])
    flat = lax.psum(flat, "dp")
    gain_a, gain_f, routed = flat[:width], flat[width : 2 * width], flat[2 * width : 3 * width]
    table = flat[3 * width :].reshape(rel_table.shape[1:])
    micros, length = inputs.shape[:2]
    return (
        sec.reshape(1, micros, length, width),
        dgrad.reshape(1, micros, length, width),
        gain_a[None],
        g_qkv[None],
        table[None],
        g_att[None],
        gain_f[None],
        jnp.stack([routed, -routed], axis=1)[None],
        g_in[None],
        g_out[None],
    )


def solution(mesh):
    placed = (
        P(None, "dp", None),
        P(None, "dp", None),
        P(None, "dp"),
        P("pipe", None, "dp", None),
        P("pipe", None),
        P("pipe", None, None, "tensor"),
        P("pipe", None, "tensor"),
        P("pipe", "tensor", None),
        P("pipe", None),
        P("pipe", None, None),
        P("pipe", None, None, "tensor"),
        P("pipe", None, "tensor", None),
    )
    return jax.shard_map(
        per_device,
        mesh=mesh,
        in_specs=placed,
        out_specs=(
            P("pipe", None, "dp", None),
            P("pipe", None, "dp", None),
            P("pipe", None),
            P("pipe", None, "dp", "tensor"),
            P("pipe", None, "tensor"),
            P("pipe", "tensor", "dp"),
            P("pipe", None),
            P("pipe", None, None),
            P("pipe", None, "dp", "tensor"),
            P("pipe", None, "tensor", "dp"),
        ),
        check_vma=False,
    )
```

```python
import functools

import jax
import jax.numpy as jnp
import numpy as np
from jax import lax
from jax.experimental import pallas as pl
from jax.experimental.pallas import tpu as pltpu
from jax.sharding import PartitionSpec as P

HEAD = 64
LEN = 128
PAIRS = 3
SEQS = 2
RING = 4
STAGES = ((0, 12), (12, 24), (24, 30))
epsilon = 1e-06
masked_value = -1e30
F32 = jnp.float32
BF16 = jnp.bfloat16
NT = (((1,), (1,)), ((), ()))
TN = (((0,), (0,)), ((), ()))


def far_limits(buckets):
    half = buckets // 2
    exact = half // 2
    distance = np.arange(LEN)
    ratio = np.log(np.maximum(distance, 1) / exact) / np.log(128.0 / exact)
    bucket = np.minimum(exact + np.floor(ratio * (half - exact) + 1e-09).astype(np.int64), half - 1)
    bucket = np.where(distance < exact, distance, bucket)
    return [int(np.argmax(bucket >= b)) for b in range(1, half) if np.any(bucket >= b)]


def bucket_map(buckets):
    query = lax.broadcasted_iota(jnp.int32, (LEN, LEN), 0)
    key = lax.broadcasted_iota(jnp.int32, (LEN, LEN), 1)
    offset = key - query
    distance = jnp.abs(offset)
    bucket = jnp.where(offset > 0, buckets // 2, 0)
    for limit in far_limits(buckets):
        bucket = bucket + jnp.where(distance >= limit, 1, 0)
    return bucket


def dot(a, b, dims=None):
    if dims is None:
        return jnp.dot(a, b, preferred_element_type=F32)
    return lax.dot_general(a, b, dims, preferred_element_type=F32)


def over_rows(values):
    return jnp.sum(values, axis=0, keepdims=True)


def over_lanes(values):
    return jnp.sum(values, axis=1, keepdims=True)


def kernel(
    x_hbm, dy_hbm, segs, routes, gain_a, table, gain_f, rdiff, wqkv_hbm, watt_hbm, win_hbm, wout_hbm,
    sec, dgrad, g_out, g_in, g_qkv, g_att, small,
    wqkv, watt, win, wout, hs, dys, xt, nt, rt, at, proj, probs, mixed, after, slope, act2, back2,
    result, chosens, dproj, send, recv, bias, dsum, tables, grads, wide0, wide1, wide2, narrow0, narrow1,
    narrow2, pair0, pair1, pair2, own, lots,
    load_sem, out_sem, in_sem, pipe_out, pipe_in, ring_out, ring_in, lot_out, lot_in,
):
    pipe = lax.axis_index("pipe")
    tensor = lax.axis_index("tensor")
    first = pipe == 0
    last = pipe == 1
    chunks, rows, width = hs.shape
    hidden = slope.shape[-1]
    step = 512
    buckets = table.shape[0]

    loads = [
        pltpu.make_async_copy(source, target, load_sem.at[i])
        for i, (source, target) in enumerate(
            ((wqkv_hbm, wqkv), (watt_hbm, watt), (win_hbm, win), (wout_hbm, wout))
        )
    ]
    load_x = pltpu.make_async_copy(x_hbm, hs, load_sem.at[4])
    load_dy = pltpu.make_async_copy(dy_hbm, dys, load_sem.at[4])

    @pl.when(first)
    def _():
        load_x.start()

    @pl.when(last)
    def _():
        load_dy.start()

    for load in loads:
        load.start()

    barrier = pltpu.get_barrier_semaphore()
    pl.semaphore_signal(barrier, inc=1, device_id={"tensor": 1 - tensor}, device_id_type=pl.DeviceIdType.MESH)
    pl.semaphore_signal(barrier, inc=1, device_id={"pipe": 1 - pipe}, device_id_type=pl.DeviceIdType.MESH)
    place = lax.axis_index("dp")
    at_x, at_y, at_z = place // (2 * RING), place // RING % 2, place % RING

    def neighbour(on_x, steps):
        if on_x:
            return {"dp": (at_x + steps) % RING * 2 * RING + at_y * RING + at_z}
        return {"dp": at_x * 2 * RING + at_y * RING + (at_z + steps) % RING}

    across = {"dp": at_x * 2 * RING + (1 - at_y) * RING + at_z}
    peers = [neighbour(on_x, steps) for on_x in (True, False) for steps in (1, RING - 1)] + [across]
    for peer in peers:
        pl.semaphore_signal(barrier, inc=1, device_id=peer, device_id_type=pl.DeviceIdType.MESH)
    pl.semaphore_wait(barrier, 2 + len(peers))

    def to_other_core(slot):
        return pltpu.make_async_remote_copy(
            src_ref=send, dst_ref=recv.at[slot], send_sem=out_sem.at[slot],
            recv_sem=in_sem.at[slot], device_id={"tensor": 1 - tensor},
            device_id_type=pl.DeviceIdType.MESH,
        )

    def to_other_section(source, target, slot):
        return pltpu.make_async_remote_copy(
            src_ref=source, dst_ref=target, send_sem=pipe_out.at[slot],
            recv_sem=pipe_in.at[slot], device_id={"pipe": 1 - pipe},
            device_id_type=pl.DeviceIdType.MESH,
        )

    def forward_copy(c):
        return to_other_section(sec.at[c], hs.at[c], c)

    def backward_copy(c):
        return to_other_section(dgrad.at[c], dys.at[c], chunks + c)

    def exchanged(slot, part):
        send[...] = part.astype(BF16)
        copy = to_other_core(slot)
        copy.start()
        copy.wait()
        return send[...].astype(F32) + recv[slot].astype(F32)

    bucket = bucket_map(buckets)
    lane = lax.broadcasted_iota(jnp.int32, (LEN, LEN), 1)
    upper = lane >= HEAD
    bias[...] = jnp.zeros_like(bias)
    dsum[...] = jnp.zeros_like(dsum)
    own[...] = jnp.zeros_like(own)
    tables[...] = jnp.zeros_like(tables)

    def add_bias(b, carry):
        hit = bucket == b
        for pair in range(PAIRS):
            for side in range(2):
                at_lanes = pl.ds(side * LEN, LEN)
                bias[pair, :, at_lanes] = jnp.where(hit, table[b, 2 * pair + side], bias[pair, :, at_lanes])
        return carry

    lax.fori_loop(0, buckets, add_bias, 0)

    def stacked(values):
        zero = jnp.zeros_like(values)
        return jnp.concatenate([jnp.where(upper, zero, values), jnp.where(upper, values, zero)], axis=0)

    def unstacked(values):
        return jnp.where(upper, values[LEN:], values[:LEN])

    def per_head(values, reduce):
        left = reduce(values[:, :LEN], axis=1, keepdims=True)
        right = reduce(values[:, LEN:], axis=1, keepdims=True)
        return jnp.concatenate(
            [jnp.broadcast_to(left, (LEN, LEN)), jnp.broadcast_to(right, (LEN, LEN))], axis=1
        )

    def keep(tile, left, right):
        left, right = [
            side.reshape(RING, 2, RING, side.shape[0] // (2 * RING * RING), LEN) for side in (left, right)
        ]
        both = jnp.concatenate([left, right], axis=3).astype(BF16)
        grads[:, :, :, :, pl.ds(pl.multiple_of(tile * LEN, LEN), LEN)] = both

    def product_tiles(tile, lefts, rights, count):
        def one(n, carry):
            lanes = pl.ds(pl.multiple_of(n * 2 * LEN, 2 * LEN), 2 * LEN)
            made = dot(lefts[...], rights[:, lanes])
            keep(tile + n, made[:, :LEN], made[:, LEN:])
            return carry

        lax.fori_loop(0, count, one, 0)

    out_tiles = 2 * hidden // (2 * LEN)
    wides, narrows, doubles = (wide0, wide1, wide2), (narrow0, narrow1, narrow2), (pair0, pair1, pair2)

    def lanes_of(stage, part):
        begin, end = STAGES[stage]
        count = (end - begin) // 2
        return begin + part * count, count

    class Ring:
        def __init__(self, stage, part, phase):
            begin, count = lanes_of(stage, part)
            self.lanes = pl.ds(begin * LEN, count * LEN)
            self.part, self.phase = part, phase
            on_x = (part == 0) == (phase == 0)
            self.me = at_x if on_x else at_z
            self.up, self.down, self.far = [(self.me + steps) % RING for steps in (1, 3, 2)]
            self.landing = (wides, narrows)[phase][stage].at[part]
            base = ((stage * 2 + part) * 2 + phase) * 6
            plan = ((self.far, 0, 1), (self.far, 1, 3), (self.up, 1, 1), (self.down, 0, 3), (self.up, 0, 1), (self.down, 1, 3))
            slots = (0, 1, 3, 4, 2, 5)
            self.copies = [
                pltpu.make_async_remote_copy(
                    src_ref=self.block(whose, half), dst_ref=self.landing.at[slot], send_sem=ring_out.at[base + i],
                    recv_sem=ring_in.at[base + i], device_id=neighbour(on_x, steps),
                    device_id_type=pl.DeviceIdType.MESH,
                )
                for i, ((whose, half, steps), slot) in enumerate(zip(plan, slots))
            ]

        def block(self, whose, half):
            if self.phase == 0:
                if self.part == 0:
                    return grads.at[whose, half, :, :, self.lanes]
                return grads.at[:, half, whose, :, self.lanes]
            if self.part == 0:
                return grads.at[at_x, half, whose, :, self.lanes]
            return grads.at[whose, half, at_z, :, self.lanes]

        def pieces(self, refs):
            return [[ref.at[i] for ref in refs] for i in range(RING)] if self.phase == 0 else [refs]

        def add(self, *refs):
            for target, *others in self.pieces(refs):
                total = target[...].astype(F32)
                for other in others:
                    total = total + other[...].astype(F32)
                target[...] = total.astype(BF16)

        def begin(self):
            for copy in self.copies[:4]:
                copy.start()

        def relay(self):
            self.copies[0].wait_recv()
            self.add(self.block(self.up, 0), self.landing.at[0])
            self.copies[4].start()
            self.copies[1].wait_recv()
            self.add(self.block(self.down, 1), self.landing.at[1])
            self.copies[5].start()

        def close(self):
            for copy in self.copies[2:]:
                copy.wait_recv()
            for half in range(2):
                self.add(self.block(self.me, half), self.landing.at[2 + half], self.landing.at[4 + half])

        def drain(self):
            for copy in self.copies:
                copy.wait_send()

    rings = [[[Ring(stage, part, phase) for part in range(2)] for phase in range(2)] for stage in range(len(STAGES))]

    def swap(stage, part):
        begin, count = lanes_of(stage, part)
        slot = len(STAGES) * 24 + stage * 2 + part
        return pltpu.make_async_remote_copy(
            src_ref=grads.at[at_x, 1 - at_y, at_z, :, pl.ds(begin * LEN, count * LEN)],
            dst_ref=doubles[stage].at[part], send_sem=ring_out.at[slot], recv_sem=ring_in.at[slot],
            device_id=across, device_id_type=pl.DeviceIdType.MESH,
        )

    def begin(stage, phase):
        for ring in rings[stage][phase]:
            ring.begin()

    def relay(stage, phase):
        for ring in rings[stage][phase]:
            ring.relay()

    def close(stage, phase):
        for part, ring in enumerate(rings[stage][phase]):
            ring.close()
            if phase == 0:
                rings[stage][1][part].begin()
            else:
                swap(stage, part).start()

    def place_tile(tile, top, bottom):
        pair = pl.ds(tile % out_tiles * 2 * LEN, 2 * LEN)
        if tile < out_tiles:
            g_out[:, pair] = jnp.concatenate([top, bottom], axis=1)
        elif tile < 2 * out_tiles:
            within = (tile - out_tiles) * 2 * LEN
            g_in[within // hidden, :, pl.ds(within % hidden, 2 * LEN)] = jnp.concatenate([top, bottom], axis=1)
        elif tile < 2 * out_tiles + 5:
            at_block = 2 * (tile - 2 * out_tiles)
            g_qkv[at_block // PAIRS, :, pl.ds(at_block % PAIRS * LEN, LEN)] = top
            if tile < 2 * out_tiles + 4:
                g_qkv[(at_block + 1) // PAIRS, :, pl.ds((at_block + 1) % PAIRS * LEN, LEN)] = bottom
            else:
                g_att[:, 2 * LEN :] = bottom
        else:
            g_att[:, : 2 * LEN] = jnp.concatenate([top, bottom], axis=1)

    def settle(stage):
        for part in range(2):
            swap(stage, part).wait_recv()
            begin_tile, count = lanes_of(stage, part)
            lanes = pl.ds(begin_tile * LEN, count * LEN)
            total = grads[at_x, at_y, at_z, :, lanes].astype(F32) + doubles[stage][part].astype(F32)
            half = total.shape[0] // 2
            for i in range(count):
                here = slice(i * LEN, (i + 1) * LEN)
                place_tile(begin_tile + i, total[:half, here], total[half:, here])

    def lot(slot, source, target, peer):
        return pltpu.make_async_remote_copy(
            src_ref=source, dst_ref=lots.at[target], send_sem=lot_out.at[slot], recv_sem=lot_in.at[slot],
            device_id=peer, device_id_type=pl.DeviceIdType.MESH,
        )

    lot_copies = []
    for phase in range(2):
        up, down = neighbour(phase == 0, 1), neighbour(phase == 0, RING - 1)
        base = 4 * phase
        lot_copies += [
            lot(3 * phase, own.at[phase], base, up),
            lot(3 * phase + 1, own.at[phase], base + 1, down),
            lot(3 * phase + 2, lots.at[base], base + 2, up),
        ]
    lot_copies.append(lot(6, own.at[2], 8, across))

    def lots_open(phase):
        lot_copies[3 * phase].start()
        lot_copies[3 * phase + 1].start()

    def lots_pass(phase):
        lot_copies[3 * phase].wait_recv()
        lot_copies[3 * phase + 2].start()

    def lots_sum(phase):
        lot_copies[3 * phase + 1].wait_recv()
        lot_copies[3 * phase + 2].wait_recv()
        base = 4 * phase
        own[phase + 1] = (own[phase] + lots[base + 2]) + (lots[base] + lots[base + 1])

    def expert_gradients():
        product_tiles(0, rt, act2, out_tiles)
        begin(0, 0)
        product_tiles(out_tiles, nt, back2, out_tiles)
        begin(1, 0)

    for load in loads:
        load.wait()

    @pl.when(first)
    def _():
        load_x.wait()

    def forward(c, carry):
        @pl.when(last)
        def _():
            forward_copy(c).wait_recv()

        spot = pl.multiple_of(c * rows, rows)
        here = pl.ds(spot, rows)
        h = hs[c].astype(F32)
        scale = lax.rsqrt(jnp.mean(h * h, axis=1, keepdims=True) + epsilon)
        normed = (h * scale * gain_a[...]).astype(BF16)
        xt[:, here] = normed.T
        for part in range(3):
            proj[part, here, :] = dot(normed, wqkv[part]).astype(BF16)
        for s in range(SEQS):
            seq = pl.ds(pl.multiple_of(spot + s * LEN, LEN), LEN)
            along = jnp.broadcast_to(segs[pl.ds(c * SEQS + s, 1), :].astype(F32), (LEN, LEN))
            same = along == along.T
            same = jnp.concatenate([same, same], axis=1)
            for pair in range(PAIRS):
                lanes = pl.ds(pair * LEN, LEN)
                query = proj[0, seq, lanes]
                keys = stacked(proj[1, seq, lanes])
                values = stacked(proj[2, seq, lanes])
                scores = dot(query, keys, NT) * HEAD ** (-0.5) + bias[pair]
                scores = jnp.where(same, scores, masked_value)
                raised = jnp.exp(scores - per_head(scores, jnp.max))
                prob = raised / per_head(raised, jnp.sum)
                probs[c * SEQS + s, pair] = prob
                mixed[seq, lanes] = dot(prob.astype(BF16), values).astype(BF16)
        a = h + exchanged(4 * c, dot(mixed[here, :], watt[...]))
        after[here, :] = a
        scale = lax.rsqrt(jnp.mean(a * a, axis=1, keepdims=True) + epsilon)
        normed2 = (a * scale * gain_f[...]).astype(BF16)
        nt[:, here] = normed2.T
        route = routes[c]
        sign = (1 - 2 * route).astype(F32)
        logit = over_lanes(normed2.astype(F32) * rdiff[...])
        chosen = 1.0 / (1.0 + jnp.exp(-sign * logit))
        chosens[c] = chosen
        to_zero = (route == 0).astype(BF16)
        to_one = (route == 1).astype(BF16)
        doubled = jnp.concatenate([normed2 * to_zero, normed2 * to_one], axis=1)

        def inner_tile(n, carry):
            lanes = pl.ds(pl.multiple_of(n * step, step), step)
            inner = dot(doubled, win[:, lanes])
            squared = inner * inner
            root = np.sqrt(2 / np.pi).astype(np.float32)
            bend = jnp.tanh(root * inner * (1.0 + 0.044715 * squared))
            steep = 0.5 * (1.0 + bend) + 0.5 * inner * (1.0 - bend * bend) * root * (
                1.0 + 3 * 0.044715 * squared
            )
            slope[here, lanes] = steep.astype(BF16)
            active = (0.5 * inner * (1.0 + bend)).astype(BF16)
            act2[here, lanes] = active * to_zero
            act2[here, pl.ds(pl.multiple_of(hidden + n * step, step), step)] = active * to_one
            return carry

        lax.fori_loop(0, hidden // step, inner_tile, 0)
        total = exchanged(4 * c + 1, dot(act2[here, :], wout[...]))
        result[here, :] = total.astype(BF16)
        sec[c] = (after[here, :] + chosen * total).astype(BF16)

        @pl.when(first)
        def _():
            forward_copy(c).start()

        return carry

    lax.fori_loop(0, chunks, forward, 0)

    @pl.when(last)
    def _():
        load_dy.wait()

    def backward(c, carry):
        @pl.when(first)
        def _():
            backward_copy(c).wait_recv()

        spot = pl.multiple_of(c * rows, rows)
        here = pl.ds(spot, rows)
        dy = dys[c].astype(F32)
        route = routes[c]
        sign = (1 - 2 * route).astype(F32)
        to_zero = (route == 0).astype(BF16)
        to_one = (route == 1).astype(BF16)
        chosen = chosens[c]
        d_logit = sign * over_lanes(dy * result[here, :].astype(F32)) * chosen * (1.0 - chosen)
        d_result = (chosen * dy).astype(BF16)
        rt[:, here] = d_result.T
        zero_part = d_result * to_zero
        one_part = d_result * to_one

        def active_tile(n, carry):
            low = pl.multiple_of(n * step, step)
            high = pl.multiple_of(hidden + n * step, step)
            d_active = dot(zero_part, wout[pl.ds(low, step), :], NT) + dot(
                one_part, wout[pl.ds(high, step), :], NT
            )
            d_inner = (d_active * slope[here, pl.ds(low, step)].astype(F32)).astype(BF16)
            back2[here, pl.ds(low, step)] = d_inner * to_zero
            back2[here, pl.ds(high, step)] = d_inner * to_one
            return carry

        lax.fori_loop(0, hidden // step, active_tile, 0)

        @pl.when(first & (c == chunks - 1))
        def _():
            expert_gradients()

        d_normed2 = dot(back2[here, :hidden], win[:width, :], NT) + dot(
            back2[here, hidden:], win[width:, :], NT
        )
        d_normed2 = exchanged(4 * c + 2, d_normed2) + d_logit * rdiff[...]
        a = after[here, :]
        scale = lax.rsqrt(jnp.mean(a * a, axis=1, keepdims=True) + epsilon)
        plain = a * scale
        normed2 = (plain * gain_f[...]).astype(BF16).astype(F32)
        own[0, 1:2, :] += over_rows(d_normed2 * plain)
        own[0, 2:3, :] += over_rows(normed2 * d_logit)
        pulled = d_normed2 * gain_f[...]
        d_after = dy + scale * (pulled - plain * jnp.mean(pulled * plain, axis=1, keepdims=True))
        after[here, :] = d_after
        d_attn = d_after.astype(BF16)
        at[:, here] = d_attn.T
        d_mixed = dot(d_attn, watt[...], NT).astype(BF16)
        for s in range(SEQS):
            seq = pl.ds(pl.multiple_of(spot + s * LEN, LEN), LEN)
            for pair in range(PAIRS):
                lanes = pl.ds(pair * LEN, LEN)
                query = proj[0, seq, lanes]
                keys = stacked(proj[1, seq, lanes])
                values = stacked(proj[2, seq, lanes])
                prob = probs[c * SEQS + s, pair]
                d_mix = d_mixed[s * LEN : (s + 1) * LEN, pair * LEN : (pair + 1) * LEN]
                product = prob * dot(d_mix, values, NT)
                d_scores = (product - prob * per_head(product, jnp.sum)).astype(BF16)
                dsum[pair] += d_scores.astype(F32)
                dproj[seq, pl.ds(pair * LEN, LEN)] = (dot(d_scores, keys) * HEAD ** (-0.5)).astype(BF16)
                d_keys = unstacked(dot(d_scores, query, TN)) * HEAD ** (-0.5)
                dproj[seq, pl.ds((PAIRS + pair) * LEN, LEN)] = d_keys.astype(BF16)
                d_values = unstacked(dot(prob.astype(BF16), d_mix, TN))
                dproj[seq, pl.ds((2 * PAIRS + pair) * LEN, LEN)] = d_values.astype(BF16)
        part = PAIRS * LEN
        d_normed = dot(dproj[here, :part], wqkv[0], NT)
        d_normed = d_normed + dot(dproj[here, part : 2 * part], wqkv[1], NT)
        d_normed = d_normed + dot(dproj[here, 2 * part :], wqkv[2], NT)
        d_normed = exchanged(4 * c + 3, d_normed)
        h = hs[c].astype(F32)
        scale = lax.rsqrt(jnp.mean(h * h, axis=1, keepdims=True) + epsilon)
        plain = h * scale
        own[0, 0:1, :] += over_rows(d_normed * plain)
        pulled = d_normed * gain_a[...]
        d_hidden = after[here, :] + scale * (
            pulled - plain * jnp.mean(pulled * plain, axis=1, keepdims=True)
        )
        dgrad[c] = d_hidden.astype(BF16)

        @pl.when(last)
        def _():
            backward_copy(c).start()

        return carry

    lax.fori_loop(0, chunks, backward, 0)

    @pl.when(last)
    def _():
        expert_gradients()

    def table_rows(b, carry):
        hit = bucket == b
        for pair in range(PAIRS):
            for side in range(2):
                picked = jnp.where(hit, dsum[pair, :, pl.ds(side * LEN, LEN)], 0.0)
                tables[pl.ds((2 * pair + side) * buckets + b, 1), :] = over_rows(picked)
        return carry

    lax.fori_loop(0, buckets, table_rows, 0)
    own[0, 3:4, : 2 * LEN] = over_rows(tables[...].T)
    lots_open(0)
    relay(0, 0)
    product_tiles(2 * out_tiles, xt, dproj, 4)
    keep(2 * out_tiles + 4, dot(xt[...], dproj[:, 8 * LEN :]), dot(at[...], mixed[:, 2 * LEN :]))
    made = dot(at[...], mixed[:, : 2 * LEN])
    keep(2 * out_tiles + 5, made[:, :LEN], made[:, LEN:])
    begin(2, 0)
    lots_pass(0)
    relay(1, 0)
    lots_sum(0)
    lots_open(1)
    close(0, 0)
    lots_pass(1)
    relay(2, 0)
    lots_sum(1)
    lot_copies[6].start()
    relay(0, 1)
    close(1, 0)
    close(0, 1)
    relay(1, 1)
    close(2, 0)
    settle(0)
    close(1, 1)
    relay(2, 1)
    settle(1)
    lot_copies[6].wait_recv()
    small[...] = own[2] + lots[8]
    close(2, 1)
    settle(2)
    for copy in lot_copies:
        copy.wait_send()
    for stage in range(len(STAGES)):
        for part in range(2):
            rings[stage][0][part].drain()
            rings[stage][1][part].drain()
            swap(stage, part).wait_send()

    def finish(c, carry):
        @pl.when(first)
        def _():
            forward_copy(c).wait_send()

        @pl.when(last)
        def _():
            backward_copy(c).wait_send()

        return carry

    lax.fori_loop(0, chunks, finish, 0)


def local_pass(inputs, cotangent, segments, routes, gain_attn, w_qkv, rel_table, w_att_out, gain_ffn, router, w_in, w_out):
    micros, length, width = inputs.shape
    chunks = micros // SEQS
    rows = SEQS * length
    tokens = micros * length
    experts, _, hidden = w_in.shape
    heads = w_att_out.shape[0]
    buckets = rel_table.shape[0]
    columns = (3 * heads + heads + 2 * experts * hidden) // 2
    vmem = pl.BlockSpec(memory_space=pltpu.VMEM)
    smem = pl.BlockSpec(memory_space=pltpu.SMEM)
    anywhere = pl.BlockSpec(memory_space=pl.ANY)
    slots = 4 * chunks
    shard = width // (2 * RING * RING)
    double = 2 * shard
    pieces = [(end - begin) // 2 * LEN for begin, end in STAGES]
    scratch = [
        pltpu.VMEM(w_qkv.shape, BF16),
        pltpu.VMEM(w_att_out.shape, BF16),
        pltpu.VMEM((experts * width, hidden), BF16),
        pltpu.VMEM((experts * hidden, width), BF16),
        pltpu.VMEM((chunks, rows, width), BF16),
        pltpu.VMEM((chunks, rows, width), BF16),
        pltpu.VMEM((width, tokens), BF16),
        pltpu.VMEM((width, tokens), BF16),
        pltpu.VMEM((width, tokens), BF16),
        pltpu.VMEM((width, tokens), BF16),
        pltpu.VMEM((3, tokens, heads), BF16),
        pltpu.VMEM((micros, PAIRS, LEN, 2 * LEN), F32),
        pltpu.VMEM((tokens, heads), BF16),
        pltpu.VMEM((tokens, width), F32),
        pltpu.VMEM((tokens, hidden), BF16),
        pltpu.VMEM((tokens, experts * hidden), BF16),
        pltpu.VMEM((tokens, experts * hidden), BF16),
        pltpu.VMEM((tokens, width), BF16),
        pltpu.VMEM((chunks, rows, 1), F32),
        pltpu.VMEM((tokens, 3 * heads), BF16),
        pltpu.VMEM((rows, width), BF16),
        pltpu.VMEM((slots, rows, width), BF16),
        pltpu.VMEM((PAIRS, LEN, 2 * LEN), F32),
        pltpu.VMEM((PAIRS, LEN, 2 * LEN), F32),
        pltpu.VMEM((2 * LEN, LEN), F32),
        pltpu.VMEM((RING, 2, RING, double, columns), BF16),
        *[pltpu.VMEM((2, 6, RING, double, piece), BF16) for piece in pieces],
        *[pltpu.VMEM((2, 6, double, piece), BF16) for piece in pieces],
        *[pltpu.VMEM((2, double, piece), BF16) for piece in pieces],
        pltpu.VMEM((3, 8, width), F32),
        pltpu.VMEM((9, 8, width), F32),
        pltpu.SemaphoreType.DMA((5,)),
        pltpu.SemaphoreType.DMA((slots,)),
        pltpu.SemaphoreType.DMA((slots,)),
        pltpu.SemaphoreType.DMA((2 * chunks,)),
        pltpu.SemaphoreType.DMA((2 * chunks,)),
        pltpu.SemaphoreType.DMA((26 * len(STAGES),)),
        pltpu.SemaphoreType.DMA((26 * len(STAGES),)),
        pltpu.SemaphoreType.DMA((7,)),
        pltpu.SemaphoreType.DMA((7,)),
    ]
    return pl.pallas_call(
        kernel,
        out_shape=[
            jax.ShapeDtypeStruct((chunks, rows, width), BF16),
            jax.ShapeDtypeStruct((chunks, rows, width), BF16),
            jax.ShapeDtypeStruct((shard, experts * hidden), F32),
            jax.ShapeDtypeStruct((experts, shard, hidden), F32),
            jax.ShapeDtypeStruct((3, shard, heads), F32),
            jax.ShapeDtypeStruct((shard, heads), F32),
            jax.ShapeDtypeStruct((8, width), F32),
        ],
        in_specs=[anywhere, anywhere, vmem, vmem, vmem, smem, vmem, vmem] + [anywhere] * 4,
        out_specs=[vmem] * 7,
        scratch_shapes=scratch,
        compiler_params=pltpu.CompilerParams(
            collective_id=0, has_side_effects=True, vmem_limit_bytes=62 * 2**20
        ),
        cost_estimate=pl.CostEstimate(flops=18 * 10**9, bytes_accessed=30 * 10**6, transcendentals=10**6),
    )(
        inputs.reshape(chunks, rows, width),
        cotangent.reshape(chunks, rows, width),
        segments,
        routes.reshape(chunks, rows, 1),
        gain_attn,
        rel_table,
        gain_ffn,
        (router[:, 0] - router[:, 1])[None, :],
        w_qkv,
        w_att_out,
        w_in.reshape(experts * width, hidden),
        w_out.reshape(experts * hidden, width),
    )


def per_device(
    inputs, cotangent, segments, routes, gain_attn, w_qkv, rel_table, w_att_out, gain_ffn, router, w_in, w_out
):
    experts, width, hidden = w_in.shape[1:]
    sec, dgrad, g_out, g_in, g_qkv, g_att, small = local_pass(
        inputs, cotangent, segments, routes[0], gain_attn, w_qkv[0], rel_table[0], w_att_out[0],
        gain_ffn, router[0], w_in[0], w_out[0],
    )
    buckets, heads = rel_table.shape[1:]
    g_out = g_out.reshape(-1, experts, hidden).transpose(1, 2, 0)
    gain_a, gain_f, routed = small[0], small[1], small[2]
    table = small[3, : buckets * heads].reshape(heads, buckets).T
    micros, length = inputs.shape[:2]
    return (
        sec.reshape(1, micros, length, width),
        dgrad.reshape(1, micros, length, width),
        gain_a[None],
        g_qkv[None],
        table[None],
        g_att.T[None],
        gain_f[None],
        jnp.stack([routed, -routed], axis=1)[None],
        g_in[None],
        g_out[None],
    )


def solution(mesh):
    placed = (
        P(None, "dp", None),
        P(None, "dp", None),
        P(None, "dp"),
        P("pipe", None, "dp", None),
        P("pipe", None),
        P("pipe", None, None, "tensor"),
        P("pipe", None, "tensor"),
        P("pipe", "tensor", None),
        P("pipe", None),
        P("pipe", None, None),
        P("pipe", None, None, "tensor"),
        P("pipe", None, "tensor", None),
    )
    return jax.shard_map(
        per_device,
        mesh=mesh,
        in_specs=placed,
        out_specs=(
            P("pipe", None, "dp", None),
            P("pipe", None, "dp", None),
            P("pipe", None),
            P("pipe", None, "dp", "tensor"),
            P("pipe", None, "tensor"),
            P("pipe", "tensor", "dp"),
            P("pipe", None),
            P("pipe", None, None),
            P("pipe", None, "dp", "tensor"),
            P("pipe", None, "tensor", "dp"),
        ),
        check_vma=False,
    )
```

```python
import functools

import jax
import jax.numpy as jnp
import numpy as np
from jax import lax
from jax.experimental import pallas as pl
from jax.experimental.pallas import tpu as pltpu
from jax.sharding import PartitionSpec as P

HEAD = 64
LEN = 128
PAIRS = 3
SEQS = 2
RING = 4
PLAN = (
    ((0, 0, 4), (1, 4, 4), (2, 8, 2), (3, 10, 2)),
    ((0, 12, 4), (1, 16, 4), (2, 20, 2), (3, 22, 2)),
    ((0, 24, 3), (1, 27, 3)),
)
PIECES = [piece for stage in PLAN for piece in stage]
CUTS = 2
epsilon = 1e-06
masked_value = -1e30
F32 = jnp.float32
BF16 = jnp.bfloat16
NT = (((1,), (1,)), ((), ()))
TN = (((0,), (0,)), ((), ()))


def far_limits(buckets):
    half = buckets // 2
    exact = half // 2
    distance = np.arange(LEN)
    ratio = np.log(np.maximum(distance, 1) / exact) / np.log(128.0 / exact)
    bucket = np.minimum(exact + np.floor(ratio * (half - exact) + 1e-09).astype(np.int64), half - 1)
    bucket = np.where(distance < exact, distance, bucket)
    return [int(np.argmax(bucket >= b)) for b in range(1, half) if np.any(bucket >= b)]


def bucket_map(buckets):
    query = lax.broadcasted_iota(jnp.int32, (LEN, LEN), 0)
    key = lax.broadcasted_iota(jnp.int32, (LEN, LEN), 1)
    offset = key - query
    distance = jnp.abs(offset)
    bucket = jnp.where(offset > 0, buckets // 2, 0)
    for limit in far_limits(buckets):
        bucket = bucket + jnp.where(distance >= limit, 1, 0)
    return bucket


def dot(a, b, dims=None):
    if dims is None:
        return jnp.dot(a, b, preferred_element_type=F32)
    return lax.dot_general(a, b, dims, preferred_element_type=F32)


def over_rows(values):
    return jnp.sum(values, axis=0, keepdims=True)


def over_lanes(values):
    return jnp.sum(values, axis=1, keepdims=True)


def kernel(
    x_hbm, dy_hbm, segs_hbm, routes_hbm, gain_a, table, gain_f, router, wqkv_hbm, watt_hbm, win_hbm, wout_hbm,
    sec_hbm, dgrad_hbm, g_out, g_in, g_qkv, g_att, g_gain_a, g_gain_f, g_router, g_table,
    segs, routes, signs, sec, dgrad, wqkv, watt, win, wout, hs, dys, xt, nt, rt, at, proj, probs, mixed, after,
    slope, act2, back2, result, chosens, dproj, send, recv, bias, dsum, tables, grads, own, lots,
    load_sem, out_sem, in_sem, pipe_out, pipe_in, half_out, half_in, far_out, far_in, ring_out, ring_in,
    lot_out, lot_in, *landings,
):
    pipe = lax.axis_index("pipe")
    tensor = lax.axis_index("tensor")
    first = pipe == 0
    last = pipe == 1
    chunks, rows, width = hs.shape
    hidden = slope.shape[-1]
    step = 512
    buckets = table.shape[-1]

    loads = [
        pltpu.make_async_copy(source, target, load_sem.at[i])
        for i, (source, target) in enumerate(
            ((wqkv_hbm, wqkv), (watt_hbm, watt), (win_hbm, win), (wout_hbm, wout))
        )
    ]
    loads_first = [
        pltpu.make_async_copy(source, target, load_sem.at[4 + i])
        for i, (source, target) in enumerate(((x_hbm, hs), (segs_hbm, segs), (routes_hbm, routes)))
    ]

    @pl.when(first)
    def _():
        for load in loads_first:
            load.start()

    for load in loads:
        load.start()

    barrier = pltpu.get_barrier_semaphore()
    pl.semaphore_signal(barrier, inc=1, device_id={"tensor": 1 - tensor}, device_id_type=pl.DeviceIdType.MESH)
    place = lax.axis_index("dp")
    at_x, at_y, at_z = place // (2 * RING), place // RING % 2, place % RING

    def neighbour(on_x, steps):
        if on_x:
            return {"dp": (at_x + steps) % RING * 2 * RING + at_y * RING + at_z}
        return {"dp": at_x * 2 * RING + at_y * RING + (at_z + steps) % RING}

    across = {"dp": at_x * 2 * RING + (1 - at_y) * RING + at_z}
    next_section = {"pipe": 1 - pipe, **across}
    peers = [next_section] + [neighbour(on_x, steps) for on_x in (True, False) for steps in (1, RING - 1)] + [across]

    def remote(source, target, out, into, device):
        return pltpu.make_async_remote_copy(
            src_ref=source, dst_ref=target, send_sem=out, recv_sem=into, device_id=device,
            device_id_type=pl.DeviceIdType.MESH,
        )

    for peer in peers:
        pl.semaphore_signal(barrier, inc=1, device_id=peer, device_id_type=pl.DeviceIdType.MESH)
    pl.semaphore_wait(barrier, 1 + len(peers))

    other_core = {"tensor": 1 - tensor}
    loads_last = [
        remote(source, target, far_out.at[i], far_in.at[i], across)
        for i, (source, target) in enumerate(((segs_hbm, segs), (routes_hbm, routes), (dy_hbm, dys)))
    ]

    @pl.when(last)
    def _():
        for load in loads_last:
            load.start()

    def to_other_core(slot):
        return remote(send, recv.at[slot], out_sem.at[slot], in_sem.at[slot], other_core)

    def crossing(source, target, c, back):
        length = rows // (2 * CUTS)
        sends, shares = [], []
        for i in range(CUTS):
            here = pl.ds(pl.multiple_of((tensor * CUTS + i) * length, length), length)
            slot = (back * chunks + c) * CUTS + i
            sends.append(
                remote(source.at[c, here], target.at[c, here], pipe_out.at[slot], pipe_in.at[slot], next_section)
            )
            shares.append(
                remote(target.at[c, here], target.at[c, here], half_out.at[slot], half_in.at[slot], other_core)
            )
        return sends, shares

    def cross(crossed):
        for copy in crossed[0]:
            copy.start()

    def land(crossed):
        for arrived, share in zip(*crossed):
            arrived.wait_recv()
            share.start()
        for share in crossed[1]:
            share.wait_recv()

    def forward_copy(c):
        return crossing(sec, hs, c, 0)

    def backward_copy(c):
        return crossing(dgrad, dys, c, 1)

    def give(source, target, c, back):
        slot = back * chunks + c
        stays = pltpu.make_async_copy(source.at[c], target.at[c], load_sem.at[7 + slot])
        leaves = remote(source.at[c], target.at[c], far_out.at[3 + slot], far_in.at[3 + slot], across)
        return stays, leaves

    def give_start(given):
        @pl.when(first)
        def _():
            given[0].start()

        @pl.when(last)
        def _():
            given[1].start()

    def give_wait(given):
        @pl.when(first)
        def _():
            given[0].wait()

        @pl.when(last)
        def _():
            given[1].wait()

    def exchanged(slot, part):
        send[...] = part.astype(BF16)
        copy = to_other_core(slot)
        copy.start()
        copy.wait()
        return send[...].astype(F32) + recv[slot].astype(F32)

    bucket = bucket_map(buckets)
    lane = lax.broadcasted_iota(jnp.int32, (LEN, LEN), 1)
    upper = lane >= HEAD
    bias[...] = jnp.zeros_like(bias)
    dsum[...] = jnp.zeros_like(dsum)
    own[...] = jnp.zeros_like(own)
    tables[...] = jnp.zeros_like(tables)

    def add_bias(b, carry):
        hit = bucket == b
        for pair in range(PAIRS):
            for side in range(2):
                at_lanes = pl.ds(side * LEN, LEN)
                bias[pair, :, at_lanes] = jnp.where(hit, table[2 * pair + side, 0, b], bias[pair, :, at_lanes])
        return carry

    lax.fori_loop(0, buckets, add_bias, 0)

    def stacked(values):
        zero = jnp.zeros_like(values)
        return jnp.concatenate([jnp.where(upper, zero, values), jnp.where(upper, values, zero)], axis=0)

    def unstacked(values):
        return jnp.where(upper, values[LEN:], values[:LEN])

    def per_head(values, reduce):
        left = reduce(values[:, :LEN], axis=1, keepdims=True)
        right = reduce(values[:, LEN:], axis=1, keepdims=True)
        return jnp.concatenate(
            [jnp.broadcast_to(left, (LEN, LEN)), jnp.broadcast_to(right, (LEN, LEN))], axis=1
        )

    def keep(tile, left, right):
        left, right = [
            side.reshape(RING, 2, RING, side.shape[0] // (2 * RING * RING), LEN) for side in (left, right)
        ]
        both = jnp.concatenate([left, right], axis=3).astype(BF16)
        grads[:, :, :, :, pl.ds(pl.multiple_of(tile * LEN, LEN), LEN)] = both

    def product_tiles(tile, lefts, rights, count):
        def one(n, carry):
            lanes = pl.ds(pl.multiple_of(n * 2 * LEN, 2 * LEN), 2 * LEN)
            made = dot(lefts[...], rights[:, lanes])
            keep(tile + n, made[:, :LEN], made[:, LEN:])
            return carry

        lax.fori_loop(0, count, one, 0)

    out_tiles = 2 * hidden // (2 * LEN)
    class Ring:
        def __init__(self, index, phase):
            kind, begin, count = PIECES[index]
            self.lanes = pl.ds(begin * LEN, count * LEN)
            self.fine = [pl.ds((begin + i * (count // 2)) * LEN, count // 2 * LEN) for i in range(2)]
            self.kind, self.phase = kind, phase
            on_x = (kind % 2 == 0) == (phase == 0)
            self.me = at_x if on_x else at_z
            self.up, self.down, self.far = [(self.me + steps) % RING for steps in (1, 3, 2)]
            self.landing = landings[3 * index + phase]
            base = index * 13 + phase * 6
            plan = ((self.far, 0, 1), (self.far, 1, 3), (self.up, 1, 1), (self.down, 0, 3), (self.up, 0, 1), (self.down, 1, 3))
            slots = (0, 1, 3, 4, 2, 5)
            self.copies = [
                remote(
                    self.block(whose, half), self.landing.at[slot], ring_out.at[base + i], ring_in.at[base + i],
                    neighbour(on_x, steps),
                )
                for i, ((whose, half, steps), slot) in enumerate(zip(plan, slots))
            ]

        def block(self, whose, half):
            if self.phase == 0:
                two = pl.ds(2 * half, 2)
                if self.kind == 0:
                    return grads.at[whose, half, :, :, self.lanes]
                if self.kind == 1:
                    return grads.at[:, half, whose, :, self.lanes]
                if self.kind == 2:
                    return grads.at[whose, at_y, two, :, self.lanes]
                return grads.at[two, at_y, whose, :, self.lanes]
            if self.kind == 0:
                return grads.at[at_x, half, whose, :, self.lanes]
            if self.kind == 1:
                return grads.at[whose, half, at_z, :, self.lanes]
            if self.kind == 2:
                return grads.at[at_x, at_y, whose, :, self.fine[half]]
            return grads.at[whose, at_y, at_z, :, self.fine[half]]

        def add(self, *refs):
            if self.phase == 0:
                for i in range(refs[1].shape[0]):
                    add_up(*[ref.at[i] for ref in refs])
            else:
                add_up(*refs)

        def begin(self):
            for copy in self.copies[:4]:
                copy.start()

        def relay(self):
            self.copies[0].wait_recv()
            self.add(self.block(self.up, 0), self.landing.at[0])
            self.copies[4].start()
            self.copies[1].wait_recv()
            self.add(self.block(self.down, 1), self.landing.at[1])
            self.copies[5].start()

        def close(self):
            for copy in self.copies[2:]:
                copy.wait_recv()
            for half in range(2):
                self.add(self.block(self.me, half), self.landing.at[2 + half], self.landing.at[4 + half])

        def drain(self):
            for copy in self.copies:
                copy.wait_send()

    def add_up(target, *others):
        total = target[...].astype(F32)
        for other in others:
            total = total + other[...].astype(F32)
        target[...] = total.astype(BF16)

    class Piece:
        def __init__(self, index):
            kind, self.tile, self.count = PIECES[index]
            self.lanes = pl.ds(self.tile * LEN, self.count * LEN)
            self.early = kind >= 2
            self.rings = [Ring(index, phase) for phase in range(2)]
            self.landing = landings[3 * index + 2]
            theirs = grads.at[:, 1 - at_y, :, :, self.lanes] if self.early else grads.at[at_x, 1 - at_y, at_z, :, self.lanes]
            slot = index * 13 + 12
            self.swap = remote(theirs, self.landing, ring_out.at[slot], ring_in.at[slot], across)

        def open(self):
            if self.early:
                self.swap.start()
            else:
                self.rings[0].begin()

        def join(self):
            self.swap.wait_recv()

            def one(i, carry):
                for j in range(RING):
                    add_up(grads.at[i, at_y, j, :, self.lanes], self.landing.at[i, j])
                return carry

            lax.fori_loop(0, RING, one, 0)
            self.rings[0].begin()

        def turn(self):
            self.rings[0].close()
            self.rings[1].begin()

        def last(self):
            self.rings[1].close()
            if not self.early:
                self.swap.start()

        def settle(self):
            total = grads[at_x, at_y, at_z, :, self.lanes].astype(F32)
            if not self.early:
                self.swap.wait_recv()
                total = total + self.landing[...].astype(F32)
            half = total.shape[0] // 2
            for i in range(self.count):
                here = slice(i * LEN, (i + 1) * LEN)
                place_tile(self.tile + i, total[:half, here], total[half:, here])

        def drain(self):
            for ring in self.rings:
                ring.drain()
            self.swap.wait_send()

    pieces, made = [], 0
    for stage in PLAN:
        pieces.append([Piece(made + i) for i in range(len(stage))])
        made += len(stage)

    def begin(stage):
        for piece in pieces[stage]:
            piece.open()

    def relay(stage, phase, early):
        for piece in pieces[stage]:
            if piece.early == early:
                piece.rings[phase].relay()

    def turn(stage, early):
        for piece in pieces[stage]:
            if piece.early == early:
                piece.turn()

    def finish_rings(stage, early):
        for piece in pieces[stage]:
            if piece.early == early:
                piece.last()

    def join(stage):
        for piece in pieces[stage]:
            if piece.early:
                piece.join()

    def settle(stage):
        for piece in pieces[stage]:
            piece.settle()

    def place_tile(tile, top, bottom):
        if tile < 2 * out_tiles:
            target = g_out if tile < out_tiles else g_in
            within = tile % out_tiles * 2 * LEN
            target[within // hidden, :, pl.ds(within % hidden, 2 * LEN)] = jnp.concatenate([top, bottom], axis=1)
        elif tile < 2 * out_tiles + 5:
            at_block = 2 * (tile - 2 * out_tiles)
            g_qkv[at_block // PAIRS, :, pl.ds(at_block % PAIRS * LEN, LEN)] = top
            if tile < 2 * out_tiles + 4:
                g_qkv[(at_block + 1) // PAIRS, :, pl.ds((at_block + 1) % PAIRS * LEN, LEN)] = bottom
            else:
                g_att[:, 2 * LEN :] = bottom
        else:
            g_att[:, : 2 * LEN] = jnp.concatenate([top, bottom], axis=1)

    def lot(slot, source, target, peer):
        return pltpu.make_async_remote_copy(
            src_ref=source, dst_ref=lots.at[target], send_sem=lot_out.at[slot], recv_sem=lot_in.at[slot],
            device_id=peer, device_id_type=pl.DeviceIdType.MESH,
        )

    lot_copies = []
    for phase in range(2):
        up, down = neighbour(phase == 0, 1), neighbour(phase == 0, RING - 1)
        base = 4 * phase
        lot_copies += [
            lot(3 * phase, own.at[phase], base, up),
            lot(3 * phase + 1, own.at[phase], base + 1, down),
            lot(3 * phase + 2, lots.at[base], base + 2, up),
        ]
    lot_copies.append(lot(6, own.at[2], 8, across))

    def lots_open(phase):
        lot_copies[3 * phase].start()
        lot_copies[3 * phase + 1].start()

    def lots_pass(phase):
        lot_copies[3 * phase].wait_recv()
        lot_copies[3 * phase + 2].start()

    def lots_sum(phase):
        lot_copies[3 * phase + 1].wait_recv()
        lot_copies[3 * phase + 2].wait_recv()
        base = 4 * phase
        own[phase + 1] = (own[phase] + lots[base + 2]) + (lots[base] + lots[base + 1])

    def expert_gradients():
        product_tiles(0, rt, act2, out_tiles)
        begin(0)
        product_tiles(out_tiles, nt, back2, out_tiles)
        begin(1)

    @pl.when(first)
    def _():
        for load in loads_first:
            load.wait()

    @pl.when(last)
    def _():
        for load in loads_last[:2]:
            load.wait_recv()

    split = router[0:1, :] - router[1:2, :]

    def column(values):
        return jnp.broadcast_to(values, (LEN, LEN)).T[:, :1]

    def sign_rows(c, carry):
        for s in range(SEQS):
            signs[c, pl.ds(s * LEN, LEN), :] = column((1 - 2 * routes[c * SEQS + s]).astype(F32))
        return carry

    lax.fori_loop(0, chunks, sign_rows, 0)
    for load in loads:
        load.wait()

    def forward(c, carry):
        @pl.when(last)
        def _():
            land(forward_copy(c))

        spot = pl.multiple_of(c * rows, rows)
        here = pl.ds(spot, rows)
        h = hs[c].astype(F32)
        scale = lax.rsqrt(jnp.mean(h * h, axis=1, keepdims=True) + epsilon)
        normed = (h * scale * gain_a[...]).astype(BF16)
        xt[:, here] = normed.T
        for part in range(3):
            proj[part, here, :] = dot(normed, wqkv[part]).astype(BF16)
        for s in range(SEQS):
            seq = pl.ds(pl.multiple_of(spot + s * LEN, LEN), LEN)
            along = jnp.broadcast_to(segs[pl.ds(c * SEQS + s, 1), :].astype(F32), (LEN, LEN))
            same = along == along.T
            same = jnp.concatenate([same, same], axis=1)
            for pair in range(PAIRS):
                lanes = pl.ds(pair * LEN, LEN)
                query = proj[0, seq, lanes]
                keys = stacked(proj[1, seq, lanes])
                values = stacked(proj[2, seq, lanes])
                scores = dot(query, keys, NT) * HEAD ** (-0.5) + bias[pair]
                scores = jnp.where(same, scores, masked_value)
                raised = jnp.exp(scores - per_head(scores, jnp.max))
                prob = raised / per_head(raised, jnp.sum)
                probs[c * SEQS + s, pair] = prob
                mixed[seq, lanes] = dot(prob.astype(BF16), values).astype(BF16)
        a = h + exchanged(4 * c, dot(mixed[here, :], watt[...]))
        after[here, :] = a
        scale = lax.rsqrt(jnp.mean(a * a, axis=1, keepdims=True) + epsilon)
        normed2 = (a * scale * gain_f[...]).astype(BF16)
        nt[:, here] = normed2.T
        sign = signs[c]
        logit = over_lanes(normed2.astype(F32) * split)
        chosen = 1.0 / (1.0 + jnp.exp(-sign * logit))
        chosens[c] = chosen
        to_zero = (sign > 0).astype(BF16)
        to_one = (sign < 0).astype(BF16)
        doubled = jnp.concatenate([normed2 * to_zero, normed2 * to_one], axis=1)

        def inner_tile(n, carry):
            lanes = pl.ds(pl.multiple_of(n * step, step), step)
            inner = dot(doubled, win[:, lanes])
            squared = inner * inner
            root = np.sqrt(2 / np.pi).astype(np.float32)
            bend = jnp.tanh(root * inner * (1.0 + 0.044715 * squared))
            steep = 0.5 * (1.0 + bend) + 0.5 * inner * (1.0 - bend * bend) * root * (
                1.0 + 3 * 0.044715 * squared
            )
            slope[here, lanes] = steep.astype(BF16)
            active = (0.5 * inner * (1.0 + bend)).astype(BF16)
            act2[here, lanes] = active * to_zero
            act2[here, pl.ds(pl.multiple_of(hidden + n * step, step), step)] = active * to_one
            return carry

        lax.fori_loop(0, hidden // step, inner_tile, 0)
        total = exchanged(4 * c + 1, dot(act2[here, :], wout[...]))
        result[here, :] = total.astype(BF16)
        sec[c] = (after[here, :] + chosen * total).astype(BF16)

        @pl.when(first)
        def _():
            cross(forward_copy(c))

        give_start(give(sec, sec_hbm, c, 0))

        return carry

    lax.fori_loop(0, chunks, forward, 0)

    @pl.when(last)
    def _():
        loads_last[2].wait_recv()

    def backward(c, carry):
        @pl.when(first)
        def _():
            land(backward_copy(c))

        spot = pl.multiple_of(c * rows, rows)
        here = pl.ds(spot, rows)
        dy = dys[c].astype(F32)
        sign = signs[c]
        to_zero = (sign > 0).astype(BF16)
        to_one = (sign < 0).astype(BF16)
        chosen = chosens[c]
        d_logit = sign * over_lanes(dy * result[here, :].astype(F32)) * chosen * (1.0 - chosen)
        d_result = (chosen * dy).astype(BF16)
        rt[:, here] = d_result.T
        zero_part = d_result * to_zero
        one_part = d_result * to_one

        def active_tile(n, carry):
            low = pl.multiple_of(n * step, step)
            high = pl.multiple_of(hidden + n * step, step)
            d_active = dot(zero_part, wout[pl.ds(low, step), :], NT) + dot(
                one_part, wout[pl.ds(high, step), :], NT
            )
            d_inner = (d_active * slope[here, pl.ds(low, step)].astype(F32)).astype(BF16)
            back2[here, pl.ds(low, step)] = d_inner * to_zero
            back2[here, pl.ds(high, step)] = d_inner * to_one
            return carry

        lax.fori_loop(0, hidden // step, active_tile, 0)

        @pl.when(first & (c == chunks - 1))
        def _():
            expert_gradients()

        d_normed2 = dot(back2[here, :hidden], win[:width, :], NT) + dot(
            back2[here, hidden:], win[width:, :], NT
        )
        d_normed2 = exchanged(4 * c + 2, d_normed2) + d_logit * split
        a = after[here, :]
        scale = lax.rsqrt(jnp.mean(a * a, axis=1, keepdims=True) + epsilon)
        plain = a * scale
        normed2 = (plain * gain_f[...]).astype(BF16).astype(F32)
        own[0, 1:2, :] += over_rows(d_normed2 * plain)
        own[0, 2:3, :] += over_rows(normed2 * d_logit)
        pulled = d_normed2 * gain_f[...]
        d_after = dy + scale * (pulled - plain * jnp.mean(pulled * plain, axis=1, keepdims=True))
        after[here, :] = d_after
        d_attn = d_after.astype(BF16)
        at[:, here] = d_attn.T
        d_mixed = dot(d_attn, watt[...], NT).astype(BF16)
        for s in range(SEQS):
            seq = pl.ds(pl.multiple_of(spot + s * LEN, LEN), LEN)
            for pair in range(PAIRS):
                lanes = pl.ds(pair * LEN, LEN)
                query = proj[0, seq, lanes]
                keys = stacked(proj[1, seq, lanes])
                values = stacked(proj[2, seq, lanes])
                prob = probs[c * SEQS + s, pair]
                d_mix = d_mixed[s * LEN : (s + 1) * LEN, pair * LEN : (pair + 1) * LEN]
                product = prob * dot(d_mix, values, NT)
                d_scores = (product - prob * per_head(product, jnp.sum)).astype(BF16)
                dsum[pair] += d_scores.astype(F32)
                dproj[seq, pl.ds(pair * LEN, LEN)] = (dot(d_scores, keys) * HEAD ** (-0.5)).astype(BF16)
                d_keys = unstacked(dot(d_scores, query, TN)) * HEAD ** (-0.5)
                dproj[seq, pl.ds((PAIRS + pair) * LEN, LEN)] = d_keys.astype(BF16)
                d_values = unstacked(dot(prob.astype(BF16), d_mix, TN))
                dproj[seq, pl.ds((2 * PAIRS + pair) * LEN, LEN)] = d_values.astype(BF16)
        part = PAIRS * LEN
        d_normed = dot(dproj[here, :part], wqkv[0], NT)
        d_normed = d_normed + dot(dproj[here, part : 2 * part], wqkv[1], NT)
        d_normed = d_normed + dot(dproj[here, 2 * part :], wqkv[2], NT)
        d_normed = exchanged(4 * c + 3, d_normed)
        h = hs[c].astype(F32)
        scale = lax.rsqrt(jnp.mean(h * h, axis=1, keepdims=True) + epsilon)
        plain = h * scale
        own[0, 0:1, :] += over_rows(d_normed * plain)
        pulled = d_normed * gain_a[...]
        d_hidden = after[here, :] + scale * (
            pulled - plain * jnp.mean(pulled * plain, axis=1, keepdims=True)
        )
        dgrad[c] = d_hidden.astype(BF16)

        @pl.when(last)
        def _():
            cross(backward_copy(c))

        give_start(give(dgrad, dgrad_hbm, c, 1))

        return carry

    lax.fori_loop(0, chunks, backward, 0)

    @pl.when(last)
    def _():
        expert_gradients()

    def table_rows(b, carry):
        hit = bucket == b
        for pair in range(PAIRS):
            for side in range(2):
                picked = jnp.where(hit, dsum[pair, :, pl.ds(side * LEN, LEN)], 0.0)
                tables[pl.ds((2 * pair + side) * LEN + b, 1), :] = over_rows(picked)
        return carry

    lax.fori_loop(0, buckets, table_rows, 0)
    own[0, 3:4, :] = over_rows(tables[...].T)
    lots_open(0)
    relay(0, 0, False)
    product_tiles(2 * out_tiles, xt, dproj, 4)
    keep(2 * out_tiles + 4, dot(xt[...], dproj[:, 8 * LEN :]), dot(at[...], mixed[:, 2 * LEN :]))
    made = dot(at[...], mixed[:, : 2 * LEN])
    keep(2 * out_tiles + 5, made[:, :LEN], made[:, LEN:])
    begin(2)
    join(0)
    lots_pass(0)
    relay(1, 0, False)
    lots_sum(0)
    lots_open(1)
    turn(0, False)
    join(1)
    relay(0, 0, True)
    lots_pass(1)
    relay(2, 0, False)
    lots_sum(1)
    lot_copies[6].start()
    relay(0, 1, False)
    turn(1, False)
    turn(0, True)
    relay(1, 0, True)
    finish_rings(0, False)
    relay(1, 1, False)
    turn(2, False)
    relay(0, 1, True)
    turn(1, True)
    finish_rings(1, False)
    relay(2, 1, False)
    finish_rings(0, True)
    settle(0)
    relay(1, 1, True)
    finish_rings(2, False)
    finish_rings(1, True)
    settle(1)
    lot_copies[6].wait_recv()
    small = own[2] + lots[8]
    g_gain_a[...] = small[0:1, :]
    g_gain_f[...] = small[1:2, :]
    g_router[0:1, :] = small[2:3, :]
    g_router[1:2, :] = -small[2:3, :]
    for head in range(2 * PAIRS):
        g_table[head] = small[3:4, head * LEN : head * LEN + buckets]
    settle(2)
    for copy in lot_copies:
        copy.wait_send()
    for stage in pieces:
        for piece in stage:
            piece.drain()

    @pl.when(last)
    def _():
        for load in loads_last:
            load.wait_send()

    def finish(c, carry):
        give_wait(give(sec, sec_hbm, c, 0))
        give_wait(give(dgrad, dgrad_hbm, c, 1))

        @pl.when(first)
        def _():
            for copy in forward_copy(c)[0] + backward_copy(c)[1]:
                copy.wait_send()

        @pl.when(last)
        def _():
            for copy in backward_copy(c)[0] + forward_copy(c)[1]:
                copy.wait_send()

        return carry

    lax.fori_loop(0, chunks, finish, 0)


def copy_out(*refs):
    count = len(refs) // 3
    sources, targets, held = refs[:count], refs[count : 2 * count], refs[2 * count : 3 * count]
    sem_in, sem_out = refs[3 * count :]
    arrive = [pltpu.make_async_copy(*ends, sem_in.at[i]) for i, ends in enumerate(zip(sources, held))]
    leave = [pltpu.make_async_copy(*ends, sem_out.at[i]) for i, ends in enumerate(zip(held, targets))]
    for copy in arrive:
        copy.start()
    for first, second in zip(arrive, leave):
        first.wait()
        second.start()
    for copy in leave:
        copy.wait()


def local_pass(inputs, cotangent, segments, routes, gain_attn, w_qkv, rel_table, w_att_out, gain_ffn, router, w_in, w_out):
    micros, length, width = inputs.shape
    chunks = micros // SEQS
    rows = SEQS * length
    tokens = micros * length
    experts, _, hidden = w_in.shape
    heads = w_att_out.shape[0]
    buckets = rel_table.shape[1]
    count = len(PIECES)
    columns = (3 * heads + heads + 2 * experts * hidden) // 2
    vmem = pl.BlockSpec(memory_space=pltpu.VMEM)
    smem = pl.BlockSpec(memory_space=pltpu.SMEM)
    anywhere = pl.BlockSpec(memory_space=pl.ANY)
    slots = 4 * chunks
    shard = width // (2 * RING * RING)
    double = 2 * shard
    landings = []
    for kind, _, tiles in PIECES:
        wide = tiles * LEN
        if kind < 2:
            landings += [(6, RING, double, wide), (6, double, wide), (double, wide)]
        else:
            landings += [(6, 2, double, wide), (6, double, wide // 2), (RING, RING, double, wide)]
    scratch = [
        pltpu.VMEM((micros, length), jnp.int32),
        pltpu.VMEM((micros, 1, length), jnp.int32),
        pltpu.VMEM((chunks, rows, 1), F32),
        pltpu.VMEM((chunks, rows, width), BF16),
        pltpu.VMEM((chunks, rows, width), BF16),
        pltpu.VMEM(w_qkv.shape, BF16),
        pltpu.VMEM(w_att_out.shape, BF16),
        pltpu.VMEM((experts * width, hidden), BF16),
        pltpu.VMEM((experts * hidden, width), BF16),
        pltpu.VMEM((chunks, rows, width), BF16),
        pltpu.VMEM((chunks, rows, width), BF16),
        pltpu.VMEM((width, tokens), BF16),
        pltpu.VMEM((width, tokens), BF16),
        pltpu.VMEM((width, tokens), BF16),
        pltpu.VMEM((width, tokens), BF16),
        pltpu.VMEM((3, tokens, heads), BF16),
        pltpu.VMEM((micros, PAIRS, LEN, 2 * LEN), F32),
        pltpu.VMEM((tokens, heads), BF16),
        pltpu.VMEM((tokens, width), F32),
        pltpu.VMEM((tokens, hidden), BF16),
        pltpu.VMEM((tokens, experts * hidden), BF16),
        pltpu.VMEM((tokens, experts * hidden), BF16),
        pltpu.VMEM((tokens, width), BF16),
        pltpu.VMEM((chunks, rows, 1), F32),
        pltpu.VMEM((tokens, 3 * heads), BF16),
        pltpu.VMEM((rows, width), BF16),
        pltpu.VMEM((slots, rows, width), BF16),
        pltpu.VMEM((PAIRS, LEN, 2 * LEN), F32),
        pltpu.VMEM((PAIRS, LEN, 2 * LEN), F32),
        pltpu.VMEM((2 * PAIRS * LEN, LEN), F32),
        pltpu.VMEM((RING, 2, RING, double, columns), BF16),
        pltpu.VMEM((3, 8, width), F32),
        pltpu.VMEM((9, 8, width), F32),
        pltpu.SemaphoreType.DMA((7 + 2 * chunks,)),
        pltpu.SemaphoreType.DMA((slots,)),
        pltpu.SemaphoreType.DMA((slots,)),
        pltpu.SemaphoreType.DMA((2 * chunks * CUTS,)),
        pltpu.SemaphoreType.DMA((2 * chunks * CUTS,)),
        pltpu.SemaphoreType.DMA((2 * chunks * CUTS,)),
        pltpu.SemaphoreType.DMA((2 * chunks * CUTS,)),
        pltpu.SemaphoreType.DMA((3 + 2 * chunks,)),
        pltpu.SemaphoreType.DMA((3 + 2 * chunks,)),
        pltpu.SemaphoreType.DMA((13 * count,)),
        pltpu.SemaphoreType.DMA((13 * count,)),
        pltpu.SemaphoreType.DMA((7,)),
        pltpu.SemaphoreType.DMA((7,)),
        *[pltpu.VMEM(shape, BF16) for shape in landings],
    ]
    results = pl.pallas_call(
        kernel,
        out_shape=[
            jax.ShapeDtypeStruct((chunks, rows, width), BF16),
            jax.ShapeDtypeStruct((chunks, rows, width), BF16),
            jax.ShapeDtypeStruct((experts, shard, hidden), F32),
            jax.ShapeDtypeStruct((experts, shard, hidden), F32),
            jax.ShapeDtypeStruct((3, shard, heads), F32),
            jax.ShapeDtypeStruct((shard, heads), F32),
            jax.ShapeDtypeStruct((1, width), F32),
            jax.ShapeDtypeStruct((1, width), F32),
            jax.ShapeDtypeStruct((2, width), F32),
            jax.ShapeDtypeStruct((2 * PAIRS, 1, buckets), F32),
        ],
        in_specs=[anywhere] * 4 + [vmem, smem, vmem, vmem] + [anywhere] * 4,
        out_specs=[anywhere] * 2 + [vmem] * 8,
        scratch_shapes=scratch,
        compiler_params=pltpu.CompilerParams(
            collective_id=0, has_side_effects=True, vmem_limit_bytes=62 * 2**20
        ),
        cost_estimate=pl.CostEstimate(flops=18 * 10**9, bytes_accessed=30 * 10**6, transcendentals=10**6),
    )(
        inputs.reshape(chunks, rows, width),
        cotangent.reshape(chunks, rows, width),
        segments,
        jnp.swapaxes(routes, 1, 2),
        gain_attn,
        jnp.transpose(rel_table, (2, 0, 1)),
        gain_ffn,
        router.T,
        w_qkv,
        w_att_out,
        w_in.reshape(experts * width, hidden),
        w_out.reshape(experts * hidden, width),
    )
    return pl.pallas_call(
        copy_out,
        out_shape=[jax.ShapeDtypeStruct(made.shape, made.dtype) for made in results],
        in_specs=[anywhere] * len(results),
        out_specs=[anywhere] * len(results),
        scratch_shapes=[pltpu.VMEM(made.shape, made.dtype) for made in results]
        + [pltpu.SemaphoreType.DMA((len(results),))] * 2,
    )(*results)


def per_device(
    inputs, cotangent, segments, routes, gain_attn, w_qkv, rel_table, w_att_out, gain_ffn, router, w_in, w_out
):
    experts, width, hidden = w_in.shape[1:]
    sec, dgrad, g_out, g_in, g_qkv, g_att, gain_a, gain_f, g_router, table = local_pass(
        inputs, cotangent, segments, routes[0], gain_attn, w_qkv[0], rel_table, w_att_out[0],
        gain_ffn, router[0], w_in[0], w_out[0],
    )
    micros, length = inputs.shape[:2]
    return (
        sec.reshape(1, micros, length, width),
        dgrad.reshape(1, micros, length, width),
        gain_a,
        g_qkv[None],
        jnp.transpose(table, (1, 2, 0)),
        g_att.T[None],
        gain_f,
        g_router.T[None],
        g_in[None],
        jnp.swapaxes(g_out, 1, 2)[None],
    )


def solution(mesh):
    placed = (
        P(None, "dp", None),
        P(None, "dp", None),
        P(None, "dp"),
        P("pipe", None, "dp", None),
        P("pipe", None),
        P("pipe", None, None, "tensor"),
        P("pipe", None, "tensor"),
        P("pipe", "tensor", None),
        P("pipe", None),
        P("pipe", None, None),
        P("pipe", None, None, "tensor"),
        P("pipe", None, "tensor", None),
    )
    return jax.shard_map(
        per_device,
        mesh=mesh,
        in_specs=placed,
        out_specs=(
            P("pipe", None, "dp", None),
            P("pipe", None, "dp", None),
            P("pipe", None),
            P("pipe", None, "dp", "tensor"),
            P("pipe", None, "tensor"),
            P("pipe", "tensor", "dp"),
            P("pipe", None),
            P("pipe", None, None),
            P("pipe", None, "dp", "tensor"),
            P("pipe", None, "tensor", "dp"),
        ),
        check_vma=False,
    )
```

```python
import functools

import jax
import jax.numpy as jnp
import numpy as np
from jax import lax
from jax.experimental import pallas as pl
from jax.experimental.pallas import tpu as pltpu
from jax.sharding import PartitionSpec as P

HEAD = 64
LEN = 128
PAIRS = 3
SEQS = 2
RING = 4
PLAN = (
    ((0, 0, 4), (1, 4, 4), (2, 8, 2), (3, 10, 2)),
    ((0, 12, 4), (1, 16, 4), (2, 20, 2), (3, 22, 2)),
    ((0, 24, 3), (1, 27, 3)),
)
PIECES = [piece for stage in PLAN for piece in stage]
CUTS = 2
epsilon = 1e-06
masked_value = -1e30
F32 = jnp.float32
BF16 = jnp.bfloat16
NT = (((1,), (1,)), ((), ()))
TN = (((0,), (0,)), ((), ()))


def far_limits(buckets):
    half = buckets // 2
    exact = half // 2
    distance = np.arange(LEN)
    ratio = np.log(np.maximum(distance, 1) / exact) / np.log(128.0 / exact)
    bucket = np.minimum(exact + np.floor(ratio * (half - exact) + 1e-09).astype(np.int64), half - 1)
    bucket = np.where(distance < exact, distance, bucket)
    return [int(np.argmax(bucket >= b)) for b in range(1, half) if np.any(bucket >= b)]


def bucket_map(buckets):
    query = lax.broadcasted_iota(jnp.int32, (LEN, LEN), 0)
    key = lax.broadcasted_iota(jnp.int32, (LEN, LEN), 1)
    offset = key - query
    distance = jnp.abs(offset)
    bucket = jnp.where(offset > 0, buckets // 2, 0)
    for limit in far_limits(buckets):
        bucket = bucket + jnp.where(distance >= limit, 1, 0)
    return bucket


def dot(a, b, dims=None):
    if dims is None:
        return jnp.dot(a, b, preferred_element_type=F32)
    return lax.dot_general(a, b, dims, preferred_element_type=F32)


def over_rows(values):
    return jnp.sum(values, axis=0, keepdims=True)


def over_lanes(values):
    return jnp.sum(values, axis=1, keepdims=True)


def kernel(
    x_hbm, dy_hbm, segs_hbm, routes_hbm, gain_a, table, gain_f, router, wqkv_hbm, watt_hbm, win_hbm, wout_hbm,
    sec_hbm, dgrad_hbm, g_out, g_in, g_qkv, g_att, g_gain_a, g_gain_f, g_router, g_table,
    segs, routes, signs, sec, dgrad, wqkv, watt, win, wout, hs, dys, xt, nt, rt, at, proj, probs, mixed, after,
    slope, act2, back2, result, chosens, dproj, send, recv, bias, dsum, tables, grads, own, lots,
    load_sem, out_sem, in_sem, pipe_out, pipe_in, half_out, half_in, far_out, far_in, ring_out, ring_in,
    lot_out, lot_in, *landings,
):
    pipe = lax.axis_index("pipe")
    tensor = lax.axis_index("tensor")
    first = pipe == 0
    last = pipe == 1
    chunks, rows, width = hs.shape
    hidden = slope.shape[-1]
    buckets = table.shape[-1]

    loads = [
        pltpu.make_async_copy(source, target, load_sem.at[i])
        for i, (source, target) in enumerate(
            ((wqkv_hbm, wqkv), (watt_hbm, watt), (win_hbm, win), (wout_hbm, wout))
        )
    ]
    loads_first = [
        pltpu.make_async_copy(source, target, load_sem.at[4 + i])
        for i, (source, target) in enumerate(((x_hbm, hs), (segs_hbm, segs), (routes_hbm, routes)))
    ]

    @pl.when(first)
    def _():
        for load in loads_first:
            load.start()

    for load in loads:
        load.start()

    barrier = pltpu.get_barrier_semaphore()
    pl.semaphore_signal(barrier, inc=1, device_id={"tensor": 1 - tensor}, device_id_type=pl.DeviceIdType.MESH)
    place = lax.axis_index("dp")
    at_x, at_y, at_z = place // (2 * RING), place // RING % 2, place % RING

    def neighbour(on_x, steps):
        if on_x:
            return {"dp": (at_x + steps) % RING * 2 * RING + at_y * RING + at_z}
        return {"dp": at_x * 2 * RING + at_y * RING + (at_z + steps) % RING}

    across = {"dp": at_x * 2 * RING + (1 - at_y) * RING + at_z}
    next_section = {"pipe": 1 - pipe, **across}
    peers = [next_section] + [neighbour(on_x, steps) for on_x in (True, False) for steps in (1, RING - 1)] + [across]

    def remote(source, target, out, into, device):
        return pltpu.make_async_remote_copy(
            src_ref=source, dst_ref=target, send_sem=out, recv_sem=into, device_id=device,
            device_id_type=pl.DeviceIdType.MESH,
        )

    for peer in peers:
        pl.semaphore_signal(barrier, inc=1, device_id=peer, device_id_type=pl.DeviceIdType.MESH)
    pl.semaphore_wait(barrier, 1 + len(peers))

    other_core = {"tensor": 1 - tensor}
    loads_last = [
        remote(source, target, far_out.at[i], far_in.at[i], across)
        for i, (source, target) in enumerate(((segs_hbm, segs), (routes_hbm, routes), (dy_hbm, dys)))
    ]

    @pl.when(last)
    def _():
        for load in loads_last:
            load.start()

    def exchanged(slot, part):
        send[...] = part.astype(BF16)
        copy = remote(send, recv.at[slot % 2], out_sem.at[slot], in_sem.at[slot], other_core)
        copy.start()
        copy.wait()
        return send[...].astype(F32) + recv[slot % 2].astype(F32)

    def crossing(source, target, c, back):
        length = rows // (2 * CUTS)
        sends, shares = [], []
        for i in range(CUTS):
            here = pl.ds(pl.multiple_of((tensor * CUTS + i) * length, length), length)
            slot = (back * chunks + c) * CUTS + i
            sends.append(
                remote(source.at[c, here], target.at[c, here], pipe_out.at[slot], pipe_in.at[slot], next_section)
            )
            shares.append(
                remote(target.at[c, here], target.at[c, here], half_out.at[slot], half_in.at[slot], other_core)
            )
        return sends, shares

    def cross(crossed):
        for copy in crossed[0]:
            copy.start()

    def land(crossed):
        for arrived, share in zip(*crossed):
            arrived.wait_recv()
            share.start()
        for share in crossed[1]:
            share.wait_recv()

    def forward_copy(c):
        return crossing(sec, hs, c, 0)

    def backward_copy(c):
        return crossing(dgrad, dys, c, 1)

    def give(source, target, c, back):
        slot = back * chunks + c
        stays = pltpu.make_async_copy(source.at[c], target.at[c], load_sem.at[7 + slot])
        leaves = remote(source.at[c], target.at[c], far_out.at[3 + slot], far_in.at[3 + slot], across)
        return stays, leaves

    def give_start(given):
        @pl.when(first)
        def _():
            given[0].start()

        @pl.when(last)
        def _():
            given[1].start()

    def give_wait(given):
        @pl.when(first)
        def _():
            given[0].wait()

        @pl.when(last)
        def _():
            given[1].wait()

    bucket = bucket_map(buckets)
    lane = lax.broadcasted_iota(jnp.int32, (LEN, LEN), 1)
    upper = lane >= HEAD
    bias[...] = jnp.zeros_like(bias)
    dsum[...] = jnp.zeros_like(dsum)
    own[...] = jnp.zeros_like(own)
    tables[...] = jnp.zeros_like(tables)

    def add_bias(b, carry):
        hit = bucket == b
        for pair in range(PAIRS):
            for side in range(2):
                at_lanes = pl.ds(side * LEN, LEN)
                bias[pair, :, at_lanes] = jnp.where(hit, table[2 * pair + side, 0, b], bias[pair, :, at_lanes])
        return carry

    lax.fori_loop(0, buckets, add_bias, 0)

    def stacked(values):
        zero = jnp.zeros_like(values)
        return jnp.concatenate([jnp.where(upper, zero, values), jnp.where(upper, values, zero)], axis=0)

    def unstacked(values):
        return jnp.where(upper, values[LEN:], values[:LEN])

    def per_head(values, reduce):
        left = reduce(values[:, :LEN], axis=1, keepdims=True)
        right = reduce(values[:, LEN:], axis=1, keepdims=True)
        return jnp.concatenate(
            [jnp.broadcast_to(left, (LEN, LEN)), jnp.broadcast_to(right, (LEN, LEN))], axis=1
        )

    def keep(tile, left, right):
        left, right = [
            side.reshape(RING, 2, RING, side.shape[0] // (2 * RING * RING), LEN) for side in (left, right)
        ]
        both = jnp.concatenate([left, right], axis=3).astype(BF16)
        grads[:, :, :, :, pl.ds(pl.multiple_of(tile * LEN, LEN), LEN)] = both

    def product_tiles(tile, lefts, rights, count):
        def one(n, carry):
            lanes = pl.ds(pl.multiple_of(n * 4 * LEN, 4 * LEN), 4 * LEN)
            made = dot(lefts[...], rights[:, lanes])
            keep(tile + 2 * n, made[:, :LEN], made[:, LEN : 2 * LEN])
            keep(tile + 2 * n + 1, made[:, 2 * LEN : 3 * LEN], made[:, 3 * LEN :])
            return carry

        lax.fori_loop(0, count // 2, one, 0)

    out_tiles = 2 * hidden // (2 * LEN)
    class Ring:
        def __init__(self, index, phase):
            kind, begin, count = PIECES[index]
            self.lanes = pl.ds(begin * LEN, count * LEN)
            self.fine = [pl.ds((begin + i * (count // 2)) * LEN, count // 2 * LEN) for i in range(2)]
            self.kind, self.phase = kind, phase
            on_x = (kind % 2 == 0) == (phase == 0)
            self.me = at_x if on_x else at_z
            self.up, self.down, self.far = [(self.me + steps) % RING for steps in (1, 3, 2)]
            self.landing = landings[3 * index + phase]
            base = index * 13 + phase * 6
            plan = ((self.far, 0, 1), (self.far, 1, 3), (self.up, 1, 1), (self.down, 0, 3), (self.up, 0, 1), (self.down, 1, 3))
            slots = (0, 1, 3, 4, 2, 5)
            self.copies = [
                remote(
                    self.block(whose, half), self.landing.at[slot], ring_out.at[base + i], ring_in.at[base + i],
                    neighbour(on_x, steps),
                )
                for i, ((whose, half, steps), slot) in enumerate(zip(plan, slots))
            ]

        def block(self, whose, half):
            if self.phase == 0:
                two = pl.ds(2 * half, 2)
                if self.kind == 0:
                    return grads.at[whose, half, :, :, self.lanes]
                if self.kind == 1:
                    return grads.at[:, half, whose, :, self.lanes]
                if self.kind == 2:
                    return grads.at[whose, at_y, two, :, self.lanes]
                return grads.at[two, at_y, whose, :, self.lanes]
            if self.kind == 0:
                return grads.at[at_x, half, whose, :, self.lanes]
            if self.kind == 1:
                return grads.at[whose, half, at_z, :, self.lanes]
            if self.kind == 2:
                return grads.at[at_x, at_y, whose, :, self.fine[half]]
            return grads.at[whose, at_y, at_z, :, self.fine[half]]

        def add(self, *refs):
            if self.phase == 0:
                for i in range(refs[1].shape[0]):
                    add_up(*[ref.at[i] for ref in refs])
            else:
                add_up(*refs)

        def begin(self):
            for copy in self.copies[:4]:
                copy.start()

        def relay(self):
            self.copies[0].wait_recv()
            self.add(self.block(self.up, 0), self.landing.at[0])
            self.copies[4].start()
            self.copies[1].wait_recv()
            self.add(self.block(self.down, 1), self.landing.at[1])
            self.copies[5].start()

        def close(self):
            for copy in self.copies[2:]:
                copy.wait_recv()
            for half in range(2):
                self.add(self.block(self.me, half), self.landing.at[2 + half], self.landing.at[4 + half])

        def drain(self):
            for copy in self.copies:
                copy.wait_send()

    def add_up(target, *others):
        total = target[...].astype(F32)
        for other in others:
            total = total + other[...].astype(F32)
        target[...] = total.astype(BF16)

    class Piece:
        def __init__(self, index):
            kind, self.tile, self.count = PIECES[index]
            self.lanes = pl.ds(self.tile * LEN, self.count * LEN)
            self.early = kind >= 2
            self.rings = [Ring(index, phase) for phase in range(2)]
            self.landing = landings[3 * index + 2]
            theirs = grads.at[:, 1 - at_y, :, :, self.lanes] if self.early else grads.at[at_x, 1 - at_y, at_z, :, self.lanes]
            slot = index * 13 + 12
            self.swap = remote(theirs, self.landing, ring_out.at[slot], ring_in.at[slot], across)

        def open(self):
            if self.early:
                self.swap.start()
            else:
                self.rings[0].begin()

        def join(self):
            self.swap.wait_recv()

            def one(i, carry):
                for j in range(RING):
                    add_up(grads.at[i, at_y, j, :, self.lanes], self.landing.at[i, j])
                return carry

            lax.fori_loop(0, RING, one, 0)
            self.rings[0].begin()

        def turn(self):
            self.rings[0].close()
            self.rings[1].begin()

        def last(self):
            self.rings[1].close()
            if not self.early:
                self.swap.start()

        def settle(self):
            total = grads[at_x, at_y, at_z, :, self.lanes].astype(F32)
            if not self.early:
                self.swap.wait_recv()
                total = total + self.landing[...].astype(F32)
            half = total.shape[0] // 2
            for i in range(self.count):
                here = slice(i * LEN, (i + 1) * LEN)
                place_tile(self.tile + i, total[:half, here], total[half:, here])

        def drain(self):
            for ring in self.rings:
                ring.drain()
            self.swap.wait_send()

    pieces, made = [], 0
    for stage in PLAN:
        pieces.append([Piece(made + i) for i in range(len(stage))])
        made += len(stage)

    def begin(stage):
        for piece in pieces[stage]:
            piece.open()

    def relay(stage, phase, early):
        for piece in pieces[stage]:
            if piece.early == early:
                piece.rings[phase].relay()

    def turn(stage, early):
        for piece in pieces[stage]:
            if piece.early == early:
                piece.turn()

    def finish_rings(stage, early):
        for piece in pieces[stage]:
            if piece.early == early:
                piece.last()

    def join(stage):
        for piece in pieces[stage]:
            if piece.early:
                piece.join()

    def settle(stage):
        for piece in pieces[stage]:
            piece.settle()

    def place_tile(tile, top, bottom):
        if tile < 2 * out_tiles:
            target = g_out if tile < out_tiles else g_in
            within = tile % out_tiles * 2 * LEN
            target[within // hidden, :, pl.ds(within % hidden, 2 * LEN)] = jnp.concatenate([top, bottom], axis=1)
        elif tile < 2 * out_tiles + 5:
            at_block = 2 * (tile - 2 * out_tiles)
            g_qkv[at_block // PAIRS, :, pl.ds(at_block % PAIRS * LEN, LEN)] = top
            if tile < 2 * out_tiles + 4:
                g_qkv[(at_block + 1) // PAIRS, :, pl.ds((at_block + 1) % PAIRS * LEN, LEN)] = bottom
            else:
                g_att[:, 2 * LEN :] = bottom
        else:
            g_att[:, : 2 * LEN] = jnp.concatenate([top, bottom], axis=1)

    def lot(slot, source, target, peer):
        return pltpu.make_async_remote_copy(
            src_ref=source, dst_ref=lots.at[target], send_sem=lot_out.at[slot], recv_sem=lot_in.at[slot],
            device_id=peer, device_id_type=pl.DeviceIdType.MESH,
        )

    lot_copies = []
    for phase in range(2):
        up, down = neighbour(phase == 0, 1), neighbour(phase == 0, RING - 1)
        base = 4 * phase
        lot_copies += [
            lot(3 * phase, own.at[phase], base, up),
            lot(3 * phase + 1, own.at[phase], base + 1, down),
            lot(3 * phase + 2, lots.at[base], base + 2, up),
        ]
    lot_copies.append(lot(6, own.at[2], 8, across))

    def lots_open(phase):
        lot_copies[3 * phase].start()
        lot_copies[3 * phase + 1].start()

    def lots_pass(phase):
        lot_copies[3 * phase].wait_recv()
        lot_copies[3 * phase + 2].start()

    def lots_sum(phase):
        lot_copies[3 * phase + 1].wait_recv()
        lot_copies[3 * phase + 2].wait_recv()
        base = 4 * phase
        own[phase + 1] = (own[phase] + lots[base + 2]) + (lots[base] + lots[base + 1])

    def out_gradients():
        product_tiles(0, rt, act2, out_tiles)
        begin(0)

    def in_gradients():
        product_tiles(out_tiles, nt, back2, out_tiles)
        begin(1)
        relay(0, 0, False)

    @pl.when(first)
    def _():
        for load in loads_first:
            load.wait()

    @pl.when(last)
    def _():
        for load in loads_last[:2]:
            load.wait_recv()

    split = router[0:1, :] - router[1:2, :]

    def column(values):
        return jnp.broadcast_to(values, (LEN, LEN)).T[:, :1]

    def sign_rows(c, carry):
        for s in range(SEQS):
            signs[c, pl.ds(s * LEN, LEN), :] = column((1 - 2 * routes[c * SEQS + s]).astype(F32))
        return carry

    lax.fori_loop(0, chunks, sign_rows, 0)
    for load in loads[:2]:
        load.wait()

    def forward(c, carry):
        @pl.when(last)
        def _():
            land(forward_copy(c))

        spot = pl.multiple_of(c * rows, rows)
        here = pl.ds(spot, rows)
        h = hs[c].astype(F32)
        scale = lax.rsqrt(jnp.mean(h * h, axis=1, keepdims=True) + epsilon)
        normed = (h * scale * gain_a[...]).astype(BF16)
        xt[:, here] = normed.T
        for part in range(3):
            proj[part, here, :] = dot(normed, wqkv[part]).astype(BF16)
        for s in range(SEQS):
            seq = pl.ds(pl.multiple_of(spot + s * LEN, LEN), LEN)
            along = jnp.broadcast_to(segs[pl.ds(c * SEQS + s, 1), :].astype(F32), (LEN, LEN))
            same = along == along.T
            same = jnp.concatenate([same, same], axis=1)
            for pair in range(PAIRS):
                lanes = pl.ds(pair * LEN, LEN)
                query = proj[0, seq, lanes]
                keys = stacked(proj[1, seq, lanes])
                values = stacked(proj[2, seq, lanes])
                scores = dot(query, keys, NT) * HEAD ** (-0.5) + bias[pair]
                scores = jnp.where(same, scores, masked_value)
                raised = jnp.exp(scores - per_head(scores, jnp.max))
                prob = raised / per_head(raised, jnp.sum)
                probs[c * SEQS + s, pair] = prob
                mixed[seq, lanes] = dot(prob.astype(BF16), values).astype(BF16)
        a = h + exchanged(4 * c, dot(mixed[here, :], watt[...]))
        after[here, :] = a
        scale = lax.rsqrt(jnp.mean(a * a, axis=1, keepdims=True) + epsilon)
        normed2 = (a * scale * gain_f[...]).astype(BF16)
        nt[:, here] = normed2.T
        sign = signs[c]
        logit = over_lanes(normed2.astype(F32) * split)
        chosen = 1.0 / (1.0 + jnp.exp(-sign * logit))
        chosens[c] = chosen
        to_zero = (sign > 0).astype(BF16)
        to_one = (sign < 0).astype(BF16)
        doubled = jnp.concatenate([normed2 * to_zero, normed2 * to_one], axis=1)

        @pl.when(c == 0)
        def _():
            for load in loads[2:]:
                load.wait()

        inner = dot(doubled, win[...])
        squared = inner * inner
        root = np.sqrt(2 / np.pi).astype(np.float32)
        bend = jnp.tanh(root * inner * (1.0 + 0.044715 * squared))
        steep = 0.5 * (1.0 + bend) + 0.5 * inner * (1.0 - bend * bend) * root * (1.0 + 3 * 0.044715 * squared)
        slope[here, :] = steep.astype(BF16)
        active = (0.5 * inner * (1.0 + bend)).astype(BF16)
        act2[here, :hidden] = active * to_zero
        act2[here, hidden:] = active * to_one
        total = exchanged(4 * c + 1, dot(act2[here, :], wout[...]))
        result[here, :] = total.astype(BF16)
        sec[c] = (after[here, :] + chosen * total).astype(BF16)

        @pl.when(first)
        def _():
            cross(forward_copy(c))

        give_start(give(sec, sec_hbm, c, 0))

        return carry

    lax.fori_loop(0, chunks, forward, 0)

    @pl.when(last)
    def _():
        loads_last[2].wait_recv()

    def backward(c, carry):
        @pl.when(first)
        def _():
            land(backward_copy(c))

        spot = pl.multiple_of(c * rows, rows)
        here = pl.ds(spot, rows)
        dy = dys[c].astype(F32)
        sign = signs[c]
        to_zero = (sign > 0).astype(BF16)
        to_one = (sign < 0).astype(BF16)
        chosen = chosens[c]
        d_logit = sign * over_lanes(dy * result[here, :].astype(F32)) * chosen * (1.0 - chosen)
        d_result = (chosen * dy).astype(BF16)
        rt[:, here] = d_result.T
        zero_part = d_result * to_zero
        one_part = d_result * to_one

        @pl.when(first & (c == chunks - 1))
        def _():
            out_gradients()

        d_active = dot(zero_part, wout[:hidden, :], NT) + dot(one_part, wout[hidden:, :], NT)
        d_inner = (d_active * slope[here, :].astype(F32)).astype(BF16)
        back2[here, :hidden] = d_inner * to_zero
        back2[here, hidden:] = d_inner * to_one

        @pl.when(first & (c == chunks - 1))
        def _():
            in_gradients()

        d_normed2 = dot(back2[here, :hidden], win[:width, :], NT) + dot(
            back2[here, hidden:], win[width:, :], NT
        )
        d_normed2 = exchanged(4 * c + 2, d_normed2)
        d_normed2 = d_normed2 + d_logit * split
        a = after[here, :]
        scale = lax.rsqrt(jnp.mean(a * a, axis=1, keepdims=True) + epsilon)
        plain = a * scale
        normed2 = (plain * gain_f[...]).astype(BF16).astype(F32)
        own[0, 1:2, :] += over_rows(d_normed2 * plain)
        own[0, 2:3, :] += over_rows(normed2 * d_logit)
        pulled = d_normed2 * gain_f[...]
        d_after = dy + scale * (pulled - plain * jnp.mean(pulled * plain, axis=1, keepdims=True))
        after[here, :] = d_after
        d_attn = d_after.astype(BF16)
        at[:, here] = d_attn.T
        d_mixed = dot(d_attn, watt[...], NT).astype(BF16)
        for s in range(SEQS):
            seq = pl.ds(pl.multiple_of(spot + s * LEN, LEN), LEN)
            for pair in range(PAIRS):
                lanes = pl.ds(pair * LEN, LEN)
                query = proj[0, seq, lanes]
                keys = stacked(proj[1, seq, lanes])
                values = stacked(proj[2, seq, lanes])
                prob = probs[c * SEQS + s, pair]
                d_mix = d_mixed[s * LEN : (s + 1) * LEN, pair * LEN : (pair + 1) * LEN]
                product = prob * dot(d_mix, values, NT)
                d_scores = (product - prob * per_head(product, jnp.sum)).astype(BF16)
                dsum[pair] += d_scores.astype(F32)
                dproj[seq, pl.ds(pair * LEN, LEN)] = (dot(d_scores, keys) * HEAD ** (-0.5)).astype(BF16)
                d_keys = unstacked(dot(d_scores, query, TN)) * HEAD ** (-0.5)
                dproj[seq, pl.ds((PAIRS + pair) * LEN, LEN)] = d_keys.astype(BF16)
                d_values = unstacked(dot(prob.astype(BF16), d_mix, TN))
                dproj[seq, pl.ds((2 * PAIRS + pair) * LEN, LEN)] = d_values.astype(BF16)
        part = PAIRS * LEN
        d_normed = dot(dproj[here, :part], wqkv[0], NT)
        d_normed = d_normed + dot(dproj[here, part : 2 * part], wqkv[1], NT)
        d_normed = d_normed + dot(dproj[here, 2 * part :], wqkv[2], NT)
        d_normed = exchanged(4 * c + 3, d_normed)
        h = hs[c].astype(F32)
        scale = lax.rsqrt(jnp.mean(h * h, axis=1, keepdims=True) + epsilon)
        plain = h * scale
        own[0, 0:1, :] += over_rows(d_normed * plain)
        pulled = d_normed * gain_a[...]
        d_hidden = after[here, :] + scale * (
            pulled - plain * jnp.mean(pulled * plain, axis=1, keepdims=True)
        )
        dgrad[c] = d_hidden.astype(BF16)

        @pl.when(last)
        def _():
            cross(backward_copy(c))

        give_start(give(dgrad, dgrad_hbm, c, 1))

        return carry

    lax.fori_loop(0, chunks, backward, 0)

    @pl.when(last)
    def _():
        out_gradients()
        in_gradients()

    def table_rows(b, carry):
        hit = bucket == b
        for pair in range(PAIRS):
            for side in range(2):
                picked = jnp.where(hit, dsum[pair, :, pl.ds(side * LEN, LEN)], 0.0)
                tables[pl.ds((2 * pair + side) * LEN + b, 1), :] = over_rows(picked)
        return carry

    lax.fori_loop(0, buckets, table_rows, 0)
    own[0, 3:4, :] = over_rows(tables[...].T)
    lots_open(0)
    product_tiles(2 * out_tiles, xt, dproj, 4)
    keep(2 * out_tiles + 4, dot(xt[...], dproj[:, 8 * LEN :]), dot(at[...], mixed[:, 2 * LEN :]))
    made = dot(at[...], mixed[:, : 2 * LEN])
    keep(2 * out_tiles + 5, made[:, :LEN], made[:, LEN:])
    begin(2)
    lots_pass(0)
    relay(1, 0, False)
    lots_sum(0)
    lots_open(1)
    join(0)
    turn(0, False)
    lots_pass(1)
    relay(2, 0, False)
    lots_sum(1)
    lot_copies[6].start()
    relay(0, 0, True)
    turn(1, False)
    join(1)
    relay(0, 1, False)
    turn(0, True)
    turn(2, False)
    relay(1, 1, False)
    relay(1, 0, True)
    finish_rings(0, False)
    relay(0, 1, True)
    relay(2, 1, False)
    turn(1, True)
    finish_rings(1, False)
    finish_rings(0, True)
    settle(0)
    finish_rings(2, False)
    relay(1, 1, True)
    finish_rings(1, True)
    settle(1)
    lot_copies[6].wait_recv()
    small = own[2] + lots[8]
    g_gain_a[...] = small[0:1, :]
    g_gain_f[...] = small[1:2, :]
    g_router[0:1, :] = small[2:3, :]
    g_router[1:2, :] = -small[2:3, :]
    for head in range(2 * PAIRS):
        g_table[head] = small[3:4, head * LEN : head * LEN + buckets]
    settle(2)
    for copy in lot_copies:
        copy.wait_send()
    for stage in pieces:
        for piece in stage:
            piece.drain()

    @pl.when(last)
    def _():
        for load in loads_last:
            load.wait_send()

    def finish(c, carry):
        give_wait(give(sec, sec_hbm, c, 0))
        give_wait(give(dgrad, dgrad_hbm, c, 1))

        @pl.when(first)
        def _():
            for copy in forward_copy(c)[0] + backward_copy(c)[1]:
                copy.wait_send()

        @pl.when(last)
        def _():
            for copy in backward_copy(c)[0] + forward_copy(c)[1]:
                copy.wait_send()

        return carry

    lax.fori_loop(0, chunks, finish, 0)


def copy_out(*refs):
    count = len(refs) // 3
    sources, targets, held = refs[:count], refs[count : 2 * count], refs[2 * count : 3 * count]
    sem_in, sem_out = refs[3 * count :]
    arrive = [pltpu.make_async_copy(*ends, sem_in.at[i]) for i, ends in enumerate(zip(sources, held))]
    leave = [pltpu.make_async_copy(*ends, sem_out.at[i]) for i, ends in enumerate(zip(held, targets))]
    for copy in arrive:
        copy.start()
    for first, second in zip(arrive, leave):
        first.wait()
        second.start()
    for copy in leave:
        copy.wait()


def local_pass(inputs, cotangent, segments, routes, gain_attn, w_qkv, rel_table, w_att_out, gain_ffn, router, w_in, w_out):
    micros, length, width = inputs.shape
    chunks = micros // SEQS
    rows = SEQS * length
    tokens = micros * length
    experts, _, hidden = w_in.shape
    heads = w_att_out.shape[0]
    buckets = rel_table.shape[1]
    count = len(PIECES)
    columns = (3 * heads + heads + 2 * experts * hidden) // 2
    vmem = pl.BlockSpec(memory_space=pltpu.VMEM)
    smem = pl.BlockSpec(memory_space=pltpu.SMEM)
    anywhere = pl.BlockSpec(memory_space=pl.ANY)
    slots = 4 * chunks
    shard = width // (2 * RING * RING)
    double = 2 * shard
    landings = []
    for kind, _, tiles in PIECES:
        wide = tiles * LEN
        if kind < 2:
            landings += [(6, RING, double, wide), (6, double, wide), (double, wide)]
        else:
            landings += [(6, 2, double, wide), (6, double, wide // 2), (RING, RING, double, wide)]
    scratch = [
        pltpu.VMEM((micros, length), jnp.int32),
        pltpu.VMEM((micros, 1, length), jnp.int32),
        pltpu.VMEM((chunks, rows, 1), F32),
        pltpu.VMEM((chunks, rows, width), BF16),
        pltpu.VMEM((chunks, rows, width), BF16),
        pltpu.VMEM(w_qkv.shape, BF16),
        pltpu.VMEM(w_att_out.shape, BF16),
        pltpu.VMEM((experts * width, hidden), BF16),
        pltpu.VMEM((experts * hidden, width), BF16),
        pltpu.VMEM((chunks, rows, width), BF16),
        pltpu.VMEM((chunks, rows, width), BF16),
        pltpu.VMEM((width, tokens), BF16),
        pltpu.VMEM((width, tokens), BF16),
        pltpu.VMEM((width, tokens), BF16),
        pltpu.VMEM((width, tokens), BF16),
        pltpu.VMEM((3, tokens, heads), BF16),
        pltpu.VMEM((micros, PAIRS, LEN, 2 * LEN), F32),
        pltpu.VMEM((tokens, heads), BF16),
        pltpu.VMEM((tokens, width), F32),
        pltpu.VMEM((tokens, hidden), BF16),
        pltpu.VMEM((tokens, experts * hidden), BF16),
        pltpu.VMEM((tokens, experts * hidden), BF16),
        pltpu.VMEM((tokens, width), BF16),
        pltpu.VMEM((chunks, rows, 1), F32),
        pltpu.VMEM((tokens, 3 * heads), BF16),
        pltpu.VMEM((rows, width), BF16),
        pltpu.VMEM((2, rows, width), BF16),
        pltpu.VMEM((PAIRS, LEN, 2 * LEN), F32),
        pltpu.VMEM((PAIRS, LEN, 2 * LEN), F32),
        pltpu.VMEM((2 * PAIRS * LEN, LEN), F32),
        pltpu.VMEM((RING, 2, RING, double, columns), BF16),
        pltpu.VMEM((3, 8, width), F32),
        pltpu.VMEM((9, 8, width), F32),
        pltpu.SemaphoreType.DMA((7 + 2 * chunks,)),
        pltpu.SemaphoreType.DMA((slots,)),
        pltpu.SemaphoreType.DMA((slots,)),
        pltpu.SemaphoreType.DMA((2 * chunks * CUTS,)),
        pltpu.SemaphoreType.DMA((2 * chunks * CUTS,)),
        pltpu.SemaphoreType.DMA((2 * chunks * CUTS,)),
        pltpu.SemaphoreType.DMA((2 * chunks * CUTS,)),
        pltpu.SemaphoreType.DMA((3 + 2 * chunks,)),
        pltpu.SemaphoreType.DMA((3 + 2 * chunks,)),
        pltpu.SemaphoreType.DMA((13 * count,)),
        pltpu.SemaphoreType.DMA((13 * count,)),
        pltpu.SemaphoreType.DMA((7,)),
        pltpu.SemaphoreType.DMA((7,)),
        *[pltpu.VMEM(shape, BF16) for shape in landings],
    ]
    results = pl.pallas_call(
        kernel,
        out_shape=[
            jax.ShapeDtypeStruct((chunks, rows, width), BF16),
            jax.ShapeDtypeStruct((chunks, rows, width), BF16),
            jax.ShapeDtypeStruct((experts, shard, hidden), F32),
            jax.ShapeDtypeStruct((experts, shard, hidden), F32),
            jax.ShapeDtypeStruct((3, shard, heads), F32),
            jax.ShapeDtypeStruct((shard, heads), F32),
            jax.ShapeDtypeStruct((1, width), F32),
            jax.ShapeDtypeStruct((1, width), F32),
            jax.ShapeDtypeStruct((2, width), F32),
            jax.ShapeDtypeStruct((2 * PAIRS, 1, buckets), F32),
        ],
        in_specs=[anywhere] * 4 + [vmem, smem, vmem, vmem] + [anywhere] * 4,
        out_specs=[anywhere] * 2 + [vmem] * 8,
        scratch_shapes=scratch,
        compiler_params=pltpu.CompilerParams(
            collective_id=0, has_side_effects=True, vmem_limit_bytes=62 * 2**20
        ),
        cost_estimate=pl.CostEstimate(flops=18 * 10**9, bytes_accessed=30 * 10**6, transcendentals=10**6),
    )(
        inputs.reshape(chunks, rows, width),
        cotangent.reshape(chunks, rows, width),
        segments,
        jnp.swapaxes(routes, 1, 2),
        gain_attn,
        jnp.transpose(rel_table, (2, 0, 1)),
        gain_ffn,
        router.T,
        w_qkv,
        w_att_out,
        w_in.reshape(experts * width, hidden),
        w_out.reshape(experts * hidden, width),
    )
    return pl.pallas_call(
        copy_out,
        out_shape=[jax.ShapeDtypeStruct(made.shape, made.dtype) for made in results],
        in_specs=[anywhere] * len(results),
        out_specs=[anywhere] * len(results),
        scratch_shapes=[pltpu.VMEM(made.shape, made.dtype) for made in results]
        + [pltpu.SemaphoreType.DMA((len(results),))] * 2,
    )(*results)


def per_device(
    inputs, cotangent, segments, routes, gain_attn, w_qkv, rel_table, w_att_out, gain_ffn, router, w_in, w_out
):
    experts, width, hidden = w_in.shape[1:]
    sec, dgrad, g_out, g_in, g_qkv, g_att, gain_a, gain_f, g_router, table = local_pass(
        inputs, cotangent, segments, routes[0], gain_attn, w_qkv[0], rel_table, w_att_out[0],
        gain_ffn, router[0], w_in[0], w_out[0],
    )
    micros, length = inputs.shape[:2]
    return (
        sec.reshape(1, micros, length, width),
        dgrad.reshape(1, micros, length, width),
        gain_a,
        g_qkv[None],
        jnp.transpose(table, (1, 2, 0)),
        g_att.T[None],
        gain_f,
        g_router.T[None],
        g_in[None],
        jnp.swapaxes(g_out, 1, 2)[None],
    )


def solution(mesh):
    placed = (
        P(None, "dp", None),
        P(None, "dp", None),
        P(None, "dp"),
        P("pipe", None, "dp", None),
        P("pipe", None),
        P("pipe", None, None, "tensor"),
        P("pipe", None, "tensor"),
        P("pipe", "tensor", None),
        P("pipe", None),
        P("pipe", None, None),
        P("pipe", None, None, "tensor"),
        P("pipe", None, "tensor", None),
    )
    return jax.shard_map(
        per_device,
        mesh=mesh,
        in_specs=placed,
        out_specs=(
            P("pipe", None, "dp", None),
            P("pipe", None, "dp", None),
            P("pipe", None),
            P("pipe", None, "dp", "tensor"),
            P("pipe", None, "tensor"),
            P("pipe", "tensor", "dp"),
            P("pipe", None),
            P("pipe", None, None),
            P("pipe", None, "dp", "tensor"),
            P("pipe", None, "tensor", "dp"),
        ),
        check_vma=False,
    )
```

```python
import functools

import jax
import jax.numpy as jnp
import numpy as np
from jax import lax
from jax.experimental import pallas as pl
from jax.experimental.pallas import tpu as pltpu
from jax.sharding import PartitionSpec as P

HEAD = 64
LEN = 128
PAIRS = 3
SEQS = 2
RING = 4
PLAN = (
    ((0, 0, 4), (1, 4, 4), (2, 8, 2), (3, 10, 2)),
    ((0, 12, 4), (1, 16, 4), (2, 20, 2), (3, 22, 2)),
    ((0, 24, 3), (1, 27, 3)),
)
PIECES = [piece for stage in PLAN for piece in stage]
CUTS = 2
epsilon = 1e-06
masked_value = -1e30
F32 = jnp.float32
BF16 = jnp.bfloat16
NT = (((1,), (1,)), ((), ()))
TN = (((0,), (0,)), ((), ()))


def far_limits(buckets):
    half = buckets // 2
    exact = half // 2
    distance = np.arange(LEN)
    ratio = np.log(np.maximum(distance, 1) / exact) / np.log(128.0 / exact)
    bucket = np.minimum(exact + np.floor(ratio * (half - exact) + 1e-09).astype(np.int64), half - 1)
    bucket = np.where(distance < exact, distance, bucket)
    return [int(np.argmax(bucket >= b)) for b in range(1, half) if np.any(bucket >= b)]


def bucket_map(buckets):
    query = lax.broadcasted_iota(jnp.int32, (LEN, LEN), 0)
    key = lax.broadcasted_iota(jnp.int32, (LEN, LEN), 1)
    offset = key - query
    distance = jnp.abs(offset)
    bucket = jnp.where(offset > 0, buckets // 2, 0)
    for limit in far_limits(buckets):
        bucket = bucket + jnp.where(distance >= limit, 1, 0)
    return bucket


def dot(a, b, dims=None):
    if dims is None:
        return jnp.dot(a, b, preferred_element_type=F32)
    return lax.dot_general(a, b, dims, preferred_element_type=F32)


def over_rows(values):
    return jnp.sum(values, axis=0, keepdims=True)


def over_lanes(values):
    return jnp.sum(values, axis=1, keepdims=True)


def kernel(
    x_hbm, dy_hbm, segs_hbm, routes_hbm, gain_a, table, gain_f, router, wqkv_hbm, watt_hbm, win_hbm, wout_hbm,
    sec_hbm, dgrad_hbm, g_out, g_in, g_qkv, g_att, g_gain_a, g_gain_f, g_router, g_table,
    segs, routes, signs, sec, dgrad, wqkv, watt, win, wout, hs, dys, xt, nt, rt, at, proj, probs, mixed, after,
    slope, act2, back2, result, chosens, dproj, send, recv, bias, dsum, tables, grads, own, lots,
    load_sem, out_sem, in_sem, pipe_out, pipe_in, half_out, half_in, far_out, far_in, ring_out, ring_in,
    lot_out, lot_in, *landings,
):
    pipe = lax.axis_index("pipe")
    tensor = lax.axis_index("tensor")
    first = pipe == 0
    last = pipe == 1
    chunks, rows, width = hs.shape
    hidden = slope.shape[-1]
    buckets = table.shape[-1]

    loads = [
        pltpu.make_async_copy(source, target, load_sem.at[i])
        for i, (source, target) in enumerate(
            ((wqkv_hbm, wqkv), (watt_hbm, watt), (win_hbm, win), (wout_hbm, wout))
        )
    ]
    loads_first = [
        pltpu.make_async_copy(source, target, load_sem.at[4 + i])
        for i, (source, target) in enumerate(((x_hbm, hs), (segs_hbm, segs), (routes_hbm, routes)))
    ]

    @pl.when(first)
    def _():
        for load in loads_first:
            load.start()

    for load in loads[:2]:
        load.start()

    barrier = pltpu.get_barrier_semaphore()
    pl.semaphore_signal(barrier, inc=1, device_id={"tensor": 1 - tensor}, device_id_type=pl.DeviceIdType.MESH)
    place = lax.axis_index("dp")
    at_x, at_y, at_z = place // (2 * RING), place // RING % 2, place % RING

    def neighbour(on_x, steps):
        if on_x:
            return {"dp": (at_x + steps) % RING * 2 * RING + at_y * RING + at_z}
        return {"dp": at_x * 2 * RING + at_y * RING + (at_z + steps) % RING}

    across = {"dp": at_x * 2 * RING + (1 - at_y) * RING + at_z}
    next_section = {"pipe": 1 - pipe, **across}
    peers = [next_section] + [neighbour(on_x, steps) for on_x in (True, False) for steps in (1, RING - 1)] + [across]

    def remote(source, target, out, into, device):
        return pltpu.make_async_remote_copy(
            src_ref=source, dst_ref=target, send_sem=out, recv_sem=into, device_id=device,
            device_id_type=pl.DeviceIdType.MESH,
        )

    for peer in peers:
        pl.semaphore_signal(barrier, inc=1, device_id=peer, device_id_type=pl.DeviceIdType.MESH)

    other_core = {"tensor": 1 - tensor}
    loads_last = [
        remote(source, target, far_out.at[i], far_in.at[i], across)
        for i, (source, target) in enumerate(((segs_hbm, segs), (routes_hbm, routes), (dy_hbm, dys)))
    ]

    def exchanged(slot, part, meanwhile=lambda: None):
        send[...] = part.astype(BF16)
        copy = remote(send, recv.at[slot % 2], out_sem.at[slot], in_sem.at[slot], other_core)
        copy.start()
        beside = meanwhile()
        copy.wait()
        return send[...].astype(F32) + recv[slot % 2].astype(F32), beside

    def crossing(source, target, c, back):
        length = rows // (2 * CUTS)
        sends, shares = [], []
        for i in range(CUTS):
            here = pl.ds(pl.multiple_of((tensor * CUTS + i) * length, length), length)
            slot = (back * chunks + c) * CUTS + i
            sends.append(
                remote(source.at[c, here], target.at[c, here], pipe_out.at[slot], pipe_in.at[slot], next_section)
            )
            shares.append(
                remote(target.at[c, here], target.at[c, here], half_out.at[slot], half_in.at[slot], other_core)
            )
        return sends, shares

    def cross(crossed):
        for copy in crossed[0]:
            copy.start()

    def land(crossed):
        for arrived, share in zip(*crossed):
            arrived.wait_recv()
            share.start()
        for share in crossed[1]:
            share.wait_recv()

    def forward_copy(c):
        return crossing(sec, hs, c, 0)

    def backward_copy(c):
        return crossing(dgrad, dys, c, 1)

    def give(source, target, c, back):
        slot = back * chunks + c
        stays = pltpu.make_async_copy(source.at[c], target.at[c], load_sem.at[7 + slot])
        leaves = remote(source.at[c], target.at[c], far_out.at[3 + slot], far_in.at[3 + slot], across)
        return stays, leaves

    def give_start(given):
        @pl.when(first)
        def _():
            given[0].start()

        @pl.when(last)
        def _():
            given[1].start()

    def give_wait(given):
        @pl.when(first)
        def _():
            given[0].wait()

        @pl.when(last)
        def _():
            given[1].wait()

    bucket = bucket_map(buckets)
    lane = lax.broadcasted_iota(jnp.int32, (LEN, LEN), 1)
    upper = lane >= HEAD
    bias[...] = jnp.zeros_like(bias)
    dsum[...] = jnp.zeros_like(dsum)
    own[...] = jnp.zeros_like(own)
    tables[...] = jnp.zeros_like(tables)

    def add_bias(b, carry):
        hit = bucket == b
        for pair in range(PAIRS):
            for side in range(2):
                at_lanes = pl.ds(side * LEN, LEN)
                bias[pair, :, at_lanes] = jnp.where(hit, table[2 * pair + side, 0, b], bias[pair, :, at_lanes])
        return carry

    lax.fori_loop(0, buckets, add_bias, 0)
    pl.semaphore_wait(barrier, 1 + len(peers))

    @pl.when(last)
    def _():
        for load in loads_last:
            load.start()

    def stacked(values):
        zero = jnp.zeros_like(values)
        return jnp.concatenate([jnp.where(upper, zero, values), jnp.where(upper, values, zero)], axis=0)

    def unstacked(values):
        return jnp.where(upper, values[LEN:], values[:LEN])

    def per_head(values, reduce):
        left = reduce(values[:, :LEN], axis=1, keepdims=True)
        right = reduce(values[:, LEN:], axis=1, keepdims=True)
        return jnp.concatenate(
            [jnp.broadcast_to(left, (LEN, LEN)), jnp.broadcast_to(right, (LEN, LEN))], axis=1
        )

    def keep(tile, left, right):
        left, right = [
            side.reshape(RING, 2, RING, side.shape[0] // (2 * RING * RING), LEN) for side in (left, right)
        ]
        both = jnp.concatenate([left, right], axis=3).astype(BF16)
        grads[:, :, :, :, pl.ds(pl.multiple_of(tile * LEN, LEN), LEN)] = both

    def product_tiles(tile, lefts, rights, count, skip=0):
        def one(n, carry):
            lanes = pl.ds(pl.multiple_of(skip * 2 * LEN + n * 4 * LEN, 4 * LEN), 4 * LEN)
            made = dot(lefts[...], rights[:, lanes])
            keep(tile + 2 * n, made[:, :LEN], made[:, LEN : 2 * LEN])
            keep(tile + 2 * n + 1, made[:, 2 * LEN : 3 * LEN], made[:, 3 * LEN :])
            return carry

        lax.fori_loop(0, count // 2, one, 0)

    out_tiles = 2 * hidden // (2 * LEN)
    class Ring:
        def __init__(self, index, phase):
            kind, begin, count = PIECES[index]
            self.lanes = pl.ds(begin * LEN, count * LEN)
            self.fine = [pl.ds((begin + i * (count // 2)) * LEN, count // 2 * LEN) for i in range(2)]
            self.kind, self.phase = kind, phase
            on_x = (kind % 2 == 0) == (phase == 0)
            self.me = at_x if on_x else at_z
            self.up, self.down, self.far = [(self.me + steps) % RING for steps in (1, 3, 2)]
            self.landing = landings[3 * index + phase]
            base = index * 13 + phase * 6
            plan = ((self.far, 0, 1), (self.far, 1, 3), (self.up, 1, 1), (self.down, 0, 3), (self.up, 0, 1), (self.down, 1, 3))
            slots = (0, 1, 3, 4, 2, 5)
            self.copies = [
                remote(
                    self.block(whose, half), self.landing.at[slot], ring_out.at[base + i], ring_in.at[base + i],
                    neighbour(on_x, steps),
                )
                for i, ((whose, half, steps), slot) in enumerate(zip(plan, slots))
            ]

        def block(self, whose, half):
            if self.phase == 0:
                two = pl.ds(2 * half, 2)
                if self.kind == 0:
                    return grads.at[whose, half, :, :, self.lanes]
                if self.kind == 1:
                    return grads.at[:, half, whose, :, self.lanes]
                if self.kind == 2:
                    return grads.at[whose, at_y, two, :, self.lanes]
                return grads.at[two, at_y, whose, :, self.lanes]
            if self.kind == 0:
                return grads.at[at_x, half, whose, :, self.lanes]
            if self.kind == 1:
                return grads.at[whose, half, at_z, :, self.lanes]
            if self.kind == 2:
                return grads.at[at_x, at_y, whose, :, self.fine[half]]
            return grads.at[whose, at_y, at_z, :, self.fine[half]]

        def add(self, *refs):
            if self.phase == 0:
                for i in range(refs[1].shape[0]):
                    add_up(*[ref.at[i] for ref in refs])
            else:
                add_up(*refs)

        def begin(self):
            for copy in self.copies[:4]:
                copy.start()

        def relay(self):
            self.copies[0].wait_recv()
            self.add(self.block(self.up, 0), self.landing.at[0])
            self.copies[4].start()
            self.copies[1].wait_recv()
            self.add(self.block(self.down, 1), self.landing.at[1])
            self.copies[5].start()

        def close(self):
            for copy in self.copies[2:]:
                copy.wait_recv()
            for half in range(2):
                self.add(self.block(self.me, half), self.landing.at[2 + half], self.landing.at[4 + half])

        def drain(self):
            for copy in self.copies:
                copy.wait_send()

    def add_up(target, *others):
        total = target[...].astype(F32)
        for other in others:
            total = total + other[...].astype(F32)
        target[...] = total.astype(BF16)

    class Piece:
        def __init__(self, index):
            kind, self.tile, self.count = PIECES[index]
            self.lanes = pl.ds(self.tile * LEN, self.count * LEN)
            self.early = kind >= 2
            self.rings = [Ring(index, phase) for phase in range(2)]
            self.landing = landings[3 * index + 2]
            theirs = grads.at[:, 1 - at_y, :, :, self.lanes] if self.early else grads.at[at_x, 1 - at_y, at_z, :, self.lanes]
            slot = index * 13 + 12
            self.swap = remote(theirs, self.landing, ring_out.at[slot], ring_in.at[slot], across)

        def open(self):
            if self.early:
                self.swap.start()
            else:
                self.rings[0].begin()

        def join(self):
            self.swap.wait_recv()

            def one(i, carry):
                for j in range(RING):
                    add_up(grads.at[i, at_y, j, :, self.lanes], self.landing.at[i, j])
                return carry

            lax.fori_loop(0, RING, one, 0)
            self.rings[0].begin()

        def turn(self):
            self.rings[0].close()
            self.rings[1].begin()

        def last(self):
            self.rings[1].close()
            if not self.early:
                self.swap.start()

        def settle(self):
            total = grads[at_x, at_y, at_z, :, self.lanes].astype(F32)
            if not self.early:
                self.swap.wait_recv()
                total = total + self.landing[...].astype(F32)
            half = total.shape[0] // 2
            for i in range(self.count):
                here = slice(i * LEN, (i + 1) * LEN)
                place_tile(self.tile + i, total[:half, here], total[half:, here])

        def drain(self):
            for ring in self.rings:
                ring.drain()
            self.swap.wait_send()

    pieces, made = [], 0
    for stage in PLAN:
        pieces.append([Piece(made + i) for i in range(len(stage))])
        made += len(stage)

    def begin(stage):
        for piece in pieces[stage]:
            piece.open()

    def relay(stage, phase, early):
        for piece in pieces[stage]:
            if piece.early == early:
                piece.rings[phase].relay()

    def turn(stage, early):
        for piece in pieces[stage]:
            if piece.early == early:
                piece.turn()

    def finish_rings(stage, early):
        for piece in pieces[stage]:
            if piece.early == early:
                piece.last()

    def join(stage):
        for piece in pieces[stage]:
            if piece.early:
                piece.join()

    def settle(stage):
        for piece in pieces[stage]:
            piece.settle()

    def place_tile(tile, top, bottom):
        if tile < 2 * out_tiles:
            target = g_out if tile < out_tiles else g_in
            within = tile % out_tiles * 2 * LEN
            target[within // hidden, :, pl.ds(within % hidden, 2 * LEN)] = jnp.concatenate([top, bottom], axis=1)
        elif tile < 2 * out_tiles + 5:
            at_block = 2 * (tile - 2 * out_tiles)
            g_qkv[at_block // PAIRS, :, pl.ds(at_block % PAIRS * LEN, LEN)] = top
            if tile < 2 * out_tiles + 4:
                g_qkv[(at_block + 1) // PAIRS, :, pl.ds((at_block + 1) % PAIRS * LEN, LEN)] = bottom
            else:
                g_att[:, 2 * LEN :] = bottom
        else:
            g_att[:, : 2 * LEN] = jnp.concatenate([top, bottom], axis=1)

    def lot(slot, source, target, peer):
        return pltpu.make_async_remote_copy(
            src_ref=source, dst_ref=lots.at[target], send_sem=lot_out.at[slot], recv_sem=lot_in.at[slot],
            device_id=peer, device_id_type=pl.DeviceIdType.MESH,
        )

    lot_copies = []
    for phase in range(2):
        up, down = neighbour(phase == 0, 1), neighbour(phase == 0, RING - 1)
        base = 4 * phase
        lot_copies += [
            lot(3 * phase, own.at[phase], base, up),
            lot(3 * phase + 1, own.at[phase], base + 1, down),
            lot(3 * phase + 2, lots.at[base], base + 2, up),
        ]
    lot_copies.append(lot(6, own.at[2], 8, across))

    def lots_open(phase):
        lot_copies[3 * phase].start()
        lot_copies[3 * phase + 1].start()

    def lots_pass(phase):
        lot_copies[3 * phase].wait_recv()
        lot_copies[3 * phase + 2].start()

    def lots_sum(phase):
        lot_copies[3 * phase + 1].wait_recv()
        lot_copies[3 * phase + 2].wait_recv()
        base = 4 * phase
        own[phase + 1] = (own[phase] + lots[base + 2]) + (lots[base] + lots[base + 1])

    def out_gradients():
        done = 0
        for piece in pieces[0]:
            if piece.tile + piece.count > done:
                until = piece.tile + piece.count
                until += until % 4
                product_tiles(done, rt, act2, until - done, done)
                done = until
            piece.open()

    def in_gradients():
        product_tiles(out_tiles, nt, back2, out_tiles)
        begin(1)
        relay(0, 0, False)

    @pl.when(first)
    def _():
        for load in loads_first:
            load.wait()

    @pl.when(last)
    def _():
        for load in loads_last[:2]:
            load.wait_recv()

    split = router[0:1, :] - router[1:2, :]

    def column(values):
        return jnp.broadcast_to(values, (LEN, LEN)).T[:, :1]

    def sign_rows(c, carry):
        for s in range(SEQS):
            signs[c, pl.ds(s * LEN, LEN), :] = column((1 - 2 * routes[c * SEQS + s]).astype(F32))
        return carry

    lax.fori_loop(0, chunks, sign_rows, 0)
    for load in loads[:2]:
        load.wait()
    for load in loads[2:]:
        load.start()

    def forward(c, carry):
        @pl.when(last)
        def _():
            land(forward_copy(c))

        spot = pl.multiple_of(c * rows, rows)
        here = pl.ds(spot, rows)
        h = hs[c].astype(F32)
        scale = lax.rsqrt(jnp.mean(h * h, axis=1, keepdims=True) + epsilon)
        normed = (h * scale * gain_a[...]).astype(BF16)
        xt[:, here] = normed.T
        for part in range(3):
            proj[part, here, :] = dot(normed, wqkv[part]).astype(BF16)
        for s in range(SEQS):
            seq = pl.ds(pl.multiple_of(spot + s * LEN, LEN), LEN)
            along = jnp.broadcast_to(segs[pl.ds(c * SEQS + s, 1), :].astype(F32), (LEN, LEN))
            same = along == along.T
            same = jnp.concatenate([same, same], axis=1)
            for pair in range(PAIRS):
                lanes = pl.ds(pair * LEN, LEN)
                query = proj[0, seq, lanes]
                keys = stacked(proj[1, seq, lanes])
                values = stacked(proj[2, seq, lanes])
                scores = dot(query, keys, NT) * HEAD ** (-0.5) + bias[pair]
                scores = jnp.where(same, scores, masked_value)
                raised = jnp.exp(scores - per_head(scores, jnp.max))
                prob = raised / per_head(raised, jnp.sum)
                probs[c * SEQS + s, pair] = prob
                mixed[seq, lanes] = dot(prob.astype(BF16), values).astype(BF16)
        a = h + exchanged(4 * c, dot(mixed[here, :], watt[...]))[0]
        after[here, :] = a
        scale = lax.rsqrt(jnp.mean(a * a, axis=1, keepdims=True) + epsilon)
        normed2 = (a * scale * gain_f[...]).astype(BF16)
        sign = signs[c]
        logit = over_lanes(normed2.astype(F32) * split)
        chosen = 1.0 / (1.0 + jnp.exp(-sign * logit))
        chosens[c] = chosen
        to_zero = (sign > 0).astype(BF16)
        to_one = (sign < 0).astype(BF16)
        doubled = jnp.concatenate([normed2 * to_zero, normed2 * to_one], axis=1)

        @pl.when(c == 0)
        def _():
            for load in loads[2:]:
                load.wait()

        root = np.sqrt(2 / np.pi).astype(np.float32)

        def half_of(value, squared):
            return 0.5 * (1.0 + jnp.tanh(root * value * (1.0 + 0.044715 * squared)))

        sides = [(pl.ds(i * (hidden // 2), hidden // 2), pl.ds(hidden + i * (hidden // 2), hidden // 2)) for i in range(2)]
        for low, high in sides:
            value = dot(doubled, win[:, low])
            slope[here, low] = value.astype(BF16)
            active = (value * half_of(value, value * value)).astype(BF16)
            act2[here, low] = active * to_zero
            act2[here, high] = active * to_one

        def slopes():
            nt[:, here] = normed2.T
            for low, _ in sides:
                value = slope[here, low].astype(F32)
                squared = value * value
                half = half_of(value, squared)
                steep = half + 2.0 * value * half * (1.0 - half) * (root * (1.0 + 3 * 0.044715 * squared))
                slope[here, low] = steep.astype(BF16)

        total, _ = exchanged(4 * c + 1, dot(act2[here, :], wout[...]), slopes)
        result[here, :] = total.astype(BF16)
        sec[c] = (after[here, :] + chosen * total).astype(BF16)

        @pl.when(first)
        def _():
            cross(forward_copy(c))

        give_start(give(sec, sec_hbm, c, 0))

        return carry

    lax.fori_loop(0, chunks, forward, 0)

    @pl.when(last)
    def _():
        loads_last[2].wait_recv()

    def backward(c, carry):
        @pl.when(first)
        def _():
            land(backward_copy(c))

        spot = pl.multiple_of(c * rows, rows)
        here = pl.ds(spot, rows)
        dy = dys[c].astype(F32)
        sign = signs[c]
        to_zero = (sign > 0).astype(BF16)
        to_one = (sign < 0).astype(BF16)
        chosen = chosens[c]
        d_logit = sign * over_lanes(dy * result[here, :].astype(F32)) * chosen * (1.0 - chosen)
        d_result = (chosen * dy).astype(BF16)
        rt[:, here] = d_result.T
        zero_part = d_result * to_zero
        one_part = d_result * to_one

        @pl.when(first & (c == chunks - 1))
        def _():
            out_gradients()

        d_active = dot(zero_part, wout[:hidden, :], NT) + dot(one_part, wout[hidden:, :], NT)
        d_inner = (d_active * slope[here, :].astype(F32)).astype(BF16)
        back2[here, :hidden] = d_inner * to_zero
        back2[here, hidden:] = d_inner * to_one

        @pl.when(first & (c == chunks - 1))
        def _():
            in_gradients()

        d_normed2 = dot(back2[here, :hidden], win[:width, :], NT) + dot(
            back2[here, hidden:], win[width:, :], NT
        )

        def unit_after():
            a = after[here, :]
            scale = lax.rsqrt(jnp.mean(a * a, axis=1, keepdims=True) + epsilon)
            plain = a * scale
            normed2 = (plain * gain_f[...]).astype(BF16).astype(F32)
            own[0, 2:3, :] += over_rows(normed2 * d_logit)
            return scale, plain

        d_normed2, (scale, plain) = exchanged(4 * c + 2, d_normed2, unit_after)
        d_normed2 = d_normed2 + d_logit * split
        own[0, 1:2, :] += over_rows(d_normed2 * plain)
        pulled = d_normed2 * gain_f[...]
        d_after = dy + scale * (pulled - plain * jnp.mean(pulled * plain, axis=1, keepdims=True))
        after[here, :] = d_after
        d_attn = d_after.astype(BF16)
        at[:, here] = d_attn.T
        d_mixed = dot(d_attn, watt[...], NT).astype(BF16)
        for s in range(SEQS):
            seq = pl.ds(pl.multiple_of(spot + s * LEN, LEN), LEN)
            for pair in range(PAIRS):
                lanes = pl.ds(pair * LEN, LEN)
                query = proj[0, seq, lanes]
                keys = stacked(proj[1, seq, lanes])
                values = stacked(proj[2, seq, lanes])
                prob = probs[c * SEQS + s, pair]
                d_mix = d_mixed[s * LEN : (s + 1) * LEN, pair * LEN : (pair + 1) * LEN]
                product = prob * dot(d_mix, values, NT)
                d_scores = (product - prob * per_head(product, jnp.sum)).astype(BF16)
                dsum[pair] += d_scores.astype(F32)
                dproj[seq, pl.ds(pair * LEN, LEN)] = (dot(d_scores, keys) * HEAD ** (-0.5)).astype(BF16)
                d_keys = unstacked(dot(d_scores, query, TN)) * HEAD ** (-0.5)
                dproj[seq, pl.ds((PAIRS + pair) * LEN, LEN)] = d_keys.astype(BF16)
                d_values = unstacked(dot(prob.astype(BF16), d_mix, TN))
                dproj[seq, pl.ds((2 * PAIRS + pair) * LEN, LEN)] = d_values.astype(BF16)
        part = PAIRS * LEN
        d_normed = dot(dproj[here, :part], wqkv[0], NT)
        d_normed = d_normed + dot(dproj[here, part : 2 * part], wqkv[1], NT)
        d_normed = d_normed + dot(dproj[here, 2 * part :], wqkv[2], NT)

        def unit_hidden():
            h = hs[c].astype(F32)
            scale = lax.rsqrt(jnp.mean(h * h, axis=1, keepdims=True) + epsilon)
            return scale, h * scale

        d_normed, (scale, plain) = exchanged(4 * c + 3, d_normed, unit_hidden)
        own[0, 0:1, :] += over_rows(d_normed * plain)
        pulled = d_normed * gain_a[...]
        d_hidden = after[here, :] + scale * (
            pulled - plain * jnp.mean(pulled * plain, axis=1, keepdims=True)
        )
        dgrad[c] = d_hidden.astype(BF16)

        @pl.when(last)
        def _():
            cross(backward_copy(c))

        give_start(give(dgrad, dgrad_hbm, c, 1))

        return carry

    lax.fori_loop(0, chunks, backward, 0)

    @pl.when(last)
    def _():
        out_gradients()
        in_gradients()

    def table_rows(b, carry):
        hit = bucket == b
        for pair in range(PAIRS):
            for side in range(2):
                picked = jnp.where(hit, dsum[pair, :, pl.ds(side * LEN, LEN)], 0.0)
                tables[pl.ds((2 * pair + side) * LEN + b, 1), :] = over_rows(picked)
        return carry

    lax.fori_loop(0, buckets, table_rows, 0)
    own[0, 3:4, :] = over_rows(tables[...].T)
    lots_open(0)
    product_tiles(2 * out_tiles, xt, dproj, 4)
    keep(2 * out_tiles + 4, dot(xt[...], dproj[:, 8 * LEN :]), dot(at[...], mixed[:, 2 * LEN :]))
    made = dot(at[...], mixed[:, : 2 * LEN])
    keep(2 * out_tiles + 5, made[:, :LEN], made[:, LEN:])
    begin(2)
    lots_pass(0)
    relay(1, 0, False)
    lots_sum(0)
    lots_open(1)
    join(0)
    turn(0, False)
    lots_pass(1)
    relay(2, 0, False)
    lots_sum(1)
    lot_copies[6].start()
    relay(0, 0, True)
    turn(1, False)
    join(1)
    relay(0, 1, False)
    turn(0, True)
    turn(2, False)
    relay(1, 1, False)
    relay(1, 0, True)
    finish_rings(0, False)
    relay(0, 1, True)
    relay(2, 1, False)
    turn(1, True)
    finish_rings(1, False)
    finish_rings(0, True)
    settle(0)
    finish_rings(2, False)
    relay(1, 1, True)
    finish_rings(1, True)
    settle(1)
    lot_copies[6].wait_recv()
    small = own[2] + lots[8]
    g_gain_a[...] = small[0:1, :]
    g_gain_f[...] = small[1:2, :]
    g_router[0:1, :] = small[2:3, :]
    g_router[1:2, :] = -small[2:3, :]
    for head in range(2 * PAIRS):
        g_table[head] = small[3:4, head * LEN : head * LEN + buckets]
    settle(2)
    for copy in lot_copies:
        copy.wait_send()
    for stage in pieces:
        for piece in stage:
            piece.drain()

    @pl.when(last)
    def _():
        for load in loads_last:
            load.wait_send()

    def finish(c, carry):
        give_wait(give(sec, sec_hbm, c, 0))
        give_wait(give(dgrad, dgrad_hbm, c, 1))

        @pl.when(first)
        def _():
            for copy in forward_copy(c)[0] + backward_copy(c)[1]:
                copy.wait_send()

        @pl.when(last)
        def _():
            for copy in backward_copy(c)[0] + forward_copy(c)[1]:
                copy.wait_send()

        return carry

    lax.fori_loop(0, chunks, finish, 0)


def copy_out(*refs):
    count = len(refs) // 3
    sources, targets, held = refs[:count], refs[count : 2 * count], refs[2 * count : 3 * count]
    sem_in, sem_out = refs[3 * count :]
    arrive = [pltpu.make_async_copy(*ends, sem_in.at[i]) for i, ends in enumerate(zip(sources, held))]
    leave = [pltpu.make_async_copy(*ends, sem_out.at[i]) for i, ends in enumerate(zip(held, targets))]
    for copy in arrive:
        copy.start()
    for first, second in zip(arrive, leave):
        first.wait()
        second.start()
    for copy in leave:
        copy.wait()


def local_pass(inputs, cotangent, segments, routes, gain_attn, w_qkv, rel_table, w_att_out, gain_ffn, router, w_in, w_out):
    micros, length, width = inputs.shape
    chunks = micros // SEQS
    rows = SEQS * length
    tokens = micros * length
    experts, _, hidden = w_in.shape
    heads = w_att_out.shape[0]
    buckets = rel_table.shape[1]
    count = len(PIECES)
    columns = (3 * heads + heads + 2 * experts * hidden) // 2
    vmem = pl.BlockSpec(memory_space=pltpu.VMEM)
    smem = pl.BlockSpec(memory_space=pltpu.SMEM)
    anywhere = pl.BlockSpec(memory_space=pl.ANY)
    slots = 4 * chunks
    shard = width // (2 * RING * RING)
    double = 2 * shard
    landings = []
    for kind, _, tiles in PIECES:
        wide = tiles * LEN
        if kind < 2:
            landings += [(6, RING, double, wide), (6, double, wide), (double, wide)]
        else:
            landings += [(6, 2, double, wide), (6, double, wide // 2), (RING, RING, double, wide)]
    scratch = [
        pltpu.VMEM((micros, length), jnp.int32),
        pltpu.VMEM((micros, 1, length), jnp.int32),
        pltpu.VMEM((chunks, rows, 1), F32),
        pltpu.VMEM((chunks, rows, width), BF16),
        pltpu.VMEM((chunks, rows, width), BF16),
        pltpu.VMEM(w_qkv.shape, BF16),
        pltpu.VMEM(w_att_out.shape, BF16),
        pltpu.VMEM((experts * width, hidden), BF16),
        pltpu.VMEM((experts * hidden, width), BF16),
        pltpu.VMEM((chunks, rows, width), BF16),
        pltpu.VMEM((chunks, rows, width), BF16),
        pltpu.VMEM((width, tokens), BF16),
        pltpu.VMEM((width, tokens), BF16),
        pltpu.VMEM((width, tokens), BF16),
        pltpu.VMEM((width, tokens), BF16),
        pltpu.VMEM((3, tokens, heads), BF16),
        pltpu.VMEM((micros, PAIRS, LEN, 2 * LEN), F32),
        pltpu.VMEM((tokens, heads), BF16),
        pltpu.VMEM((tokens, width), F32),
        pltpu.VMEM((tokens, hidden), BF16),
        pltpu.VMEM((tokens, experts * hidden), BF16),
        pltpu.VMEM((tokens, experts * hidden), BF16),
        pltpu.VMEM((tokens, width), BF16),
        pltpu.VMEM((chunks, rows, 1), F32),
        pltpu.VMEM((tokens, 3 * heads), BF16),
        pltpu.VMEM((rows, width), BF16),
        pltpu.VMEM((2, rows, width), BF16),
        pltpu.VMEM((PAIRS, LEN, 2 * LEN), F32),
        pltpu.VMEM((PAIRS, LEN, 2 * LEN), F32),
        pltpu.VMEM((2 * PAIRS * LEN, LEN), F32),
        pltpu.VMEM((RING, 2, RING, double, columns), BF16),
        pltpu.VMEM((3, 8, width), F32),
        pltpu.VMEM((9, 8, width), F32),
        pltpu.SemaphoreType.DMA((7 + 2 * chunks,)),
        pltpu.SemaphoreType.DMA((slots,)),
        pltpu.SemaphoreType.DMA((slots,)),
        pltpu.SemaphoreType.DMA((2 * chunks * CUTS,)),
        pltpu.SemaphoreType.DMA((2 * chunks * CUTS,)),
        pltpu.SemaphoreType.DMA((2 * chunks * CUTS,)),
        pltpu.SemaphoreType.DMA((2 * chunks * CUTS,)),
        pltpu.SemaphoreType.DMA((3 + 2 * chunks,)),
        pltpu.SemaphoreType.DMA((3 + 2 * chunks,)),
        pltpu.SemaphoreType.DMA((13 * count,)),
        pltpu.SemaphoreType.DMA((13 * count,)),
        pltpu.SemaphoreType.DMA((7,)),
        pltpu.SemaphoreType.DMA((7,)),
        *[pltpu.VMEM(shape, BF16) for shape in landings],
    ]
    results = pl.pallas_call(
        kernel,
        out_shape=[
            jax.ShapeDtypeStruct((chunks, rows, width), BF16),
            jax.ShapeDtypeStruct((chunks, rows, width), BF16),
            jax.ShapeDtypeStruct((experts, shard, hidden), F32),
            jax.ShapeDtypeStruct((experts, shard, hidden), F32),
            jax.ShapeDtypeStruct((3, shard, heads), F32),
            jax.ShapeDtypeStruct((shard, heads), F32),
            jax.ShapeDtypeStruct((1, width), F32),
            jax.ShapeDtypeStruct((1, width), F32),
            jax.ShapeDtypeStruct((2, width), F32),
            jax.ShapeDtypeStruct((2 * PAIRS, 1, buckets), F32),
        ],
        in_specs=[anywhere] * 4 + [vmem, smem, vmem, vmem] + [anywhere] * 4,
        out_specs=[anywhere] * 2 + [vmem] * 8,
        scratch_shapes=scratch,
        compiler_params=pltpu.CompilerParams(
            collective_id=0, has_side_effects=True, vmem_limit_bytes=62 * 2**20
        ),
        cost_estimate=pl.CostEstimate(flops=18 * 10**9, bytes_accessed=30 * 10**6, transcendentals=10**6),
    )(
        inputs.reshape(chunks, rows, width),
        cotangent.reshape(chunks, rows, width),
        segments,
        jnp.swapaxes(routes, 1, 2),
        gain_attn,
        jnp.transpose(rel_table, (2, 0, 1)),
        gain_ffn,
        router.T,
        w_qkv,
        w_att_out,
        w_in.reshape(experts * width, hidden),
        w_out.reshape(experts * hidden, width),
    )
    return pl.pallas_call(
        copy_out,
        out_shape=[jax.ShapeDtypeStruct(made.shape, made.dtype) for made in results],
        in_specs=[anywhere] * len(results),
        out_specs=[anywhere] * len(results),
        scratch_shapes=[pltpu.VMEM(made.shape, made.dtype) for made in results]
        + [pltpu.SemaphoreType.DMA((len(results),))] * 2,
    )(*results)


def per_device(
    inputs, cotangent, segments, routes, gain_attn, w_qkv, rel_table, w_att_out, gain_ffn, router, w_in, w_out
):
    experts, width, hidden = w_in.shape[1:]
    sec, dgrad, g_out, g_in, g_qkv, g_att, gain_a, gain_f, g_router, table = local_pass(
        inputs, cotangent, segments, routes[0], gain_attn, w_qkv[0], rel_table, w_att_out[0],
        gain_ffn, router[0], w_in[0], w_out[0],
    )
    micros, length = inputs.shape[:2]
    return (
        sec.reshape(1, micros, length, width),
        dgrad.reshape(1, micros, length, width),
        gain_a,
        g_qkv[None],
        jnp.transpose(table, (1, 2, 0)),
        g_att.T[None],
        gain_f,
        g_router.T[None],
        g_in[None],
        jnp.swapaxes(g_out, 1, 2)[None],
    )


def solution(mesh):
    placed = (
        P(None, "dp", None),
        P(None, "dp", None),
        P(None, "dp"),
        P("pipe", None, "dp", None),
        P("pipe", None),
        P("pipe", None, None, "tensor"),
        P("pipe", None, "tensor"),
        P("pipe", "tensor", None),
        P("pipe", None),
        P("pipe", None, None),
        P("pipe", None, None, "tensor"),
        P("pipe", None, "tensor", None),
    )
    return jax.shard_map(
        per_device,
        mesh=mesh,
        in_specs=placed,
        out_specs=(
            P("pipe", None, "dp", None),
            P("pipe", None, "dp", None),
            P("pipe", None),
            P("pipe", None, "dp", "tensor"),
            P("pipe", None, "tensor"),
            P("pipe", "tensor", "dp"),
            P("pipe", None),
            P("pipe", None, None),
            P("pipe", None, "dp", "tensor"),
            P("pipe", None, "tensor", "dp"),
        ),
        check_vma=False,
    )
```

```python
import functools

import jax
import jax.numpy as jnp
import numpy as np
from jax import lax
from jax.experimental import pallas as pl
from jax.experimental.pallas import tpu as pltpu
from jax.sharding import PartitionSpec as P

HEAD = 64
LEN = 128
PAIRS = 3
SEQS = 2
RING = 4
PLAN = (
    ((0, 0, 4), (1, 4, 4), (2, 8, 2), (3, 10, 2)),
    ((0, 12, 4), (1, 16, 4), (2, 20, 2), (3, 22, 2)),
    ((0, 24, 3), (1, 27, 3)),
)
PIECES = [piece for stage in PLAN for piece in stage]
CUTS = 2
epsilon = 1e-06
masked_value = -1e30
F32 = jnp.float32
BF16 = jnp.bfloat16
NT = (((1,), (1,)), ((), ()))
TN = (((0,), (0,)), ((), ()))


def far_limits(buckets):
    half = buckets // 2
    exact = half // 2
    distance = np.arange(LEN)
    ratio = np.log(np.maximum(distance, 1) / exact) / np.log(128.0 / exact)
    bucket = np.minimum(exact + np.floor(ratio * (half - exact) + 1e-09).astype(np.int64), half - 1)
    bucket = np.where(distance < exact, distance, bucket)
    return [int(np.argmax(bucket >= b)) for b in range(1, half) if np.any(bucket >= b)]


def bucket_map(buckets):
    query = lax.broadcasted_iota(jnp.int32, (LEN, LEN), 0)
    key = lax.broadcasted_iota(jnp.int32, (LEN, LEN), 1)
    offset = key - query
    distance = jnp.abs(offset)
    bucket = jnp.where(offset > 0, buckets // 2, 0)
    for limit in far_limits(buckets):
        bucket = bucket + jnp.where(distance >= limit, 1, 0)
    return bucket


def dot(a, b, dims=None):
    if dims is None:
        return jnp.dot(a, b, preferred_element_type=F32)
    return lax.dot_general(a, b, dims, preferred_element_type=F32)


def over_rows(values):
    return jnp.sum(values, axis=0, keepdims=True)


def over_lanes(values):
    return jnp.sum(values, axis=1, keepdims=True)


def kernel(
    x_hbm, dy_hbm, segs_hbm, routes_hbm, gain_a, table, gain_f, router, wqkv_hbm, watt_hbm, win_hbm, wout_hbm,
    sec_hbm, dgrad_hbm, g_out, g_in, g_qkv, g_att, g_gain_a, g_gain_f, g_router, g_table,
    segs, routes, signs, sec, dgrad, wqkv, watt, win, wout, hs, dys, xt, nt, rt, at, proj, probs, mixed, after,
    slope, act2, back2, result, chosens, dproj, send, recv, bias, dsum, tables, grads, own, lots,
    load_sem, out_sem, in_sem, pipe_out, pipe_in, half_out, half_in, far_out, far_in, ring_out, ring_in,
    lot_out, lot_in, *landings,
):
    pipe = lax.axis_index("pipe")
    tensor = lax.axis_index("tensor")
    first = pipe == 0
    last = pipe == 1
    chunks, rows, width = hs.shape
    hidden = slope.shape[-1]
    buckets = table.shape[-1]

    loads = [
        pltpu.make_async_copy(source, target, load_sem.at[i])
        for i, (source, target) in enumerate(
            ((wqkv_hbm, wqkv), (watt_hbm, watt), (win_hbm, win), (wout_hbm, wout))
        )
    ]
    loads_first = [
        pltpu.make_async_copy(source, target, load_sem.at[4 + i])
        for i, (source, target) in enumerate(((x_hbm, hs), (segs_hbm, segs), (routes_hbm, routes)))
    ]

    @pl.when(first)
    def _():
        for load in loads_first:
            load.start()

    for load in loads[:2]:
        load.start()

    barrier = pltpu.get_barrier_semaphore()
    pl.semaphore_signal(barrier, inc=1, device_id={"tensor": 1 - tensor}, device_id_type=pl.DeviceIdType.MESH)
    place = lax.axis_index("dp")
    at_x, at_y, at_z = place // (2 * RING), place // RING % 2, place % RING

    def neighbour(on_x, steps):
        if on_x:
            return {"dp": (at_x + steps) % RING * 2 * RING + at_y * RING + at_z}
        return {"dp": at_x * 2 * RING + at_y * RING + (at_z + steps) % RING}

    across = {"dp": at_x * 2 * RING + (1 - at_y) * RING + at_z}
    next_section = {"pipe": 1 - pipe, **across}
    peers = [next_section] + [neighbour(on_x, steps) for on_x in (True, False) for steps in (1, RING - 1)] + [across]

    def remote(source, target, out, into, device):
        return pltpu.make_async_remote_copy(
            src_ref=source, dst_ref=target, send_sem=out, recv_sem=into, device_id=device,
            device_id_type=pl.DeviceIdType.MESH,
        )

    for peer in peers:
        pl.semaphore_signal(barrier, inc=1, device_id=peer, device_id_type=pl.DeviceIdType.MESH)

    other_core = {"tensor": 1 - tensor}
    loads_last = [
        remote(source, target, far_out.at[i], far_in.at[i], across)
        for i, (source, target) in enumerate(((segs_hbm, segs), (routes_hbm, routes), (dy_hbm, dys)))
    ]

    def exchanged(slot, part, meanwhile=lambda: None):
        send[...] = part.astype(BF16)
        copy = remote(send, recv.at[slot % 2], out_sem.at[slot], in_sem.at[slot], other_core)
        copy.start()
        beside = meanwhile()
        copy.wait()
        return send[...].astype(F32) + recv[slot % 2].astype(F32), beside

    def crossing(source, target, c, back):
        length = rows // (2 * CUTS)
        sends, shares = [], []
        for i in range(CUTS):
            here = pl.ds(pl.multiple_of((tensor * CUTS + i) * length, length), length)
            slot = (back * chunks + c) * CUTS + i
            sends.append(
                remote(source.at[c, here], target.at[c, here], pipe_out.at[slot], pipe_in.at[slot], next_section)
            )
            shares.append(
                remote(target.at[c, here], target.at[c, here], half_out.at[slot], half_in.at[slot], other_core)
            )
        return sends, shares

    def cross(crossed):
        for copy in crossed[0]:
            copy.start()

    def land(crossed):
        for arrived, share in zip(*crossed):
            arrived.wait_recv()
            share.start()
        for share in crossed[1]:
            share.wait_recv()

    def forward_copy(c):
        return crossing(sec, hs, c, 0)

    def backward_copy(c):
        return crossing(dgrad, dys, c, 1)

    def give(source, target, c, back):
        slot = back * chunks + c
        stays = pltpu.make_async_copy(source.at[c], target.at[c], load_sem.at[7 + slot])
        leaves = remote(source.at[c], target.at[c], far_out.at[3 + slot], far_in.at[3 + slot], across)
        return stays, leaves

    def give_start(given):
        @pl.when(first)
        def _():
            given[0].start()

        @pl.when(last)
        def _():
            given[1].start()

    def give_wait(given):
        @pl.when(first)
        def _():
            given[0].wait()

        @pl.when(last)
        def _():
            given[1].wait()

    bucket = bucket_map(buckets)
    lane = lax.broadcasted_iota(jnp.int32, (LEN, LEN), 1)
    upper = lane >= HEAD
    bias[...] = jnp.zeros_like(bias)
    dsum[...] = jnp.zeros_like(dsum)
    own[...] = jnp.zeros_like(own)
    tables[...] = jnp.zeros_like(tables)

    def add_bias(b, carry):
        hit = bucket == b
        for pair in range(PAIRS):
            for side in range(2):
                at_lanes = pl.ds(side * LEN, LEN)
                bias[pair, :, at_lanes] = jnp.where(hit, table[2 * pair + side, 0, b], bias[pair, :, at_lanes])
        return carry

    lax.fori_loop(0, buckets, add_bias, 0)
    pl.semaphore_wait(barrier, 1 + len(peers))

    @pl.when(last)
    def _():
        for load in loads_last:
            load.start()

    def stacked(values):
        zero = jnp.zeros_like(values)
        return jnp.concatenate([jnp.where(upper, zero, values), jnp.where(upper, values, zero)], axis=0)

    def unstacked(values):
        return jnp.where(upper, values[LEN:], values[:LEN])

    def per_head(values, reduce):
        left = reduce(values[:, :LEN], axis=1, keepdims=True)
        right = reduce(values[:, LEN:], axis=1, keepdims=True)
        return jnp.concatenate(
            [jnp.broadcast_to(left, (LEN, LEN)), jnp.broadcast_to(right, (LEN, LEN))], axis=1
        )

    def keep(tile, left, right):
        left, right = [
            side.reshape(RING, 2, RING, side.shape[0] // (2 * RING * RING), LEN) for side in (left, right)
        ]
        both = jnp.concatenate([left, right], axis=3).astype(BF16)
        grads[:, :, :, :, pl.ds(pl.multiple_of(tile * LEN, LEN), LEN)] = both

    def product_tiles(tile, lefts, rights, count, skip=0):
        def one(n, carry):
            lanes = pl.ds(pl.multiple_of(skip * 2 * LEN + n * 4 * LEN, 4 * LEN), 4 * LEN)
            made = dot(lefts[...], rights[:, lanes])
            keep(tile + 2 * n, made[:, :LEN], made[:, LEN : 2 * LEN])
            keep(tile + 2 * n + 1, made[:, 2 * LEN : 3 * LEN], made[:, 3 * LEN :])
            return carry

        lax.fori_loop(0, count // 2, one, 0)

    out_tiles = 2 * hidden // (2 * LEN)
    class Ring:
        def __init__(self, index, phase):
            kind, begin, count = PIECES[index]
            self.lanes = pl.ds(begin * LEN, count * LEN)
            self.fine = [pl.ds((begin + i * (count // 2)) * LEN, count // 2 * LEN) for i in range(2)]
            self.kind, self.phase = kind, phase
            on_x = (kind % 2 == 0) == (phase == 0)
            self.me = at_x if on_x else at_z
            self.up, self.down, self.far = [(self.me + steps) % RING for steps in (1, 3, 2)]
            self.landing = landings[3 * index + phase]
            base = index * 13 + phase * 6
            plan = ((self.far, 0, 1), (self.far, 1, 3), (self.up, 1, 1), (self.down, 0, 3), (self.up, 0, 1), (self.down, 1, 3))
            slots = (0, 1, 3, 4, 2, 5)
            self.copies = [
                remote(
                    self.block(whose, half), self.landing.at[slot], ring_out.at[base + i], ring_in.at[base + i],
                    neighbour(on_x, steps),
                )
                for i, ((whose, half, steps), slot) in enumerate(zip(plan, slots))
            ]

        def block(self, whose, half):
            if self.phase == 0:
                two = pl.ds(2 * half, 2)
                if self.kind == 0:
                    return grads.at[whose, half, :, :, self.lanes]
                if self.kind == 1:
                    return grads.at[:, half, whose, :, self.lanes]
                if self.kind == 2:
                    return grads.at[whose, at_y, two, :, self.lanes]
                return grads.at[two, at_y, whose, :, self.lanes]
            if self.kind == 0:
                return grads.at[at_x, half, whose, :, self.lanes]
            if self.kind == 1:
                return grads.at[whose, half, at_z, :, self.lanes]
            if self.kind == 2:
                return grads.at[at_x, at_y, whose, :, self.fine[half]]
            return grads.at[whose, at_y, at_z, :, self.fine[half]]

        def add(self, *refs):
            if self.phase == 0:
                for i in range(refs[1].shape[0]):
                    add_up(*[ref.at[i] for ref in refs])
            else:
                add_up(*refs)

        def begin(self):
            for copy in self.copies[:4]:
                copy.start()

        def relay(self):
            self.copies[0].wait_recv()
            self.add(self.block(self.up, 0), self.landing.at[0])
            self.copies[4].start()
            self.copies[1].wait_recv()
            self.add(self.block(self.down, 1), self.landing.at[1])
            self.copies[5].start()

        def close(self):
            for copy in self.copies[2:]:
                copy.wait_recv()
            for half in range(2):
                self.add(self.block(self.me, half), self.landing.at[2 + half], self.landing.at[4 + half])

        def drain(self):
            for copy in self.copies:
                copy.wait_send()

    def add_up(target, *others):
        total = target[...].astype(F32)
        for other in others:
            total = total + other[...].astype(F32)
        target[...] = total.astype(BF16)

    class Piece:
        def __init__(self, index):
            kind, self.tile, self.count = PIECES[index]
            self.lanes = pl.ds(self.tile * LEN, self.count * LEN)
            self.early = kind >= 2
            self.rings = [Ring(index, phase) for phase in range(2)]
            self.landing = landings[3 * index + 2]
            theirs = grads.at[:, 1 - at_y, :, :, self.lanes] if self.early else grads.at[at_x, 1 - at_y, at_z, :, self.lanes]
            slot = index * 13 + 12
            self.swap = remote(theirs, self.landing, ring_out.at[slot], ring_in.at[slot], across)

        def open(self):
            if self.early:
                self.swap.start()
            else:
                self.rings[0].begin()

        def join(self):
            self.swap.wait_recv()

            def one(i, carry):
                for j in range(RING):
                    add_up(grads.at[i, at_y, j, :, self.lanes], self.landing.at[i, j])
                return carry

            lax.fori_loop(0, RING, one, 0)
            self.rings[0].begin()

        def turn(self):
            self.rings[0].close()
            self.rings[1].begin()

        def last(self):
            self.rings[1].close()
            if not self.early:
                self.swap.start()

        def settle(self):
            total = grads[at_x, at_y, at_z, :, self.lanes].astype(F32)
            if not self.early:
                self.swap.wait_recv()
                total = total + self.landing[...].astype(F32)
            half = total.shape[0] // 2
            for i in range(self.count):
                here = slice(i * LEN, (i + 1) * LEN)
                place_tile(self.tile + i, total[:half, here], total[half:, here])

        def drain(self):
            for ring in self.rings:
                ring.drain()
            self.swap.wait_send()

    pieces, made = [], 0
    for stage in PLAN:
        pieces.append([Piece(made + i) for i in range(len(stage))])
        made += len(stage)

    def begin(stage):
        for piece in pieces[stage]:
            piece.open()

    def relay(stage, phase, early):
        for piece in pieces[stage]:
            if piece.early == early:
                piece.rings[phase].relay()

    def turn(stage, early):
        for piece in pieces[stage]:
            if piece.early == early:
                piece.turn()

    def finish_rings(stage, early):
        for piece in pieces[stage]:
            if piece.early == early:
                piece.last()

    def join(stage):
        for piece in pieces[stage]:
            if piece.early:
                piece.join()

    def settle(stage):
        for piece in pieces[stage]:
            piece.settle()

    def place_tile(tile, top, bottom):
        if tile < 2 * out_tiles:
            target = g_out if tile < out_tiles else g_in
            within = tile % out_tiles * 2 * LEN
            target[within // hidden, :, pl.ds(within % hidden, 2 * LEN)] = jnp.concatenate([top, bottom], axis=1)
        elif tile < 2 * out_tiles + 5:
            at_block = 2 * (tile - 2 * out_tiles)
            g_qkv[at_block // PAIRS, :, pl.ds(at_block % PAIRS * LEN, LEN)] = top
            if tile < 2 * out_tiles + 4:
                g_qkv[(at_block + 1) // PAIRS, :, pl.ds((at_block + 1) % PAIRS * LEN, LEN)] = bottom
            else:
                g_att[:, 2 * LEN :] = bottom
        else:
            g_att[:, : 2 * LEN] = jnp.concatenate([top, bottom], axis=1)

    def lot(slot, source, target, peer):
        return pltpu.make_async_remote_copy(
            src_ref=source, dst_ref=lots.at[target], send_sem=lot_out.at[slot], recv_sem=lot_in.at[slot],
            device_id=peer, device_id_type=pl.DeviceIdType.MESH,
        )

    lot_copies = []
    for phase in range(2):
        up, down = neighbour(phase == 0, 1), neighbour(phase == 0, RING - 1)
        base = 4 * phase
        lot_copies += [
            lot(3 * phase, own.at[phase], base, up),
            lot(3 * phase + 1, own.at[phase], base + 1, down),
            lot(3 * phase + 2, lots.at[base], base + 2, up),
        ]
    lot_copies.append(lot(6, own.at[2], 8, across))

    def lots_open(phase):
        lot_copies[3 * phase].start()
        lot_copies[3 * phase + 1].start()

    def lots_pass(phase):
        lot_copies[3 * phase].wait_recv()
        lot_copies[3 * phase + 2].start()

    def lots_sum(phase):
        lot_copies[3 * phase + 1].wait_recv()
        lot_copies[3 * phase + 2].wait_recv()
        base = 4 * phase
        own[phase + 1] = (own[phase] + lots[base + 2]) + (lots[base] + lots[base + 1])

    def expert_gradients(stage, tile, lefts, rights):
        done = 0
        for piece in pieces[stage]:
            until = piece.tile + piece.count - tile
            if until > done:
                until += until % 4
                product_tiles(tile + done, lefts, rights, until - done, done)
                done = until
            piece.open()

    def out_gradients():
        expert_gradients(0, 0, rt, act2)

    def in_gradients():
        expert_gradients(1, out_tiles, nt, back2)
        relay(0, 0, False)

    @pl.when(first)
    def _():
        for load in loads_first:
            load.wait()

    @pl.when(last)
    def _():
        for load in loads_last[:2]:
            load.wait_recv()

    split = router[0:1, :] - router[1:2, :]

    def column(values):
        return jnp.broadcast_to(values, (LEN, LEN)).T[:, :1]

    def sign_rows(c, carry):
        for s in range(SEQS):
            signs[c, pl.ds(s * LEN, LEN), :] = column((1 - 2 * routes[c * SEQS + s]).astype(F32))
        return carry

    lax.fori_loop(0, chunks, sign_rows, 0)
    for load in loads[:2]:
        load.wait()
    for load in loads[2:]:
        load.start()

    def forward(c, carry):
        @pl.when(last)
        def _():
            land(forward_copy(c))

        spot = pl.multiple_of(c * rows, rows)
        here = pl.ds(spot, rows)
        h = hs[c].astype(F32)
        scale = lax.rsqrt(jnp.mean(h * h, axis=1, keepdims=True) + epsilon)
        normed = (h * scale * gain_a[...]).astype(BF16)
        xt[:, here] = normed.T
        for part in range(3):
            proj[part, here, :] = dot(normed, wqkv[part]).astype(BF16)
        for s in range(SEQS):
            seq = pl.ds(pl.multiple_of(spot + s * LEN, LEN), LEN)
            along = jnp.broadcast_to(segs[pl.ds(c * SEQS + s, 1), :].astype(F32), (LEN, LEN))
            same = along == along.T
            same = jnp.concatenate([same, same], axis=1)
            for pair in range(PAIRS):
                lanes = pl.ds(pair * LEN, LEN)
                query = proj[0, seq, lanes]
                keys = stacked(proj[1, seq, lanes])
                values = stacked(proj[2, seq, lanes])
                scores = dot(query, keys, NT) * HEAD ** (-0.5) + bias[pair]
                scores = jnp.where(same, scores, masked_value)
                raised = jnp.exp(scores - per_head(scores, jnp.max))
                prob = raised / per_head(raised, jnp.sum)
                probs[c * SEQS + s, pair] = prob
                mixed[seq, lanes] = dot(prob.astype(BF16), values).astype(BF16)
        a = h + exchanged(4 * c, dot(mixed[here, :], watt[...]))[0]
        after[here, :] = a
        scale = lax.rsqrt(jnp.mean(a * a, axis=1, keepdims=True) + epsilon)
        normed2 = (a * scale * gain_f[...]).astype(BF16)
        sign = signs[c]
        logit = over_lanes(normed2.astype(F32) * split)
        chosen = 1.0 / (1.0 + jnp.exp(-sign * logit))
        chosens[c] = chosen
        to_zero = (sign > 0).astype(BF16)
        to_one = (sign < 0).astype(BF16)
        doubled = jnp.concatenate([normed2 * to_zero, normed2 * to_one], axis=1)

        @pl.when(c == 0)
        def _():
            for load in loads[2:]:
                load.wait()

        root = np.sqrt(2 / np.pi).astype(np.float32)

        def half_of(value, squared):
            return 0.5 * (1.0 + jnp.tanh(root * value * (1.0 + 0.044715 * squared)))

        sides = [(pl.ds(i * (hidden // 2), hidden // 2), pl.ds(hidden + i * (hidden // 2), hidden // 2)) for i in range(2)]
        for low, high in sides:
            value = dot(doubled, win[:, low])
            slope[here, low] = value.astype(BF16)
            active = (value * half_of(value, value * value)).astype(BF16)
            act2[here, low] = active * to_zero
            act2[here, high] = active * to_one

        def slopes():
            nt[:, here] = normed2.T
            for low, _ in sides:
                value = slope[here, low].astype(F32)
                squared = value * value
                half = half_of(value, squared)
                steep = half + 2.0 * value * half * (1.0 - half) * (root * (1.0 + 3 * 0.044715 * squared))
                slope[here, low] = steep.astype(BF16)

        total, _ = exchanged(4 * c + 1, dot(act2[here, :], wout[...]), slopes)
        result[here, :] = total.astype(BF16)
        sec[c] = (after[here, :] + chosen * total).astype(BF16)

        @pl.when(first)
        def _():
            cross(forward_copy(c))

        give_start(give(sec, sec_hbm, c, 0))

        return carry

    lax.fori_loop(0, chunks, forward, 0)

    @pl.when(last)
    def _():
        loads_last[2].wait_recv()

    def backward(c, carry):
        @pl.when(first)
        def _():
            land(backward_copy(c))

        spot = pl.multiple_of(c * rows, rows)
        here = pl.ds(spot, rows)
        dy = dys[c].astype(F32)
        sign = signs[c]
        to_zero = (sign > 0).astype(BF16)
        to_one = (sign < 0).astype(BF16)
        chosen = chosens[c]
        d_logit = sign * over_lanes(dy * result[here, :].astype(F32)) * chosen * (1.0 - chosen)
        d_result = (chosen * dy).astype(BF16)
        rt[:, here] = d_result.T
        zero_part = d_result * to_zero
        one_part = d_result * to_one

        @pl.when(first & (c == chunks - 1))
        def _():
            out_gradients()

        d_active = dot(zero_part, wout[:hidden, :], NT) + dot(one_part, wout[hidden:, :], NT)
        d_inner = (d_active * slope[here, :].astype(F32)).astype(BF16)
        back2[here, :hidden] = d_inner * to_zero
        back2[here, hidden:] = d_inner * to_one

        @pl.when(first & (c == chunks - 1))
        def _():
            in_gradients()

        d_normed2 = dot(back2[here, :hidden], win[:width, :], NT) + dot(
            back2[here, hidden:], win[width:, :], NT
        )

        def unit_after():
            a = after[here, :]
            scale = lax.rsqrt(jnp.mean(a * a, axis=1, keepdims=True) + epsilon)
            plain = a * scale
            normed2 = (plain * gain_f[...]).astype(BF16).astype(F32)
            own[0, 2:3, :] += over_rows(normed2 * d_logit)
            return scale, plain

        d_normed2, (scale, plain) = exchanged(4 * c + 2, d_normed2, unit_after)
        d_normed2 = d_normed2 + d_logit * split
        own[0, 1:2, :] += over_rows(d_normed2 * plain)
        pulled = d_normed2 * gain_f[...]
        d_after = dy + scale * (pulled - plain * jnp.mean(pulled * plain, axis=1, keepdims=True))
        after[here, :] = d_after
        d_attn = d_after.astype(BF16)
        at[:, here] = d_attn.T
        d_mixed = dot(d_attn, watt[...], NT).astype(BF16)
        for s in range(SEQS):
            seq = pl.ds(pl.multiple_of(spot + s * LEN, LEN), LEN)
            for pair in range(PAIRS):
                lanes = pl.ds(pair * LEN, LEN)
                query = proj[0, seq, lanes]
                keys = stacked(proj[1, seq, lanes])
                values = stacked(proj[2, seq, lanes])
                prob = probs[c * SEQS + s, pair]
                d_mix = d_mixed[s * LEN : (s + 1) * LEN, pair * LEN : (pair + 1) * LEN]
                product = prob * dot(d_mix, values, NT)
                d_scores = (product - prob * per_head(product, jnp.sum)).astype(BF16)
                dsum[pair] += d_scores.astype(F32)
                dproj[seq, pl.ds(pair * LEN, LEN)] = (dot(d_scores, keys) * HEAD ** (-0.5)).astype(BF16)
                d_keys = unstacked(dot(d_scores, query, TN)) * HEAD ** (-0.5)
                dproj[seq, pl.ds((PAIRS + pair) * LEN, LEN)] = d_keys.astype(BF16)
                d_values = unstacked(dot(prob.astype(BF16), d_mix, TN))
                dproj[seq, pl.ds((2 * PAIRS + pair) * LEN, LEN)] = d_values.astype(BF16)
        part = PAIRS * LEN
        d_normed = dot(dproj[here, :part], wqkv[0], NT)
        d_normed = d_normed + dot(dproj[here, part : 2 * part], wqkv[1], NT)
        d_normed = d_normed + dot(dproj[here, 2 * part :], wqkv[2], NT)

        def unit_hidden():
            h = hs[c].astype(F32)
            scale = lax.rsqrt(jnp.mean(h * h, axis=1, keepdims=True) + epsilon)
            return scale, h * scale

        d_normed, (scale, plain) = exchanged(4 * c + 3, d_normed, unit_hidden)
        own[0, 0:1, :] += over_rows(d_normed * plain)
        pulled = d_normed * gain_a[...]
        d_hidden = after[here, :] + scale * (
            pulled - plain * jnp.mean(pulled * plain, axis=1, keepdims=True)
        )
        dgrad[c] = d_hidden.astype(BF16)

        @pl.when(last)
        def _():
            cross(backward_copy(c))

        give_start(give(dgrad, dgrad_hbm, c, 1))

        return carry

    lax.fori_loop(0, chunks, backward, 0)

    @pl.when(last)
    def _():
        out_gradients()
        in_gradients()

    def table_rows(b, carry):
        hit = bucket == b
        for pair in range(PAIRS):
            for side in range(2):
                picked = jnp.where(hit, dsum[pair, :, pl.ds(side * LEN, LEN)], 0.0)
                tables[pl.ds((2 * pair + side) * LEN + b, 1), :] = over_rows(picked)
        return carry

    lax.fori_loop(0, buckets, table_rows, 0)
    own[0, 3:4, :] = over_rows(tables[...].T)
    lots_open(0)
    product_tiles(2 * out_tiles, xt, dproj, 4)
    keep(2 * out_tiles + 4, dot(xt[...], dproj[:, 8 * LEN :]), dot(at[...], mixed[:, 2 * LEN :]))
    made = dot(at[...], mixed[:, : 2 * LEN])
    keep(2 * out_tiles + 5, made[:, :LEN], made[:, LEN:])
    begin(2)
    lots_pass(0)
    relay(1, 0, False)
    lots_sum(0)
    lots_open(1)
    join(0)
    turn(0, False)
    lots_pass(1)
    relay(2, 0, False)
    lots_sum(1)
    lot_copies[6].start()
    relay(0, 0, True)
    turn(1, False)
    join(1)
    relay(0, 1, False)
    turn(0, True)
    turn(2, False)
    relay(1, 1, False)
    relay(1, 0, True)
    finish_rings(0, False)
    relay(0, 1, True)
    relay(2, 1, False)
    turn(1, True)
    finish_rings(1, False)
    finish_rings(0, True)
    settle(0)
    finish_rings(2, False)
    relay(1, 1, True)
    finish_rings(1, True)
    settle(1)
    lot_copies[6].wait_recv()
    small = own[2] + lots[8]
    g_gain_a[...] = small[0:1, :]
    g_gain_f[...] = small[1:2, :]
    g_router[0:1, :] = small[2:3, :]
    g_router[1:2, :] = -small[2:3, :]
    for head in range(2 * PAIRS):
        g_table[head] = small[3:4, head * LEN : head * LEN + buckets]
    settle(2)
    for copy in lot_copies:
        copy.wait_send()
    for stage in pieces:
        for piece in stage:
            piece.drain()

    @pl.when(last)
    def _():
        for load in loads_last:
            load.wait_send()

    def finish(c, carry):
        give_wait(give(sec, sec_hbm, c, 0))
        give_wait(give(dgrad, dgrad_hbm, c, 1))

        @pl.when(first)
        def _():
            for copy in forward_copy(c)[0] + backward_copy(c)[1]:
                copy.wait_send()

        @pl.when(last)
        def _():
            for copy in backward_copy(c)[0] + forward_copy(c)[1]:
                copy.wait_send()

        return carry

    lax.fori_loop(0, chunks, finish, 0)


def copy_out(*refs):
    count = len(refs) // 3
    sources, targets, held = refs[:count], refs[count : 2 * count], refs[2 * count : 3 * count]
    sem_in, sem_out = refs[3 * count :]
    arrive = [pltpu.make_async_copy(*ends, sem_in.at[i]) for i, ends in enumerate(zip(sources, held))]
    leave = [pltpu.make_async_copy(*ends, sem_out.at[i]) for i, ends in enumerate(zip(held, targets))]
    for copy in arrive:
        copy.start()
    for first, second in zip(arrive, leave):
        first.wait()
        second.start()
    for copy in leave:
        copy.wait()


def local_pass(inputs, cotangent, segments, routes, gain_attn, w_qkv, rel_table, w_att_out, gain_ffn, router, w_in, w_out):
    micros, length, width = inputs.shape
    chunks = micros // SEQS
    rows = SEQS * length
    tokens = micros * length
    experts, _, hidden = w_in.shape
    heads = w_att_out.shape[0]
    buckets = rel_table.shape[1]
    count = len(PIECES)
    columns = (3 * heads + heads + 2 * experts * hidden) // 2
    vmem = pl.BlockSpec(memory_space=pltpu.VMEM)
    smem = pl.BlockSpec(memory_space=pltpu.SMEM)
    anywhere = pl.BlockSpec(memory_space=pl.ANY)
    slots = 4 * chunks
    shard = width // (2 * RING * RING)
    double = 2 * shard
    landings = []
    for kind, _, tiles in PIECES:
        wide = tiles * LEN
        if kind < 2:
            landings += [(6, RING, double, wide), (6, double, wide), (double, wide)]
        else:
            landings += [(6, 2, double, wide), (6, double, wide // 2), (RING, RING, double, wide)]
    scratch = [
        pltpu.VMEM((micros, length), jnp.int32),
        pltpu.VMEM((micros, 1, length), jnp.int32),
        pltpu.VMEM((chunks, rows, 1), F32),
        pltpu.VMEM((chunks, rows, width), BF16),
        pltpu.VMEM((chunks, rows, width), BF16),
        pltpu.VMEM(w_qkv.shape, BF16),
        pltpu.VMEM(w_att_out.shape, BF16),
        pltpu.VMEM((experts * width, hidden), BF16),
        pltpu.VMEM((experts * hidden, width), BF16),
        pltpu.VMEM((chunks, rows, width), BF16),
        pltpu.VMEM((chunks, rows, width), BF16),
        pltpu.VMEM((width, tokens), BF16),
        pltpu.VMEM((width, tokens), BF16),
        pltpu.VMEM((width, tokens), BF16),
        pltpu.VMEM((width, tokens), BF16),
        pltpu.VMEM((3, tokens, heads), BF16),
        pltpu.VMEM((micros, PAIRS, LEN, 2 * LEN), F32),
        pltpu.VMEM((tokens, heads), BF16),
        pltpu.VMEM((tokens, width), F32),
        pltpu.VMEM((tokens, hidden), BF16),
        pltpu.VMEM((tokens, experts * hidden), BF16),
        pltpu.VMEM((tokens, experts * hidden), BF16),
        pltpu.VMEM((tokens, width), BF16),
        pltpu.VMEM((chunks, rows, 1), F32),
        pltpu.VMEM((tokens, 3 * heads), BF16),
        pltpu.VMEM((rows, width), BF16),
        pltpu.VMEM((2, rows, width), BF16),
        pltpu.VMEM((PAIRS, LEN, 2 * LEN), F32),
        pltpu.VMEM((PAIRS, LEN, 2 * LEN), F32),
        pltpu.VMEM((2 * PAIRS * LEN, LEN), F32),
        pltpu.VMEM((RING, 2, RING, double, columns), BF16),
        pltpu.VMEM((3, 8, width), F32),
        pltpu.VMEM((9, 8, width), F32),
        pltpu.SemaphoreType.DMA((7 + 2 * chunks,)),
        pltpu.SemaphoreType.DMA((slots,)),
        pltpu.SemaphoreType.DMA((slots,)),
        pltpu.SemaphoreType.DMA((2 * chunks * CUTS,)),
        pltpu.SemaphoreType.DMA((2 * chunks * CUTS,)),
        pltpu.SemaphoreType.DMA((2 * chunks * CUTS,)),
        pltpu.SemaphoreType.DMA((2 * chunks * CUTS,)),
        pltpu.SemaphoreType.DMA((3 + 2 * chunks,)),
        pltpu.SemaphoreType.DMA((3 + 2 * chunks,)),
        pltpu.SemaphoreType.DMA((13 * count,)),
        pltpu.SemaphoreType.DMA((13 * count,)),
        pltpu.SemaphoreType.DMA((7,)),
        pltpu.SemaphoreType.DMA((7,)),
        *[pltpu.VMEM(shape, BF16) for shape in landings],
    ]
    results = pl.pallas_call(
        kernel,
        out_shape=[
            jax.ShapeDtypeStruct((chunks, rows, width), BF16),
            jax.ShapeDtypeStruct((chunks, rows, width), BF16),
            jax.ShapeDtypeStruct((experts, shard, hidden), F32),
            jax.ShapeDtypeStruct((experts, shard, hidden), F32),
            jax.ShapeDtypeStruct((3, shard, heads), F32),
            jax.ShapeDtypeStruct((shard, heads), F32),
            jax.ShapeDtypeStruct((1, width), F32),
            jax.ShapeDtypeStruct((1, width), F32),
            jax.ShapeDtypeStruct((2, width), F32),
            jax.ShapeDtypeStruct((2 * PAIRS, 1, buckets), F32),
        ],
        in_specs=[anywhere] * 4 + [vmem, smem, vmem, vmem] + [anywhere] * 4,
        out_specs=[anywhere] * 2 + [vmem] * 8,
        scratch_shapes=scratch,
        compiler_params=pltpu.CompilerParams(
            collective_id=0, has_side_effects=True, vmem_limit_bytes=62 * 2**20
        ),
        cost_estimate=pl.CostEstimate(flops=18 * 10**9, bytes_accessed=30 * 10**6, transcendentals=10**6),
    )(
        inputs.reshape(chunks, rows, width),
        cotangent.reshape(chunks, rows, width),
        segments,
        jnp.swapaxes(routes, 1, 2),
        gain_attn,
        jnp.transpose(rel_table, (2, 0, 1)),
        gain_ffn,
        router.T,
        w_qkv,
        w_att_out,
        w_in.reshape(experts * width, hidden),
        w_out.reshape(experts * hidden, width),
    )
    return pl.pallas_call(
        copy_out,
        out_shape=[jax.ShapeDtypeStruct(made.shape, made.dtype) for made in results],
        in_specs=[anywhere] * len(results),
        out_specs=[anywhere] * len(results),
        scratch_shapes=[pltpu.VMEM(made.shape, made.dtype) for made in results]
        + [pltpu.SemaphoreType.DMA((len(results),))] * 2,
    )(*results)


def per_device(
    inputs, cotangent, segments, routes, gain_attn, w_qkv, rel_table, w_att_out, gain_ffn, router, w_in, w_out
):
    experts, width, hidden = w_in.shape[1:]
    sec, dgrad, g_out, g_in, g_qkv, g_att, gain_a, gain_f, g_router, table = local_pass(
        inputs, cotangent, segments, routes[0], gain_attn, w_qkv[0], rel_table, w_att_out[0],
        gain_ffn, router[0], w_in[0], w_out[0],
    )
    micros, length = inputs.shape[:2]
    return (
        sec.reshape(1, micros, length, width),
        dgrad.reshape(1, micros, length, width),
        gain_a,
        g_qkv[None],
        jnp.transpose(table, (1, 2, 0)),
        g_att.T[None],
        gain_f,
        g_router.T[None],
        g_in[None],
        jnp.swapaxes(g_out, 1, 2)[None],
    )


def solution(mesh):
    placed = (
        P(None, "dp", None),
        P(None, "dp", None),
        P(None, "dp"),
        P("pipe", None, "dp", None),
        P("pipe", None),
        P("pipe", None, None, "tensor"),
        P("pipe", None, "tensor"),
        P("pipe", "tensor", None),
        P("pipe", None),
        P("pipe", None, None),
        P("pipe", None, None, "tensor"),
        P("pipe", None, "tensor", None),
    )
    return jax.shard_map(
        per_device,
        mesh=mesh,
        in_specs=placed,
        out_specs=(
            P("pipe", None, "dp", None),
            P("pipe", None, "dp", None),
            P("pipe", None),
            P("pipe", None, "dp", "tensor"),
            P("pipe", None, "tensor"),
            P("pipe", "tensor", "dp"),
            P("pipe", None),
            P("pipe", None, None),
            P("pipe", None, "dp", "tensor"),
            P("pipe", None, "tensor", "dp"),
        ),
        check_vma=False,
    )
```
